32 devices in a mesh: dp: 4 (over x, core), fsdp: 4 (over z), tensor: 2 (over y).
Axes of the slice: x: 2, y: 2, z: 4, core: 2. Of those that a mesh axis runs over, the one named last changes fastest.
Arguments:
- activations: bfloat16 [4096, 4096], P(('dp', 'tensor'), 'fsdp'), may hold values from -6 to 6
- cotangent: bfloat16 [4096, 16384], P('dp', 'tensor'), may hold values from -6 to 6
- weight: bfloat16 [4096, 16384], P('fsdp', 'tensor'), may hold values from -0.046875 to 0.046875
- residual: bfloat16 [4, 4096, 16384], P('dp', 'fsdp', 'tensor'), may hold values from -6 to 6
- step_size: float32 [1], replicated, may hold values from 0.02 to 0.06
- kept_blocks: int32 [4, 4, 2, 8], P('dp', 'fsdp', 'tensor'), may hold values from 0 to 511, as said below
Outputs:
- input_grad: bfloat16 [4096, 4096], P(('dp', 'tensor'), 'fsdp')
- residual_out: bfloat16 [4, 4096, 16384], P('dp', 'fsdp', 'tensor')
- owned: float32 [4, 4, 2, 128, 128, 128], P('dp', 'fsdp', 'tensor')
The draws below stay inside these ranges and needn't reach their ends.
Inputs may be any that keep to these rules, and one draw needn't show every extreme that they name: The 8 entries of kept_blocks[a, f, t, :] are different block numbers.
All inputs are finite; a program needn't handle non-finite values.
Results may differ from the reference program's by a relative error of at most 0.0029.
Values may be sent and summed in bfloat16 or wider, within the bound.
No kernel may reach another device: no remote copies, remote signals or barrier semaphores. Data moves between devices by JAX's collectives and lax.ppermute only.
A program may use at most 128 MiB of HBM per device.

```python
import math
import jax
import jax.numpy as jnp
from jax import lax

D = 4096
FW = 16384
BLK = 128
KEEP = 8
TOKG = 1024
TOK = 4096
REGION_BLOCKS = 512
N_DP = 4
N_FSDP = 4
N_TENSOR = 2


def draw_kept_blocks(key, part):
    first_key, second_key = jax.random.split(jax.random.fold_in(key, 7))
    preferred_blocks = jax.random.randint(first_key, (1, N_FSDP, N_TENSOR, 1), 0, N_DP)
    baseline_score = jax.random.randint(second_key, (N_DP, N_FSDP, N_TENSOR, REGION_BLOCKS), 0, 1 << 16)
    block_numbers = jnp.arange(REGION_BLOCKS, dtype=jnp.int32)
    extra_credit = jnp.where((block_numbers % N_DP)[None, None, None, :] == preferred_blocks, 1 << 15, 0)
    block_scores = (baseline_score + extra_credit) * REGION_BLOCKS + block_numbers[None, None, None, :]
    chosen = lax.top_k(block_scores, KEEP)[1]
    return chosen.astype(jnp.int32)


def raised(result, rng, source, target, parts, factor):
    def block_of(axis_at):
        return (jnp.arange(result.shape[axis_at]) // (result.shape[axis_at] // parts)).reshape((-1,) + (1,) * (result.ndim - 1 - axis_at))

    one_side = jax.random.permutation(rng, parts)[block_of(target)]
    far = (block_of(target) + parts // 2) % parts
    return jnp.where((block_of(source) == one_side) | (block_of(source) == far), factor * result, result)


def levels(rng, extent, cuts, least, largest):
    level, own = 1.0, jax.random.fold_in(rng, 6)
    for dim, shards_of in cuts:
        draws = jnp.exp(jax.random.uniform(jax.random.fold_in(own, dim), (shards_of,), jnp.float32, least / len(cuts), largest / len(cuts)))
        level = level * jnp.repeat(draws, extent[dim] // shards_of).reshape([-1 if axis == dim else 1 for axis in range(len(extent))])
    return level


def centred(stream_key, shape, deviation, reach, cuts=(), kind=jnp.bfloat16):
    drawn = jax.random.normal(stream_key, shape, jnp.float32) * deviation
    if len(cuts) > 0:
        drawn = levels(stream_key, shape, cuts, -0.22, 0.18) * drawn
    return jnp.clip(drawn, min=-reach, max=reach).astype(kind)


def noise_with(rng, dims, scale, reach, cuts, heavy, kind=jnp.bfloat16):
    entries = scale * jax.random.normal(rng, dims, jnp.float32)
    if cuts:
        entries = entries * levels(rng, dims, cuts, -0.22, 0.18)
    return jnp.clip(raised(entries, jax.random.fold_in(rng, 3), *heavy), -reach, reach).astype(kind)


def setup_inputs(seed: int = 0) -> dict:
    key_of = jax.random.split(jax.random.key(seed), 7)
    return {
        "activations": centred(key_of[0], (TOK, D), 1.0, 6.0, ((0, 8), (1, 4))),
        "cotangent": noise_with(key_of[1], (TOK, FW), 1.0, 6.0, ((0, 4), (1, 2)), (1, 0, 4, 2.0)),
        "weight": centred(key_of[2], (D, FW), FW ** -0.5, 0.046875, ((0, 4), (1, 2))),
        "residual": centred(key_of[3], (N_DP, D, FW), 1.0, 6.0, ((0, 4), (1, 4), (2, 2))),
        "step_size": jnp.clip(jnp.exp(jax.random.uniform(key_of[4], (1,), jnp.float32, math.log(0.02), math.log(0.06))), 0.02, 0.06),
        "kept_blocks": draw_kept_blocks(jax.random.fold_in(key_of[6], 71), 0),
    }


def reference(activations, cotangent, weight, residual, step_size, kept_blocks):
    row_block_count = D // (BLK * N_FSDP)
    col_blocks = FW // (BLK * N_TENSOR)
    count = row_block_count * col_blocks
    block_numbers = jnp.arange(count, dtype=jnp.int32)
    zero = jnp.zeros((), jnp.bfloat16)

    def one_group(total, inputs):
        acts, cots, resid, picks = inputs
        gradient = jnp.dot(acts.T, cots, preferred_element_type=jnp.float32)
        accumulated = resid.astype(jnp.float32) + step_size[0] * gradient
        rounded = accumulated.astype(jnp.bfloat16)
        chosen = jnp.any(block_numbers[None, None, :, None] == picks[:, :, None, :], axis=3)
        chosen = chosen.reshape(N_FSDP, N_TENSOR, row_block_count, col_blocks).transpose(0, 2, 1, 3)
        chosen = chosen[:, :, None, :, :, None]
        shaped = rounded.reshape(N_FSDP, row_block_count, BLK, N_TENSOR, col_blocks, BLK)
        sent = jnp.where(chosen, shaped, zero)
        new_resid = jnp.where(chosen, zero, shaped).reshape(D, FW)
        blocks = sent.transpose(0, 3, 1, 4, 2, 5).reshape(N_FSDP, N_TENSOR, count, BLK, BLK)
        return total + blocks.astype(jnp.float32), new_resid

    initial_total = jnp.zeros((N_FSDP, N_TENSOR, count, BLK, BLK), jnp.float32)
    inputs = (activations.reshape(N_DP, TOKG, D), cotangent.reshape(N_DP, TOKG, FW), residual, kept_blocks)
    total, residual_out = lax.scan(one_group, initial_total, inputs)
    owned = total.reshape(N_FSDP, N_TENSOR, count // N_DP, N_DP, BLK, BLK).transpose(3, 0, 1, 2, 4, 5)

    input_grad = jnp.dot(cotangent, weight.T, preferred_element_type=jnp.float32).astype(jnp.bfloat16)
    return input_grad, residual_out, owned
```

```python
import functools

import jax
import jax.numpy as jnp
from jax import lax
from jax.experimental import pallas as pl
from jax.experimental.pallas import tpu as pltpu
from jax.sharding import PartitionSpec as P

BLK = 128
VMEM_LIMIT = 56 * 1024 * 1024


def cost(flops, nbytes):
    return pl.CostEstimate(flops=flops, bytes_accessed=nbytes, transcendentals=0)


def params():
    return pltpu.CompilerParams(vmem_limit_bytes=VMEM_LIMIT)


def dot_nt(a, b):
    return lax.dot_general(a, b, (((1,), (1,)), ((), ())), preferred_element_type=jnp.float32)


def dot_nn(a, b):
    return lax.dot_general(a, b, (((1,), (0,)), ((), ())), preferred_element_type=jnp.float32)


def input_grad_kernel(split, zero_copies, here_ref, cot_ref, w_ref, *refs):
    if split:
        away_ref, own_ref, owned_ref, acc_ref, zero_ref, sem = refs
    else:
        own_ref, owned_ref, acc_ref, zero_ref, sem = refs
    step = pl.program_id(0)
    steps = pl.num_programs(0)
    zero_rows = zero_ref.shape[0]

    def zero_copy(i):
        return pltpu.make_async_copy(zero_ref, owned_ref.at[pl.ds(i * zero_rows, zero_rows)], sem.at[i])

    @pl.when(step == 0)
    def _():
        zero_ref[...] = jnp.zeros_like(zero_ref)
        for i in range(zero_copies):
            zero_copy(i).start()
        acc_ref[...] = dot_nt(cot_ref[...], w_ref[...])

    @pl.when(step > 0)
    def _():
        acc_ref[...] += dot_nt(cot_ref[...], w_ref[...])

    @pl.when(step == steps - 1)
    def _():
        if split:
            half = own_ref.shape[0]
            mine = pl.multiple_of(here_ref[0] * half, half)
            others = pl.multiple_of((1 - here_ref[0]) * half, half)
            away_ref[...] = acc_ref[pl.ds(others, half), :].astype(jnp.bfloat16)
            own_ref[...] = acc_ref[pl.ds(mine, half), :]
        else:
            own_ref[...] = acc_ref[...]
        for i in range(zero_copies):
            zero_copy(i).wait()


def input_grad_partials(here, cot, weight, owned_count, split):
    tokens, cols = cot.shape
    rows = weight.shape[0]
    tile = min(1024, cols)
    own_rows = tokens // 2 if split else tokens
    zero_rows = min(16, owned_count)
    zero_copies = owned_count // zero_rows
    out_shape = [
        jax.ShapeDtypeStruct((own_rows, rows), jnp.float32),
        jax.ShapeDtypeStruct((owned_count, BLK, BLK), jnp.float32),
    ]
    out_specs = [
        pl.BlockSpec((own_rows, rows), lambda k, *_: (0, 0)),
        pl.BlockSpec(memory_space=pl.ANY),
    ]
    if split:
        out_shape.insert(0, jax.ShapeDtypeStruct((own_rows, rows), jnp.bfloat16))
        out_specs.insert(0, pl.BlockSpec((own_rows, rows), lambda k, *_: (0, 0)))
    return pl.pallas_call(
        functools.partial(input_grad_kernel, split, zero_copies),
        out_shape=out_shape,
        grid_spec=pltpu.PrefetchScalarGridSpec(
            num_scalar_prefetch=1,
            grid=(cols // tile,),
            in_specs=[
                pl.BlockSpec((tokens, tile), lambda k, *_: (0, k)),
                pl.BlockSpec((rows, tile), lambda k, *_: (0, k)),
            ],
            out_specs=out_specs,
            scratch_shapes=[
                pltpu.VMEM((tokens, rows), jnp.float32),
                pltpu.VMEM((zero_rows, BLK, BLK), jnp.float32),
                pltpu.SemaphoreType.DMA((zero_copies,)),
            ],
        ),
        compiler_params=params(),
        cost_estimate=cost(2 * tokens * rows * cols, 2 * cols * (tokens + rows) + 4 * owned_count * BLK * BLK),
        name="input_grad_partials",
    )(here, cot, weight)


def kept_kernel(pieces, kept_ref, place_ref, step_ref, *refs):
    act_refs = refs[:pieces]
    cot_ref, res_ref, acts_t_ref, out_ref = refs[pieces:]
    k = pl.program_id(0)
    col_blocks = place_ref[pieces]

    @pl.when(k == 0)
    def _():
        for i, act_ref in enumerate(act_refs):
            size = act_ref.shape[0]
            at = pl.multiple_of(place_ref[i] * size, size)
            acts_t_ref[:, pl.ds(at, size)] = act_ref[...].T

    row = pl.multiple_of(kept_ref[k] // col_blocks * BLK, BLK)
    gradient = dot_nn(acts_t_ref[pl.ds(row, BLK), :], cot_ref[...])
    out_ref[...] = (res_ref[...].astype(jnp.float32) + step_ref[0] * gradient).astype(jnp.bfloat16)


def kept_blocks_of(kept, place, step_size, acts, cot, residual):
    tokens, cols = cot.shape
    rows = residual.shape[0]
    col_blocks = cols // BLK
    keep = kept.shape[0]
    return pl.pallas_call(
        functools.partial(kept_kernel, len(acts)),
        out_shape=[
            jax.ShapeDtypeStruct((rows, tokens), jnp.bfloat16),
            jax.ShapeDtypeStruct((keep * BLK, BLK), jnp.bfloat16),
        ],
        grid_spec=pltpu.PrefetchScalarGridSpec(
            num_scalar_prefetch=3,
            grid=(keep,),
            in_specs=[pl.BlockSpec(a.shape, lambda k, *_: (0, 0)) for a in acts]
            + [
                pl.BlockSpec((tokens, BLK), lambda k, kept, *_: (0, kept[k] % col_blocks)),
                pl.BlockSpec((BLK, BLK), lambda k, kept, *_: (kept[k] // col_blocks, kept[k] % col_blocks)),
            ],
            out_specs=[
                pl.BlockSpec((rows, tokens), lambda k, *_: (0, 0)),
                pl.BlockSpec((BLK, BLK), lambda k, *_: (k, 0)),
            ],
        ),
        compiler_params=params(),
        cost_estimate=cost(2 * tokens * BLK * BLK * keep, 4 * tokens * rows + 2 * keep * tokens * BLK),
        name="kept_blocks",
    )(kept, place, step_size, *acts, cot, residual)


def residual_kernel(chunk, col_blocks, kept_ref, step_ref, acts_t_ref, cot_ref, res_ref, out_ref):
    step = step_ref[0]
    rows, tile = out_ref.shape
    cot = cot_ref[...]
    for at in range(0, rows, chunk):
        gradient = dot_nn(acts_t_ref[at : at + chunk, :], cot)
        out_ref[at : at + chunk, :] = (res_ref[at : at + chunk, :].astype(jnp.float32) + step * gradient).astype(
            jnp.bfloat16
        )
    tile_blocks = tile // BLK
    first = pl.program_id(0) * tile_blocks
    for k in range(kept_ref.shape[0]):
        col = kept_ref[k] % col_blocks - first

        @pl.when((col >= 0) & (col < tile_blocks))
        def _():
            row = pl.multiple_of(kept_ref[k] // col_blocks * BLK, BLK)
            out_ref[pl.ds(row, BLK), pl.ds(pl.multiple_of(col * BLK, BLK), BLK)] = jnp.zeros((BLK, BLK), jnp.bfloat16)


def residual_of(kept, step_size, acts_t, cot, residual):
    tokens, cols = cot.shape
    rows = residual.shape[0]
    tile = min(512, cols)
    return pl.pallas_call(
        functools.partial(residual_kernel, min(256, rows), cols // BLK),
        out_shape=jax.ShapeDtypeStruct((rows, cols), jnp.bfloat16),
        grid_spec=pltpu.PrefetchScalarGridSpec(
            num_scalar_prefetch=2,
            grid=(cols // tile,),
            in_specs=[
                pl.BlockSpec((rows, tokens), lambda j, *_: (0, 0)),
                pl.BlockSpec((tokens, tile), lambda j, *_: (0, j)),
                pl.BlockSpec((rows, tile), lambda j, *_: (0, j)),
            ],
            out_specs=pl.BlockSpec((rows, tile), lambda j, *_: (0, j)),
        ),
        compiler_params=params(),
        cost_estimate=cost(2 * tokens * rows * cols, 2 * tokens * (rows + cols) + 4 * rows * cols),
        name="residual_out",
    )(kept, step_size, acts_t, cot, residual)


def owned_kernel(groups, keep, label_ref, me_ref, *refs):
    block_refs = refs[:groups]
    _, out_ref, sum_ref, sem = refs[groups:]
    total = groups * keep
    me = me_ref[0]

    def copy(i):
        return pltpu.make_async_copy(sum_ref.at[i], out_ref.at[label_ref[i] // groups], sem.at[i])

    def is_first(i):
        first = label_ref[i] % groups == me
        for j in range(i // keep * keep):
            first &= label_ref[j] != label_ref[i]
        return first

    firsts = [is_first(i) for i in range(total)]
    for i in range(total):

        @pl.when(firsts[i])
        def _(i=i):
            group, slot = i // keep, i % keep
            sum_ref[i] = block_refs[group][slot * BLK : (slot + 1) * BLK, :].astype(jnp.float32)
            for j in range((group + 1) * keep, total):

                @pl.when(label_ref[j] == label_ref[i])
                def _():
                    at = j % keep * BLK
                    sum_ref[i] += block_refs[j // keep][at : at + BLK, :].astype(jnp.float32)

            copy(i).start()

    for i in range(total):

        @pl.when(firsts[i])
        def _(i=i):
            copy(i).wait()


def owned_of(labels, me, blocks, zeros):
    groups = len(blocks)
    keep = labels.shape[0] // groups
    return pl.pallas_call(
        functools.partial(owned_kernel, groups, keep),
        out_shape=jax.ShapeDtypeStruct(zeros.shape, zeros.dtype),
        grid_spec=pltpu.PrefetchScalarGridSpec(
            num_scalar_prefetch=2,
            grid=(1,),
            in_specs=[pl.BlockSpec(b.shape, lambda i, *_: (0, 0)) for b in blocks]
            + [pl.BlockSpec(memory_space=pl.ANY)],
            out_specs=pl.BlockSpec(memory_space=pl.ANY),
            scratch_shapes=[
                pltpu.VMEM((groups * keep, BLK, BLK), jnp.float32),
                pltpu.SemaphoreType.DMA((groups * keep,)),
            ],
        ),
        input_output_aliases={2 + groups: 0},
        compiler_params=params(),
        cost_estimate=cost(groups * keep * BLK * BLK, groups * keep * BLK * BLK * 6),
        name="owned",
    )(labels, me, *blocks, zeros)


def swapped(x, axis, mask):
    return lax.ppermute(x, axis, [(i, i ^ mask) for i in range(lax.axis_size(axis))])


def of_all_groups(x):
    pieces = [x]
    mask = lax.axis_size("dp") // 2
    while mask:
        pieces += [swapped(p, "dp", mask) for p in pieces]
        mask //= 2
    return pieces


def body(activations, cotangent, weight, residual, step_size, kept_blocks):
    rows, cols = weight.shape
    groups = lax.axis_size("dp")
    owned_count = (rows // BLK) * (cols // BLK) // groups
    kept = kept_blocks.reshape(-1)
    me = lax.axis_index("dp").astype(jnp.int32).reshape(1)
    here = lax.axis_index("tensor").astype(jnp.int32)
    pair = lax.axis_size("tensor") == 2
    if pair:
        acts = [activations, swapped(activations, "tensor", 1)]
        places = [here, 1 - here]
    else:
        acts = [lax.all_gather(activations, "tensor", axis=0, tiled=True)]
        places = [jnp.zeros((), jnp.int32)]
    place = jnp.stack(places + [jnp.full((), cols // BLK, jnp.int32)])
    labels = jnp.concatenate(of_all_groups(kept))

    if pair:
        away, own, zeros = input_grad_partials(here.reshape(1), cotangent, weight, owned_count, True)
        arrived = swapped(away, "tensor", 1)
    else:
        own, zeros = input_grad_partials(here.reshape(1), cotangent, weight, owned_count, False)
        summed = lax.psum_scatter(own, "tensor", scatter_dimension=0, tiled=True)

    acts_t, blocks = kept_blocks_of(kept, place, step_size, acts, cotangent, residual[0])
    all_blocks = of_all_groups(blocks)
    residual_out = residual_of(kept, step_size, acts_t, cotangent, residual[0])
    owned = owned_of(labels, me, all_blocks, zeros)
    if pair:
        summed = own + arrived.astype(jnp.float32)
    return (summed.astype(jnp.bfloat16), residual_out[None], owned.reshape(1, 1, 1, owned_count, BLK, BLK))


def solution(mesh):
    in_specs = (
        P(("dp", "tensor"), "fsdp"),
        P("dp", "tensor"),
        P("fsdp", "tensor"),
        P("dp", "fsdp", "tensor"),
        P(),
        P("dp", "fsdp", "tensor", None),
    )
    out_specs = (
        P(("dp", "tensor"), "fsdp"),
        P("dp", "fsdp", "tensor"),
        P("dp", "fsdp", "tensor", None, None, None),
    )
    return jax.shard_map(body, mesh=mesh, in_specs=in_specs, out_specs=out_specs, check_vma=False)
```

```python
import functools

import jax
import jax.numpy as jnp
from jax import lax
from jax.experimental import pallas as pl
from jax.experimental.pallas import tpu as pltpu
from jax.sharding import PartitionSpec as P

BLK = 128
MIB = 1024 * 1024


def cost(flops, nbytes):
    return pl.CostEstimate(flops=flops, bytes_accessed=nbytes, transcendentals=0)


def params(mib):
    return pltpu.CompilerParams(vmem_limit_bytes=mib * MIB)


def dot_nt(a, b):
    return lax.dot_general(a, b, (((1,), (1,)), ((), ())), preferred_element_type=jnp.float32)


def dot_nn(a, b):
    return lax.dot_general(a, b, (((1,), (0,)), ((), ())), preferred_element_type=jnp.float32)


def input_grad_kernel(split, zero_copies, here_ref, cot_ref, w_ref, *refs):
    if split:
        away_ref, own_ref, owned_ref, acc_ref, zero_ref, sem = refs
    else:
        own_ref, owned_ref, acc_ref, zero_ref, sem = refs
    step = pl.program_id(0)
    steps = pl.num_programs(0)
    zero_rows = zero_ref.shape[0]
    rows = w_ref.shape[0]
    chunk = min(256, rows)

    def zero_copy(i):
        return pltpu.make_async_copy(zero_ref, owned_ref.at[pl.ds(i * zero_rows, zero_rows)], sem.at[i])

    @pl.when(step == 0)
    def _():
        zero_ref[...] = jnp.zeros_like(zero_ref)
        for i in range(zero_copies):
            zero_copy(i).start()
        for at in range(0, rows, chunk):
            acc_ref[:, at : at + chunk] = dot_nt(cot_ref[...], w_ref[at : at + chunk, :])

    @pl.when(step > 0)
    def _():
        for at in range(0, rows, chunk):
            acc_ref[:, at : at + chunk] += dot_nt(cot_ref[...], w_ref[at : at + chunk, :])

    @pl.when(step == steps - 1)
    def _():
        if split:
            half = own_ref.shape[0]
            mine = pl.multiple_of(here_ref[0] * half, half)
            others = pl.multiple_of((1 - here_ref[0]) * half, half)
            away_ref[...] = acc_ref[pl.ds(others, half), :].astype(jnp.bfloat16)
            own_ref[...] = acc_ref[pl.ds(mine, half), :]
        else:
            own_ref[...] = acc_ref[...]
        for i in range(zero_copies):
            zero_copy(i).wait()


def input_grad_partials(here, cot, weight, owned_count, split):
    tokens, cols = cot.shape
    rows = weight.shape[0]
    tile = min(1024, cols)
    own_rows = tokens // 2 if split else tokens
    zero_rows = min(16, owned_count)
    zero_copies = owned_count // zero_rows
    out_shape = [
        jax.ShapeDtypeStruct((own_rows, rows), jnp.float32),
        jax.ShapeDtypeStruct((owned_count, BLK, BLK), jnp.float32),
    ]
    out_specs = [
        pl.BlockSpec((own_rows, rows), lambda k, *_: (0, 0)),
        pl.BlockSpec(memory_space=pl.ANY),
    ]
    if split:
        out_shape.insert(0, jax.ShapeDtypeStruct((own_rows, rows), jnp.bfloat16))
        out_specs.insert(0, pl.BlockSpec((own_rows, rows), lambda k, *_: (0, 0)))
    return pl.pallas_call(
        functools.partial(input_grad_kernel, split, zero_copies),
        out_shape=out_shape,
        grid_spec=pltpu.PrefetchScalarGridSpec(
            num_scalar_prefetch=1,
            grid=(cols // tile,),
            in_specs=[
                pl.BlockSpec((tokens, tile), lambda k, *_: (0, k)),
                pl.BlockSpec((rows, tile), lambda k, *_: (0, k)),
            ],
            out_specs=out_specs,
            scratch_shapes=[
                pltpu.VMEM((tokens, rows), jnp.float32),
                pltpu.VMEM((zero_rows, BLK, BLK), jnp.float32),
                pltpu.SemaphoreType.DMA((zero_copies,)),
            ],
        ),
        compiler_params=params(36),
        cost_estimate=cost(2 * tokens * rows * cols, 2 * cols * (tokens + rows) + 4 * owned_count * BLK * BLK),
        name="input_grad_partials",
    )(here, cot, weight)


def kept_kernel(pieces, col_blocks, kept_ref, here_ref, step_ref, *refs):
    act_refs = refs[:pieces]
    cot_ref, res_ref, acts_t_out, out_ref, acts_t_ref, cot_buf, res_buf, cot_sem, res_sem, out_sem = refs[pieces:]
    keep = cot_buf.shape[0]

    def copies(k):
        row = pl.multiple_of(kept_ref[k] // col_blocks * BLK, BLK)
        col = pl.multiple_of(kept_ref[k] % col_blocks * BLK, BLK)
        return (
            pltpu.make_async_copy(cot_ref.at[:, pl.ds(col, BLK)], cot_buf.at[k], cot_sem.at[k]),
            pltpu.make_async_copy(res_ref.at[pl.ds(row, BLK), pl.ds(col, BLK)], res_buf.at[k], res_sem.at[k]),
        )

    for k in range(keep):
        for copy in copies(k):
            copy.start()
    for i, act_ref in enumerate(act_refs):
        size = act_ref.shape[0]
        at = here_ref[0] if i == 0 else 1 - here_ref[0]
        at = pl.multiple_of(at * size, size) if pieces > 1 else 0
        acts_t_ref[:, pl.ds(at, size)] = act_ref[...].T
    out_copy = pltpu.make_async_copy(acts_t_ref, acts_t_out, out_sem)
    out_copy.start()
    for k in range(keep):
        for copy in copies(k):
            copy.wait()
        row = pl.multiple_of(kept_ref[k] // col_blocks * BLK, BLK)
        gradient = dot_nn(acts_t_ref[pl.ds(row, BLK), :], cot_buf[k])
        out_ref[k * BLK : (k + 1) * BLK, :] = (res_buf[k].astype(jnp.float32) + step_ref[0] * gradient).astype(
            jnp.bfloat16
        )
    out_copy.wait()


def kept_blocks_of(kept, here, step_size, acts, cot, residual):
    tokens, cols = cot.shape
    rows = residual.shape[0]
    keep = kept.shape[0]
    return pl.pallas_call(
        functools.partial(kept_kernel, len(acts), cols // BLK),
        out_shape=[
            jax.ShapeDtypeStruct((rows, tokens), jnp.bfloat16),
            jax.ShapeDtypeStruct((keep * BLK, BLK), jnp.bfloat16),
        ],
        grid_spec=pltpu.PrefetchScalarGridSpec(
            num_scalar_prefetch=3,
            grid=(1,),
            in_specs=[pl.BlockSpec(a.shape, lambda k, *_: (0, 0)) for a in acts]
            + [pl.BlockSpec(memory_space=pl.ANY), pl.BlockSpec(memory_space=pl.ANY)],
            out_specs=[
                pl.BlockSpec(memory_space=pl.ANY),
                pl.BlockSpec((keep * BLK, BLK), lambda k, *_: (0, 0)),
            ],
            scratch_shapes=[
                pltpu.VMEM((rows, tokens), jnp.bfloat16),
                pltpu.VMEM((keep, tokens, BLK), jnp.bfloat16),
                pltpu.VMEM((keep, BLK, BLK), jnp.bfloat16),
                pltpu.SemaphoreType.DMA((keep,)),
                pltpu.SemaphoreType.DMA((keep,)),
                pltpu.SemaphoreType.DMA,
            ],
        ),
        compiler_params=params(24),
        cost_estimate=cost(2 * tokens * BLK * BLK * keep, 4 * tokens * rows + 2 * keep * tokens * BLK),
        name="kept_blocks",
    )(kept, here, step_size, *acts, cot, residual)


def residual_kernel(chunk, col_blocks, kept_ref, step_ref, acts_t_ref, cot_ref, res_ref, out_ref):
    step = step_ref[0]
    tile = out_ref.shape[1]
    for at in range(0, tile, chunk):
        part = slice(at, at + chunk)
        gradient = dot_nn(acts_t_ref[...], cot_ref[:, part])
        out_ref[:, part] = (res_ref[:, part].astype(jnp.float32) + step * gradient).astype(jnp.bfloat16)
    tile_blocks = tile // BLK
    first = pl.program_id(0) * tile_blocks
    for k in range(kept_ref.shape[0]):
        col = kept_ref[k] % col_blocks - first

        @pl.when((col >= 0) & (col < tile_blocks))
        def _():
            row = pl.multiple_of(kept_ref[k] // col_blocks * BLK, BLK)
            out_ref[pl.ds(row, BLK), pl.ds(pl.multiple_of(col * BLK, BLK), BLK)] = jnp.zeros((BLK, BLK), jnp.bfloat16)


def residual_of(kept, step_size, acts_t, cot, residual):
    tokens, cols = cot.shape
    rows = residual.shape[0]
    tile = min(1024, cols)
    return pl.pallas_call(
        functools.partial(residual_kernel, min(512, tile), cols // BLK),
        out_shape=jax.ShapeDtypeStruct((rows, cols), jnp.bfloat16),
        grid_spec=pltpu.PrefetchScalarGridSpec(
            num_scalar_prefetch=2,
            grid=(cols // tile,),
            in_specs=[
                pl.BlockSpec((rows, tokens), lambda j, *_: (0, 0)),
                pl.BlockSpec((tokens, tile), lambda j, *_: (0, j)),
                pl.BlockSpec((rows, tile), lambda j, *_: (0, j)),
            ],
            out_specs=pl.BlockSpec((rows, tile), lambda j, *_: (0, j)),
        ),
        compiler_params=params(36),
        cost_estimate=cost(2 * tokens * rows * cols, 2 * tokens * (rows + cols) + 4 * rows * cols),
        name="residual_out",
    )(kept, step_size, acts_t, cot, residual)


def owned_kernel(groups, keep, me_ref, *refs):
    label_refs = refs[:groups]
    block_refs = refs[groups : 2 * groups]
    _, out_ref, sum_ref, slot_ref, sem = refs[2 * groups :]
    total = groups * keep
    me = me_ref[0]

    def place(i):
        return label_refs[i // keep][i % keep] // groups

    def mine(i):
        return label_refs[i // keep][i % keep] % groups == me

    def copy(i):
        return pltpu.make_async_copy(sum_ref.at[i], out_ref.at[place(i)], sem.at[i])

    for i in range(total):
        slot_ref[place(i)] = total
    for i in range(total):

        @pl.when(mine(i))
        def _(i=i):
            at = i % keep * BLK
            block = block_refs[i // keep][at : at + BLK, :].astype(jnp.float32)
            slot = slot_ref[place(i)]

            @pl.when(slot == total)
            def _():
                sum_ref[i] = block
                slot_ref[place(i)] = i

            @pl.when(slot < total)
            def _():
                sum_ref[slot] += block

    for i in range(total):

        @pl.when(mine(i) & (slot_ref[place(i)] == i))
        def _(i=i):
            copy(i).start()

    for i in range(total):

        @pl.when(mine(i) & (slot_ref[place(i)] == i))
        def _(i=i):
            copy(i).wait()


def owned_of(labels, me, blocks, zeros):
    groups = len(blocks)
    keep = labels[0].shape[0]
    return pl.pallas_call(
        functools.partial(owned_kernel, groups, keep),
        out_shape=jax.ShapeDtypeStruct(zeros.shape, zeros.dtype),
        grid_spec=pltpu.PrefetchScalarGridSpec(
            num_scalar_prefetch=1 + groups,
            grid=(1,),
            in_specs=[pl.BlockSpec(b.shape, lambda i, *_: (0, 0)) for b in blocks]
            + [pl.BlockSpec(memory_space=pl.ANY)],
            out_specs=pl.BlockSpec(memory_space=pl.ANY),
            scratch_shapes=[
                pltpu.VMEM((groups * keep, BLK, BLK), jnp.float32),
                pltpu.SMEM((zeros.shape[0],), jnp.int32),
                pltpu.SemaphoreType.DMA((groups * keep,)),
            ],
        ),
        input_output_aliases={1 + 2 * groups: 0},
        compiler_params=params(16),
        cost_estimate=cost(groups * keep * BLK * BLK, groups * keep * BLK * BLK * 6),
        name="owned",
    )(me, *labels, *blocks, zeros)


def swapped(x, axis, mask):
    return lax.ppermute(x, axis, [(i, i ^ mask) for i in range(lax.axis_size(axis))])


def of_all_groups(x):
    return [x] + [swapped(x, "dp", mask) for mask in range(1, lax.axis_size("dp"))]


def body(activations, cotangent, weight, residual, step_size, kept_blocks):
    rows, cols = weight.shape
    groups = lax.axis_size("dp")
    owned_count = (rows // BLK) * (cols // BLK) // groups
    kept = kept_blocks.reshape(-1)
    me = lax.axis_index("dp").astype(jnp.int32).reshape(1)
    here = lax.axis_index("tensor").astype(jnp.int32).reshape(1)
    pair = lax.axis_size("tensor") == 2
    if pair:
        acts = [activations, swapped(activations, "tensor", 1)]
        away, own, zeros = input_grad_partials(here, cotangent, weight, owned_count, True)
        kept, away = lax.optimization_barrier((kept, away))
        arrived = swapped(away, "tensor", 1)
    else:
        acts = [lax.all_gather(activations, "tensor", axis=0, tiled=True)]
        own, zeros = input_grad_partials(here, cotangent, weight, owned_count, False)
        summed = lax.psum_scatter(own, "tensor", scatter_dimension=0, tiled=True)
    labels = of_all_groups(kept)
    acts_t, blocks = kept_blocks_of(kept, here, step_size, acts, cotangent, residual[0])
    all_blocks = of_all_groups(blocks)
    residual_out = residual_of(kept, step_size, acts_t, cotangent, residual[0])
    owned = owned_of(labels, me, all_blocks, zeros)
    if pair:
        summed = own + arrived.astype(jnp.float32)
    return (summed.astype(jnp.bfloat16), residual_out[None], owned.reshape(1, 1, 1, owned_count, BLK, BLK))


def solution(mesh):
    in_specs = (
        P(("dp", "tensor"), "fsdp"),
        P("dp", "tensor"),
        P("fsdp", "tensor"),
        P("dp", "fsdp", "tensor"),
        P(),
        P("dp", "fsdp", "tensor", None),
    )
    out_specs = (
        P(("dp", "tensor"), "fsdp"),
        P("dp", "fsdp", "tensor"),
        P("dp", "fsdp", "tensor", None, None, None),
    )
    return jax.shard_map(body, mesh=mesh, in_specs=in_specs, out_specs=out_specs, check_vma=False)
```

```python
import functools

import jax
import jax.numpy as jnp
from jax import lax
from jax.experimental import pallas as pl
from jax.experimental.pallas import tpu as pltpu
from jax.sharding import PartitionSpec as P

BLK = 128
MIB = 1024 * 1024
LABEL_ROWS = 16
RADIX = 16


def cost(flops, nbytes):
    return pl.CostEstimate(flops=flops, bytes_accessed=nbytes, transcendentals=0)


def params(mib):
    return pltpu.CompilerParams(vmem_limit_bytes=mib * MIB)


def dot_nt(a, b):
    return lax.dot_general(a, b, (((1,), (1,)), ((), ())), preferred_element_type=jnp.float32)


def dot_nn(a, b):
    return lax.dot_general(a, b, (((1,), (0,)), ((), ())), preferred_element_type=jnp.float32)


def input_grad_kernel(split, zero_copies, here_ref, cot_ref, w_ref, *refs):
    if split:
        away_ref, own_ref, owned_ref, acc_ref, zero_ref, sem = refs
    else:
        own_ref, owned_ref, acc_ref, zero_ref, sem = refs
    step = pl.program_id(0)
    steps = pl.num_programs(0)
    zero_rows = zero_ref.shape[0]
    rows = w_ref.shape[0]
    chunk = min(256, rows)

    def zero_copy(i):
        return pltpu.make_async_copy(zero_ref, owned_ref.at[pl.ds(i * zero_rows, zero_rows)], sem.at[i])

    @pl.when(step == 0)
    def _():
        zero_ref[...] = jnp.zeros_like(zero_ref)
        for i in range(zero_copies):
            zero_copy(i).start()
        for at in range(0, rows, chunk):
            acc_ref[:, at : at + chunk] = dot_nt(cot_ref[...], w_ref[at : at + chunk, :])

    @pl.when(step > 0)
    def _():
        for at in range(0, rows, chunk):
            acc_ref[:, at : at + chunk] += dot_nt(cot_ref[...], w_ref[at : at + chunk, :])

    @pl.when(step == steps - 1)
    def _():
        if split:
            half = own_ref.shape[0]
            mine = pl.multiple_of(here_ref[0] * half, half)
            others = pl.multiple_of((1 - here_ref[0]) * half, half)
            away_ref[...] = acc_ref[pl.ds(others, half), :].astype(jnp.bfloat16)
            own_ref[...] = acc_ref[pl.ds(mine, half), :]
        else:
            own_ref[...] = acc_ref[...]
        for i in range(zero_copies):
            zero_copy(i).wait()


def input_grad_partials(here, cot, weight, owned_count, split):
    tokens, cols = cot.shape
    rows = weight.shape[0]
    tile = min(2048, cols)
    own_rows = tokens // 2 if split else tokens
    zero_rows = min(16, owned_count)
    zero_copies = owned_count // zero_rows
    out_shape = [
        jax.ShapeDtypeStruct((own_rows, rows), jnp.float32),
        jax.ShapeDtypeStruct((owned_count, BLK, BLK), jnp.float32),
    ]
    out_specs = [
        pl.BlockSpec((own_rows, rows), lambda k, *_: (0, 0)),
        pl.BlockSpec(memory_space=pl.ANY),
    ]
    if split:
        out_shape.insert(0, jax.ShapeDtypeStruct((own_rows, rows), jnp.bfloat16))
        out_specs.insert(0, pl.BlockSpec((own_rows, rows), lambda k, *_: (0, 0)))
    return pl.pallas_call(
        functools.partial(input_grad_kernel, split, zero_copies),
        out_shape=out_shape,
        grid_spec=pltpu.PrefetchScalarGridSpec(
            num_scalar_prefetch=1,
            grid=(cols // tile,),
            in_specs=[
                pl.BlockSpec((tokens, tile), lambda k, *_: (0, k)),
                pl.BlockSpec((rows, tile), lambda k, *_: (0, k)),
            ],
            out_specs=out_specs,
            scratch_shapes=[
                pltpu.VMEM((tokens, rows), jnp.float32),
                pltpu.VMEM((zero_rows, BLK, BLK), jnp.float32),
                pltpu.SemaphoreType.DMA((zero_copies,)),
            ],
        ),
        compiler_params=params(48),
        cost_estimate=cost(2 * tokens * rows * cols, 2 * cols * (tokens + rows) + 4 * owned_count * BLK * BLK),
        name="input_grad_partials",
    )(here, cot, weight)


def kept_kernel(pieces, col_blocks, kept_ref, here_ref, step_ref, *refs):
    act_refs = refs[:pieces]
    cot_ref, res_ref, acts_t_out, out_ref, acts_t_ref, cot_buf, res_buf, cot_sem, res_sem, out_sem = refs[pieces:]
    keep = cot_buf.shape[0]

    def copies(k):
        row = pl.multiple_of(kept_ref[k] // col_blocks * BLK, BLK)
        col = pl.multiple_of(kept_ref[k] % col_blocks * BLK, BLK)
        return (
            pltpu.make_async_copy(cot_ref.at[:, pl.ds(col, BLK)], cot_buf.at[k], cot_sem.at[k]),
            pltpu.make_async_copy(res_ref.at[pl.ds(row, BLK), pl.ds(col, BLK)], res_buf.at[k], res_sem.at[k]),
        )

    for k in range(keep):
        for copy in copies(k):
            copy.start()
    for i, act_ref in enumerate(act_refs):
        size = act_ref.shape[0]
        at = here_ref[0] if i == 0 else 1 - here_ref[0]
        at = pl.multiple_of(at * size, size) if pieces > 1 else 0
        acts_t_ref[:, pl.ds(at, size)] = act_ref[...].T
    out_copy = pltpu.make_async_copy(acts_t_ref, acts_t_out, out_sem)
    out_copy.start()
    for k in range(keep):
        for copy in copies(k):
            copy.wait()
        row = pl.multiple_of(kept_ref[k] // col_blocks * BLK, BLK)
        gradient = dot_nn(acts_t_ref[pl.ds(row, BLK), :], cot_buf[k])
        out_ref[k * BLK : (k + 1) * BLK, :] = (res_buf[k].astype(jnp.float32) + step_ref[0] * gradient).astype(
            jnp.bfloat16
        )
    lane = lax.broadcasted_iota(jnp.int32, (LABEL_ROWS, BLK), 1)
    low = lax.broadcasted_iota(jnp.int32, (LABEL_ROWS, BLK), 0) % 2 == 1
    label = jnp.zeros((LABEL_ROWS, BLK), jnp.int32)
    for k in range(keep):
        digit = jnp.where(low, kept_ref[k] % RADIX, kept_ref[k] // RADIX)
        label = jnp.where(lane == k, digit, label)
    out_ref[keep * BLK :, :] = label.astype(jnp.float32).astype(jnp.bfloat16)
    out_copy.wait()


def kept_blocks_of(kept, here, step_size, acts, cot, residual):
    tokens, cols = cot.shape
    rows = residual.shape[0]
    keep = kept.shape[0]
    return pl.pallas_call(
        functools.partial(kept_kernel, len(acts), cols // BLK),
        out_shape=[
            jax.ShapeDtypeStruct((rows, tokens), jnp.bfloat16),
            jax.ShapeDtypeStruct((keep * BLK + LABEL_ROWS, BLK), jnp.bfloat16),
        ],
        grid_spec=pltpu.PrefetchScalarGridSpec(
            num_scalar_prefetch=3,
            grid=(1,),
            in_specs=[pl.BlockSpec(a.shape, lambda k, *_: (0, 0)) for a in acts]
            + [pl.BlockSpec(memory_space=pltpu.HBM), pl.BlockSpec(memory_space=pltpu.HBM)],
            out_specs=[
                pl.BlockSpec(memory_space=pl.ANY),
                pl.BlockSpec((keep * BLK + LABEL_ROWS, BLK), lambda k, *_: (0, 0)),
            ],
            scratch_shapes=[
                pltpu.VMEM((rows, tokens), jnp.bfloat16),
                pltpu.VMEM((keep, tokens, BLK), jnp.bfloat16),
                pltpu.VMEM((keep, BLK, BLK), jnp.bfloat16),
                pltpu.SemaphoreType.DMA((keep,)),
                pltpu.SemaphoreType.DMA((keep,)),
                pltpu.SemaphoreType.DMA,
            ],
        ),
        compiler_params=params(50),
        cost_estimate=cost(2 * tokens * BLK * BLK * keep, 4 * tokens * rows + 2 * keep * tokens * BLK),
        name="kept_blocks",
    )(kept, here, step_size, *acts, cot, residual)


def residual_kernel(chunk, col_blocks, kept_ref, step_ref, acts_t_ref, cot_ref, res_ref, out_ref):
    step = step_ref[0]
    tile = out_ref.shape[1]

    @pl.loop(0, tile // chunk)
    def _(c):
        part = pl.ds(pl.multiple_of(c * chunk, chunk), chunk)
        gradient = dot_nn(acts_t_ref[...], cot_ref[:, part])
        out_ref[:, part] = (res_ref[:, part].astype(jnp.float32) + step * gradient).astype(jnp.bfloat16)

    tile_blocks = tile // BLK
    first = pl.program_id(0) * tile_blocks
    for k in range(kept_ref.shape[0]):
        col = kept_ref[k] % col_blocks - first

        @pl.when((col >= 0) & (col < tile_blocks))
        def _():
            row = pl.multiple_of(kept_ref[k] // col_blocks * BLK, BLK)
            out_ref[pl.ds(row, BLK), pl.ds(pl.multiple_of(col * BLK, BLK), BLK)] = jnp.zeros((BLK, BLK), jnp.bfloat16)


def residual_of(kept, step_size, acts_t, cot, residual):
    tokens, cols = cot.shape
    rows = residual.shape[0]
    tile = min(1024, cols)
    return pl.pallas_call(
        functools.partial(residual_kernel, min(256, tile), cols // BLK),
        out_shape=jax.ShapeDtypeStruct((rows, cols), jnp.bfloat16),
        grid_spec=pltpu.PrefetchScalarGridSpec(
            num_scalar_prefetch=2,
            grid=(cols // tile,),
            in_specs=[
                pl.BlockSpec((rows, tokens), lambda j, *_: (0, 0)),
                pl.BlockSpec((tokens, tile), lambda j, *_: (0, j)),
                pl.BlockSpec((rows, tile), lambda j, *_: (0, j)),
            ],
            out_specs=pl.BlockSpec((rows, tile), lambda j, *_: (0, j)),
        ),
        compiler_params=params(50),
        cost_estimate=cost(2 * tokens * rows * cols, 2 * tokens * (rows + cols) + 4 * rows * cols),
        name="residual_out",
    )(kept, step_size, acts_t, cot, residual)


def finish_kernel(groups, keep, pair, me_ref, *refs):
    if pair:
        own_ref, arrived_ref, *refs = refs
    block_refs = refs[:groups]
    refs = refs[groups + 1 :]
    if pair:
        grad_ref, *refs = refs
    out_ref, sum_ref, slot_ref, label_ref, number_ref, sem, number_sem = refs
    total = groups * keep
    me = me_ref[0]

    def place(i):
        return number_ref[i // keep, i % keep] // groups

    def mine(i):
        return number_ref[i // keep, i % keep] % groups == me

    def is_slot(i):
        return mine(i) & (slot_ref[place(i)] == i)

    def copy(i):
        return pltpu.make_async_copy(sum_ref.at[i], out_ref.at[place(i)], sem.at[i])

    @pl.when(pl.program_id(0) == 0)
    def _():
        for g, block_ref in enumerate(block_refs):
            digits = block_ref[keep * BLK :, :].astype(jnp.float32).astype(jnp.int32)
            label_ref[g : g + 1, :] = digits[0:1, :] * RADIX + digits[1:2, :]
        numbers = pltpu.make_async_copy(label_ref, number_ref, number_sem)
        numbers.start()
        numbers.wait()
        for i in range(total):
            slot_ref[place(i)] = total
        for i in range(total):

            @pl.when(mine(i))
            def _(i=i):
                at = i % keep * BLK
                block = block_refs[i // keep][at : at + BLK, :].astype(jnp.float32)
                slot = slot_ref[place(i)]

                @pl.when(slot == total)
                def _():
                    sum_ref[i] = block
                    slot_ref[place(i)] = i

                @pl.when(slot < total)
                def _():
                    sum_ref[slot] += block

        for i in range(total):

            @pl.when(is_slot(i))
            def _(i=i):
                copy(i).start()

    if pair:
        grad_ref[...] = (own_ref[...] + arrived_ref[...].astype(jnp.float32)).astype(jnp.bfloat16)

    @pl.when(pl.program_id(0) == pl.num_programs(0) - 1)
    def _():
        for i in range(total):

            @pl.when(is_slot(i))
            def _(i=i):
                copy(i).wait()


def finish(me, keep, parts, blocks, zeros):
    groups = len(blocks)
    steps = 4 if parts else 1
    part_specs = []
    out_shape = [jax.ShapeDtypeStruct(zeros.shape, zeros.dtype)]
    out_specs = [pl.BlockSpec(memory_space=pl.ANY)]
    if parts:
        rows, width = parts[0].shape
        part_specs = [pl.BlockSpec((rows // steps, width), lambda i, *_: (i, 0)) for _ in parts]
        out_shape.insert(0, jax.ShapeDtypeStruct((rows, width), jnp.bfloat16))
        out_specs.insert(0, part_specs[0])
    return pl.pallas_call(
        functools.partial(finish_kernel, groups, keep, bool(parts)),
        out_shape=out_shape,
        grid_spec=pltpu.PrefetchScalarGridSpec(
            num_scalar_prefetch=1,
            grid=(steps,),
            in_specs=part_specs
            + [pl.BlockSpec(b.shape, lambda i, *_: (0, 0)) for b in blocks]
            + [pl.BlockSpec(memory_space=pl.ANY)],
            out_specs=out_specs,
            scratch_shapes=[
                pltpu.VMEM((groups * keep, BLK, BLK), jnp.float32),
                pltpu.SMEM((zeros.shape[0],), jnp.int32),
                pltpu.VMEM((8, BLK), jnp.int32),
                pltpu.SMEM((8, BLK), jnp.int32),
                pltpu.SemaphoreType.DMA((groups * keep,)),
                pltpu.SemaphoreType.DMA,
            ],
        ),
        input_output_aliases={1 + len(parts) + groups: len(out_shape) - 1},
        compiler_params=params(16),
        cost_estimate=cost(groups * keep * BLK * BLK, groups * keep * BLK * BLK * 8),
        name="finish",
    )(me, *parts, *blocks, zeros)


def swapped(x, axis, mask):
    return lax.ppermute(x, axis, [(i, i ^ mask) for i in range(lax.axis_size(axis))])


def of_all_groups(x):
    return [x] + [swapped(x, "dp", mask) for mask in range(1, lax.axis_size("dp"))]


def body(activations, cotangent, weight, residual, step_size, kept_blocks):
    rows, cols = weight.shape
    groups = lax.axis_size("dp")
    owned_count = (rows // BLK) * (cols // BLK) // groups
    kept = kept_blocks.reshape(-1)
    me = lax.axis_index("dp").astype(jnp.int32).reshape(1)
    here = lax.axis_index("tensor").astype(jnp.int32).reshape(1)
    pair = lax.axis_size("tensor") == 2
    if pair:
        acts = [activations, swapped(activations, "tensor", 1)]
        away, own, zeros = input_grad_partials(here, cotangent, weight, owned_count, True)
        parts = [own, swapped(away, "tensor", 1)]
    else:
        acts = [lax.all_gather(activations, "tensor", axis=0, tiled=True)]
        own, zeros = input_grad_partials(here, cotangent, weight, owned_count, False)
        summed = lax.psum_scatter(own, "tensor", scatter_dimension=0, tiled=True)
        parts = []
    acts_t, blocks = kept_blocks_of(kept, here, step_size, acts, cotangent, residual[0])
    all_blocks = of_all_groups(blocks)
    residual_out = residual_of(kept, step_size, acts_t, cotangent, residual[0])
    *grads, owned = finish(me, kept.shape[0], parts, all_blocks, zeros)
    input_grad = grads[0] if pair else summed.astype(jnp.bfloat16)
    return (input_grad, residual_out[None], owned.reshape(1, 1, 1, owned_count, BLK, BLK))


def solution(mesh):
    in_specs = (
        P(("dp", "tensor"), "fsdp"),
        P("dp", "tensor"),
        P("fsdp", "tensor"),
        P("dp", "fsdp", "tensor"),
        P(),
        P("dp", "fsdp", "tensor", None),
    )
    out_specs = (
        P(("dp", "tensor"), "fsdp"),
        P("dp", "fsdp", "tensor"),
        P("dp", "fsdp", "tensor", None, None, None),
    )
    return jax.shard_map(body, mesh=mesh, in_specs=in_specs, out_specs=out_specs, check_vma=False)
```

```python
import functools

import jax
import jax.numpy as jnp
from jax import lax
from jax.experimental import pallas as pl
from jax.experimental.pallas import tpu as pltpu
from jax.sharding import PartitionSpec as P

BLK = 128
MIB = 1024 * 1024
LABEL_ROWS = 16
RADIX = 16


def cost(flops, nbytes):
    return pl.CostEstimate(flops=flops, bytes_accessed=nbytes, transcendentals=0)


def params(mib):
    return pltpu.CompilerParams(vmem_limit_bytes=mib * MIB)


def dot_nt(a, b):
    return lax.dot_general(a, b, (((1,), (1,)), ((), ())), preferred_element_type=jnp.float32)


def dot_nn(a, b):
    return lax.dot_general(a, b, (((1,), (0,)), ((), ())), preferred_element_type=jnp.float32)


def hidden_chunks(cols):
    sizes = []
    for size in (512, 1536, 2048, 4096):
        if cols > sum(sizes):
            sizes.append(min(size, cols - sum(sizes)))
    while sum(sizes) < cols:
        sizes.append(min(4096, cols - sum(sizes)))
    return sizes


def smem():
    return pl.BlockSpec(memory_space=pltpu.SMEM)


def vmem():
    return pl.BlockSpec(memory_space=pltpu.VMEM)


def anywhere():
    return pl.BlockSpec(memory_space=pl.ANY)


def input_grad_kernel(split, sizes, zero_copies, here_ref, cot_ref, w_ref, *refs):
    if split:
        away_ref, *refs = refs
    own_ref, owned_ref, acc_ref, cot_buf, w_buf, zero_ref, cot_sem, w_sem, zero_sem, own_sem = refs
    zero_rows = zero_ref.shape[0]
    rows = w_ref.shape[0]
    width = min(256, rows)
    starts = [sum(sizes[:i]) for i in range(len(sizes))]

    def loads(i):
        part = slice(starts[i], starts[i] + sizes[i])
        return (
            pltpu.make_async_copy(cot_ref.at[:, part], cot_buf.at[:, part], cot_sem.at[i]),
            pltpu.make_async_copy(w_ref.at[:, part], w_buf.at[:, part], w_sem.at[i]),
        )

    def start(i):
        if i < len(sizes):
            for copy in loads(i):
                copy.start()

    def zero_copy(i):
        return pltpu.make_async_copy(zero_ref, owned_ref.at[pl.ds(i * zero_rows, zero_rows)], zero_sem.at[i])

    start(0)
    start(1)
    zero_ref[...] = jnp.zeros_like(zero_ref)
    for i in range(len(sizes)):
        for copy in loads(i):
            copy.wait()
        start(i + 2)
        if i == len(sizes) - 1:
            for z in range(zero_copies):
                zero_copy(z).start()
        part = slice(starts[i], starts[i] + sizes[i])
        for at in range(0, rows, width):
            term = dot_nt(cot_buf[:, part], w_buf[at : at + width, part])
            if i == 0:
                acc_ref[:, at : at + width] = term
            else:
                acc_ref[:, at : at + width] += term
    if split:
        half = own_ref.shape[0]
        mine = pl.multiple_of(here_ref[0] * half, half)
        others = pl.multiple_of((1 - here_ref[0]) * half, half)
        own_copy = pltpu.make_async_copy(acc_ref.at[pl.ds(mine, half), :], own_ref, own_sem)
        own_copy.start()
        away_ref[...] = acc_ref[pl.ds(others, half), :].astype(jnp.bfloat16)
    else:
        own_copy = pltpu.make_async_copy(acc_ref, own_ref, own_sem)
        own_copy.start()
    own_copy.wait()
    for z in range(zero_copies):
        zero_copy(z).wait()


def input_grad_partials(here, cot, weight, owned_count, split):
    tokens, cols = cot.shape
    rows = weight.shape[0]
    sizes = hidden_chunks(cols)
    own_rows = tokens // 2 if split else tokens
    zero_rows = min(16, owned_count)
    zero_copies = owned_count // zero_rows
    out_shape = [
        jax.ShapeDtypeStruct((own_rows, rows), jnp.float32),
        jax.ShapeDtypeStruct((owned_count, BLK, BLK), jnp.float32),
    ]
    out_specs = [anywhere(), anywhere()]
    if split:
        out_shape.insert(0, jax.ShapeDtypeStruct((own_rows, rows), jnp.bfloat16))
        out_specs.insert(0, vmem())
    return pl.pallas_call(
        functools.partial(input_grad_kernel, split, sizes, zero_copies),
        out_shape=out_shape,
        in_specs=[smem(), anywhere(), anywhere()],
        out_specs=out_specs,
        scratch_shapes=[
            pltpu.VMEM((tokens, rows), jnp.float32),
            pltpu.VMEM((tokens, cols), jnp.bfloat16),
            pltpu.VMEM((rows, cols), jnp.bfloat16),
            pltpu.VMEM((zero_rows, BLK, BLK), jnp.float32),
            pltpu.SemaphoreType.DMA((len(sizes),)),
            pltpu.SemaphoreType.DMA((len(sizes),)),
            pltpu.SemaphoreType.DMA((zero_copies,)),
            pltpu.SemaphoreType.DMA,
        ],
        compiler_params=params(50),
        cost_estimate=cost(2 * tokens * rows * cols, 2 * cols * (tokens + rows) + 4 * owned_count * BLK * BLK),
        name="input_grad_partials",
    )(here, cot, weight)


def kept_kernel(pieces, col_blocks, kept_ref, here_ref, step_ref, *refs):
    act_refs = refs[:pieces]
    cot_ref, res_ref, acts_t_out, out_ref, acts_t_ref, cot_buf, res_buf, cot_sem, res_sem, out_sem = refs[pieces:]
    keep = cot_buf.shape[0]

    def copies(k):
        row = pl.multiple_of(kept_ref[k] // col_blocks * BLK, BLK)
        col = pl.multiple_of(kept_ref[k] % col_blocks * BLK, BLK)
        return (
            pltpu.make_async_copy(cot_ref.at[:, pl.ds(col, BLK)], cot_buf.at[k], cot_sem.at[k]),
            pltpu.make_async_copy(res_ref.at[pl.ds(row, BLK), pl.ds(col, BLK)], res_buf.at[k], res_sem.at[k]),
        )

    for k in range(keep):
        for copy in copies(k):
            copy.start()
    for i, act_ref in enumerate(act_refs):
        size = act_ref.shape[0]
        at = here_ref[0] if i == 0 else 1 - here_ref[0]
        at = pl.multiple_of(at * size, size) if pieces > 1 else 0
        acts_t_ref[:, pl.ds(at, size)] = act_ref[...].T
    out_copy = pltpu.make_async_copy(acts_t_ref, acts_t_out, out_sem)
    out_copy.start()
    for k in range(keep):
        for copy in copies(k):
            copy.wait()
    for k in range(keep):
        row = pl.multiple_of(kept_ref[k] // col_blocks * BLK, BLK)
        gradient = dot_nn(acts_t_ref[pl.ds(row, BLK), :], cot_buf[k])
        out_ref[k * BLK : (k + 1) * BLK, :] = (res_buf[k].astype(jnp.float32) + step_ref[0] * gradient).astype(
            jnp.bfloat16
        )
    lane = lax.broadcasted_iota(jnp.int32, (LABEL_ROWS, BLK), 1)
    low = lax.broadcasted_iota(jnp.int32, (LABEL_ROWS, BLK), 0) % 2 == 1
    label = jnp.zeros((LABEL_ROWS, BLK), jnp.int32)
    for k in range(keep):
        digit = jnp.where(low, kept_ref[k] % RADIX, kept_ref[k] // RADIX)
        label = jnp.where(lane == k, digit, label)
    out_ref[keep * BLK :, :] = label.astype(jnp.float32).astype(jnp.bfloat16)
    out_copy.wait()


def kept_blocks_of(kept, here, step_size, acts, cot, residual):
    tokens, cols = cot.shape
    rows = residual.shape[0]
    keep = kept.shape[0]
    return pl.pallas_call(
        functools.partial(kept_kernel, len(acts), cols // BLK),
        out_shape=[
            jax.ShapeDtypeStruct((rows, tokens), jnp.bfloat16),
            jax.ShapeDtypeStruct((keep * BLK + LABEL_ROWS, BLK), jnp.bfloat16),
        ],
        in_specs=[smem()] * 3 + [vmem() for _ in acts] + [anywhere(), anywhere()],
        out_specs=[anywhere(), vmem()],
        scratch_shapes=[
            pltpu.VMEM((rows, tokens), jnp.bfloat16),
            pltpu.VMEM((keep, tokens, BLK), jnp.bfloat16),
            pltpu.VMEM((keep, BLK, BLK), jnp.bfloat16),
            pltpu.SemaphoreType.DMA((keep,)),
            pltpu.SemaphoreType.DMA((keep,)),
            pltpu.SemaphoreType.DMA,
        ],
        compiler_params=params(50),
        cost_estimate=cost(2 * tokens * BLK * BLK * keep, 4 * tokens * rows + 2 * keep * tokens * BLK),
        name="kept_blocks",
    )(kept, here, step_size, *acts, cot, residual)


def finish_kernel(groups, keep, pair, col_blocks, me_ref, kept_ref, *refs):
    if pair:
        own_ref, arrived_ref, *refs = refs
    block_refs = refs[:groups]
    refs = refs[groups + 2 :]
    if pair:
        grad_ref, *refs = refs
    out_ref, res_ref, sum_ref, slot_ref, label_ref, number_ref, zero_ref, sem, number_sem, zero_sem, *refs = refs
    total = groups * keep
    me = me_ref[0]

    for g, block_ref in enumerate(block_refs):
        digits = block_ref[keep * BLK :, :].astype(jnp.float32).astype(jnp.int32)
        label_ref[g : g + 1, :] = digits[0:1, :] * RADIX + digits[1:2, :]
    numbers = pltpu.make_async_copy(label_ref, number_ref, number_sem)
    numbers.start()

    zero_ref[...] = jnp.zeros_like(zero_ref)
    zero_copies = []
    for k in range(keep):
        row = pl.multiple_of(kept_ref[k] // col_blocks * BLK, BLK)
        col = pl.multiple_of(kept_ref[k] % col_blocks * BLK, BLK)
        zero_copies.append(
            pltpu.make_async_copy(zero_ref, res_ref.at[pl.ds(row, BLK), pl.ds(col, BLK)], zero_sem.at[k])
        )
        zero_copies[k].start()
    numbers.wait()

    def place(i):
        return number_ref[i // keep, i % keep] // groups

    def mine(i):
        return number_ref[i // keep, i % keep] % groups == me

    def is_slot(i):
        return mine(i) & (slot_ref[place(i)] == i)

    def copy(i):
        return pltpu.make_async_copy(sum_ref.at[i], out_ref.at[place(i)], sem.at[i])

    for i in range(total):
        slot_ref[place(i)] = total
    for i in range(total):

        @pl.when(mine(i))
        def _(i=i):
            at = i % keep * BLK
            block = block_refs[i // keep][at : at + BLK, :].astype(jnp.float32)
            slot = slot_ref[place(i)]

            @pl.when(slot == total)
            def _():
                sum_ref[i] = block
                slot_ref[place(i)] = i

            @pl.when(slot < total)
            def _():
                sum_ref[slot] += block

    for i in range(total):

        @pl.when(is_slot(i))
        def _(i=i):
            copy(i).start()

    if pair:
        grad_buf, grad_sem = refs
        part = grad_buf.shape[0] // grad_sem.shape[0]
        grad_copies = []
        for c in range(grad_sem.shape[0]):
            at = slice(c * part, (c + 1) * part)
            grad_buf[at, :] = (own_ref[at, :] + arrived_ref[at, :].astype(jnp.float32)).astype(jnp.bfloat16)
            grad_copies.append(pltpu.make_async_copy(grad_buf.at[at, :], grad_ref.at[at, :], grad_sem.at[c]))
            grad_copies[c].start()
        for grad_copy in grad_copies:
            grad_copy.wait()
    for zero_copy in zero_copies:
        zero_copy.wait()
    for i in range(total):

        @pl.when(is_slot(i))
        def _(i=i):
            copy(i).wait()


def finish(me, kept, parts, blocks, zeros, residual):
    groups = len(blocks)
    keep = kept.shape[0]
    out_shape = [jax.ShapeDtypeStruct(a.shape, a.dtype) for a in (zeros, residual)]
    out_specs = [anywhere(), anywhere()]
    scratch = [
        pltpu.VMEM((groups * keep, BLK, BLK), jnp.float32),
        pltpu.SMEM((zeros.shape[0],), jnp.int32),
        pltpu.VMEM((8, BLK), jnp.int32),
        pltpu.SMEM((8, BLK), jnp.int32),
        pltpu.VMEM((BLK, BLK), jnp.bfloat16),
        pltpu.SemaphoreType.DMA((groups * keep,)),
        pltpu.SemaphoreType.DMA,
        pltpu.SemaphoreType.DMA((keep,)),
    ]
    if parts:
        out_shape.insert(0, jax.ShapeDtypeStruct(parts[0].shape, jnp.bfloat16))
        out_specs.insert(0, anywhere())
        scratch += [pltpu.VMEM(parts[0].shape, jnp.bfloat16), pltpu.SemaphoreType.DMA((4,))]
    first = 2 + len(parts) + groups
    return pl.pallas_call(
        functools.partial(finish_kernel, groups, keep, bool(parts), residual.shape[1] // BLK),
        out_shape=out_shape,
        in_specs=[smem(), smem()] + [vmem()] * (len(parts) + groups) + [anywhere(), anywhere()],
        out_specs=out_specs,
        scratch_shapes=scratch,
        input_output_aliases={first: len(out_shape) - 2, first + 1: len(out_shape) - 1},
        compiler_params=params(16),
        cost_estimate=cost(groups * keep * BLK * BLK, groups * keep * BLK * BLK * 8),
        name="finish",
    )(me, kept, *parts, *blocks, zeros, residual)


def swapped(x, axis, mask):
    return lax.ppermute(x, axis, [(i, i ^ mask) for i in range(lax.axis_size(axis))])


def of_all_groups(x):
    return [x] + [swapped(x, "dp", mask) for mask in range(1, lax.axis_size("dp"))]


def body(activations, cotangent, weight, residual, step_size, kept_blocks):
    rows, cols = weight.shape
    groups = lax.axis_size("dp")
    owned_count = (rows // BLK) * (cols // BLK) // groups
    kept = kept_blocks.reshape(-1)
    me = lax.axis_index("dp").astype(jnp.int32).reshape(1)
    here = lax.axis_index("tensor").astype(jnp.int32).reshape(1)
    pair = lax.axis_size("tensor") == 2
    if pair:
        acts = [activations, swapped(activations, "tensor", 1)]
        away, own, zeros = input_grad_partials(here, cotangent, weight, owned_count, True)
        parts = [own, swapped(away, "tensor", 1)]
    else:
        acts = [lax.all_gather(activations, "tensor", axis=0, tiled=True)]
        own, zeros = input_grad_partials(here, cotangent, weight, owned_count, False)
        summed = lax.psum_scatter(own, "tensor", scatter_dimension=0, tiled=True)
        parts = []
    acts_t, blocks = kept_blocks_of(kept, here, step_size, acts, cotangent, residual[0])
    all_blocks = of_all_groups(blocks)
    accumulated = residual[0].astype(jnp.float32) + step_size[0] * dot_nn(acts_t, cotangent)
    rounded = accumulated.astype(jnp.bfloat16)
    *grads, owned, residual_out = finish(me, kept, parts, all_blocks, zeros, rounded)
    input_grad = grads[0] if pair else summed.astype(jnp.bfloat16)
    return (input_grad, residual_out[None], owned.reshape(1, 1, 1, owned_count, BLK, BLK))


def solution(mesh):
    in_specs = (
        P(("dp", "tensor"), "fsdp"),
        P("dp", "tensor"),
        P("fsdp", "tensor"),
        P("dp", "fsdp", "tensor"),
        P(),
        P("dp", "fsdp", "tensor", None),
    )
    out_specs = (
        P(("dp", "tensor"), "fsdp"),
        P("dp", "fsdp", "tensor"),
        P("dp", "fsdp", "tensor", None, None, None),
    )
    return jax.shard_map(body, mesh=mesh, in_specs=in_specs, out_specs=out_specs, check_vma=False)
```

```python
import functools

import jax
import jax.numpy as jnp
from jax import lax
from jax.experimental import pallas as pl
from jax.experimental.pallas import tpu as pltpu
from jax.sharding import PartitionSpec as P

BLK = 128
MIB = 1024 * 1024
LABEL_ROWS = 16
RADIX = 16


def cost(flops, nbytes):
    return pl.CostEstimate(flops=flops, bytes_accessed=nbytes, transcendentals=0)


def params(mib):
    return pltpu.CompilerParams(vmem_limit_bytes=mib * MIB)


def dot_nt(a, b):
    return lax.dot_general(a, b, (((1,), (1,)), ((), ())), preferred_element_type=jnp.float32)


def dot_nn(a, b):
    return lax.dot_general(a, b, (((1,), (0,)), ((), ())), preferred_element_type=jnp.float32)


def hidden_chunks(cols):
    sizes = []
    for size in (512, 1536, 2048, 4096):
        if cols > sum(sizes):
            sizes.append(min(size, cols - sum(sizes)))
    while sum(sizes) < cols:
        sizes.append(min(4096, cols - sum(sizes)))
    return sizes


def smem():
    return pl.BlockSpec(memory_space=pltpu.SMEM)


def vmem():
    return pl.BlockSpec(memory_space=pltpu.VMEM)


def anywhere():
    return pl.BlockSpec(memory_space=pl.ANY)


def input_grad_kernel(split, sizes, zero_copies, here_ref, kept_ref, cot_ref, w_ref, res_ref, *refs):
    if split:
        acts_ref, away_ref, acts_t_ref, *refs = refs
    own_ref, owned_ref, kept_cot_ref, kept_res_ref, *refs = refs
    acc_ref, cot_buf, w_buf, zero_ref, cot_sem, w_sem, zero_sem, own_sem, kept_cot_sem, kept_res_sem, *refs = refs
    keep = kept_cot_ref.shape[0]
    col_blocks = w_ref.shape[1] // BLK
    zero_rows = zero_ref.shape[0]
    rows = w_ref.shape[0]
    width = min(256, rows)
    starts = [sum(sizes[:i]) for i in range(len(sizes))]

    def loads(i):
        part = slice(starts[i], starts[i] + sizes[i])
        return (
            pltpu.make_async_copy(cot_ref.at[:, part], cot_buf.at[:, part], cot_sem.at[i]),
            pltpu.make_async_copy(w_ref.at[:, part], w_buf.at[:, part], w_sem.at[i]),
        )

    def start(i):
        if i < len(sizes):
            for copy in loads(i):
                copy.start()

    def zero_copy(i):
        return pltpu.make_async_copy(zero_ref, owned_ref.at[pl.ds(i * zero_rows, zero_rows)], zero_sem.at[i])

    def kept_copies(k):
        row = pl.multiple_of(kept_ref[k] // col_blocks * BLK, BLK)
        col = pl.multiple_of(kept_ref[k] % col_blocks * BLK, BLK)
        return (
            pltpu.make_async_copy(cot_buf.at[:, pl.ds(col, BLK)], kept_cot_ref.at[k], kept_cot_sem.at[k]),
            pltpu.make_async_copy(res_ref.at[pl.ds(row, BLK), pl.ds(col, BLK)], kept_res_ref.at[k], kept_res_sem.at[k]),
        )

    if split:
        acts_buf, acts_sem = refs
        acts_copy = pltpu.make_async_copy(acts_ref, acts_buf, acts_sem)
        acts_copy.start()
    start(0)
    start(1)
    if split:
        acts_copy.wait()
        acts_t_ref[...] = acts_buf[...].T
    zero_ref[...] = jnp.zeros_like(zero_ref)
    for i in range(len(sizes)):
        for copy in loads(i):
            copy.wait()
        start(i + 2)
        if i == len(sizes) - 1:
            for z in range(zero_copies):
                zero_copy(z).start()
            for k in range(keep):
                for copy in kept_copies(k):
                    copy.start()
        part = slice(starts[i], starts[i] + sizes[i])
        for at in range(0, rows, width):
            term = dot_nt(cot_buf[:, part], w_buf[at : at + width, part])
            if i == 0:
                acc_ref[:, at : at + width] = term
            else:
                acc_ref[:, at : at + width] += term
    if split:
        half = own_ref.shape[0]
        mine = pl.multiple_of(here_ref[0] * half, half)
        others = pl.multiple_of((1 - here_ref[0]) * half, half)
        own_copy = pltpu.make_async_copy(acc_ref.at[pl.ds(mine, half), :], own_ref, own_sem)
        own_copy.start()
        away_ref[...] = acc_ref[pl.ds(others, half), :].astype(jnp.bfloat16)
    else:
        own_copy = pltpu.make_async_copy(acc_ref, own_ref, own_sem)
        own_copy.start()
    own_copy.wait()
    for z in range(zero_copies):
        zero_copy(z).wait()
    for k in range(keep):
        for copy in kept_copies(k):
            copy.wait()


def input_grad_partials(here, kept, cot, weight, residual, owned_count, acts):
    split = acts is not None
    keep = kept.shape[0]
    tokens, cols = cot.shape
    rows = weight.shape[0]
    sizes = hidden_chunks(cols)
    own_rows = tokens // 2 if split else tokens
    zero_rows = min(16, owned_count)
    zero_copies = owned_count // zero_rows
    out_shape = [
        jax.ShapeDtypeStruct((own_rows, rows), jnp.float32),
        jax.ShapeDtypeStruct((owned_count, BLK, BLK), jnp.float32),
        jax.ShapeDtypeStruct((keep, tokens, BLK), jnp.bfloat16),
        jax.ShapeDtypeStruct((keep, BLK, BLK), jnp.bfloat16),
    ]
    out_specs = [anywhere(), anywhere(), vmem(), vmem()]
    if split:
        out_shape.insert(0, jax.ShapeDtypeStruct((own_rows, rows), jnp.bfloat16))
        out_shape.insert(1, jax.ShapeDtypeStruct((rows, own_rows), jnp.bfloat16))
        out_specs = [vmem(), vmem()] + out_specs
    return pl.pallas_call(
        functools.partial(input_grad_kernel, split, sizes, zero_copies),
        out_shape=out_shape,
        in_specs=[smem(), smem()] + [anywhere()] * (3 + split),
        out_specs=out_specs,
        scratch_shapes=[
            pltpu.VMEM((tokens, rows), jnp.float32),
            pltpu.VMEM((tokens, cols), jnp.bfloat16),
            pltpu.VMEM((rows, cols), jnp.bfloat16),
            pltpu.VMEM((zero_rows, BLK, BLK), jnp.float32),
            pltpu.SemaphoreType.DMA((len(sizes),)),
            pltpu.SemaphoreType.DMA((len(sizes),)),
            pltpu.SemaphoreType.DMA((zero_copies,)),
            pltpu.SemaphoreType.DMA,
            pltpu.SemaphoreType.DMA((keep,)),
            pltpu.SemaphoreType.DMA((keep,)),
        ]
        + ([pltpu.VMEM(acts.shape, jnp.bfloat16), pltpu.SemaphoreType.DMA] if split else []),
        compiler_params=params(43),
        cost_estimate=cost(2 * tokens * rows * cols, 2 * cols * (tokens + rows) + 4 * owned_count * BLK * BLK),
        name="input_grad_partials",
    )(here, kept, cot, weight, residual, *([acts] if split else []))


def kept_kernel(pair, col_blocks, here_ref, kept_ref, step_ref, *refs):
    if pair:
        own_t_ref, *refs = refs
    act_ref, cot_ref, res_ref, act_t_out, out_ref, act_t_ref, sem = refs
    keep = cot_ref.shape[0]
    size = act_ref.shape[0]
    rows = [pl.ds(pl.multiple_of(kept_ref[k] // col_blocks * BLK, BLK), BLK) for k in range(keep)]
    own_at = pl.ds(pl.multiple_of(here_ref[0] * size, size), size)
    act_at = pl.ds(pl.multiple_of((1 - here_ref[0]) * size, size), size) if pair else slice(None)

    act_t_ref[...] = act_ref[...].T
    copy = pltpu.make_async_copy(act_t_ref, act_t_out, sem)
    copy.start()
    for k in range(keep):
        gradient = dot_nn(act_t_ref[rows[k], :], cot_ref[k, act_at, :])
        if pair:
            gradient += dot_nn(own_t_ref[rows[k], :], cot_ref[k, own_at, :])
        out_ref[k * BLK : (k + 1) * BLK, :] = (res_ref[k].astype(jnp.float32) + step_ref[0] * gradient).astype(
            jnp.bfloat16
        )
    lane = lax.broadcasted_iota(jnp.int32, (LABEL_ROWS, BLK), 1) % keep
    low = lax.broadcasted_iota(jnp.int32, (LABEL_ROWS, BLK), 0) % 2 == 1
    label = jnp.zeros((LABEL_ROWS, BLK), jnp.int32)
    for k in range(keep):
        digit = jnp.where(low, kept_ref[k] % RADIX, kept_ref[k] // RADIX)
        label = jnp.where(lane == k, digit, label)
    out_ref[keep * BLK :, :] = label.astype(jnp.float32).astype(jnp.bfloat16)
    copy.wait()


def kept_blocks_of(here, kept, step_size, own_t, act, kept_cot, kept_res, col_blocks):
    size, rows = act.shape
    keep, tokens = kept_cot.shape[:2]
    pair = own_t is not None
    return pl.pallas_call(
        functools.partial(kept_kernel, pair, col_blocks),
        out_shape=[
            jax.ShapeDtypeStruct((rows, size), jnp.bfloat16),
            jax.ShapeDtypeStruct((keep * BLK + LABEL_ROWS, BLK), jnp.bfloat16),
        ],
        in_specs=[smem()] * 3 + [vmem()] * (3 + pair),
        out_specs=[anywhere(), vmem()],
        scratch_shapes=[pltpu.VMEM((rows, size), jnp.bfloat16), pltpu.SemaphoreType.DMA],
        compiler_params=params(16),
        cost_estimate=cost(2 * tokens * BLK * BLK * keep, 4 * size * rows + 2 * keep * tokens * BLK),
        name="kept_blocks",
    )(here, kept, step_size, *([own_t] if pair else []), act, kept_cot, kept_res)


def column_chunks(cols):
    if cols < 2048:
        return [min(256, cols)] * max(1, cols // 256)
    return [256, 256] + [512] * (cols // 512 - 2) + [256, 256]


def residual_kernel(pieces, sizes, here_ref, step_ref, *refs):
    act_t_refs = refs[:pieces]
    cot_ref, res_ref, out_ref, acts_t_ref, cot_buf, res_buf, acc_ref, act_sem, cot_sem, res_sem, out_sem = refs[pieces:]
    step = step_ref[0]
    chunks = len(sizes)
    parts = [slice(sum(sizes[:i]), sum(sizes[: i + 1])) for i in range(chunks)]

    def loads(i):
        return (
            pltpu.make_async_copy(cot_ref.at[:, parts[i]], cot_buf.at[:, parts[i]], cot_sem.at[i]),
            pltpu.make_async_copy(res_ref.at[:, parts[i]], res_buf.at[:, parts[i]], res_sem.at[i]),
        )

    def start(i):
        if i < chunks:
            for copy in loads(i):
                copy.start()

    def store(i):
        return pltpu.make_async_copy(res_buf.at[:, parts[i]], out_ref.at[:, parts[i]], out_sem.at[i])

    def finish_chunk(i):
        part = parts[i]
        gradient = acc_ref[i % 2, :, : sizes[i]]
        res_buf[:, part] = (res_buf[:, part].astype(jnp.float32) + step * gradient).astype(jnp.bfloat16)
        store(i).start()

    act_copies = []
    for p, act_t_ref in enumerate(act_t_refs):
        size = act_t_ref.shape[1]
        at = here_ref[0] if p == 0 else 1 - here_ref[0]
        at = pl.ds(pl.multiple_of(at * size, size), size) if pieces > 1 else slice(None)
        act_copies.append(pltpu.make_async_copy(act_t_ref, acts_t_ref.at[:, at], act_sem.at[p]))
        act_copies[p].start()
    for i in range(3):
        start(i)
    for copy in act_copies:
        copy.wait()
    for i in range(chunks):
        for copy in loads(i):
            copy.wait()
        start(i + 3)
        acc_ref[i % 2, :, : sizes[i]] = dot_nn(acts_t_ref[...], cot_buf[:, parts[i]])
        if i > 0:
            finish_chunk(i - 1)
    finish_chunk(chunks - 1)
    for i in range(chunks):
        store(i).wait()


def residual_of(here, step_size, acts_t, cot, residual):
    tokens, cols = cot.shape
    rows = residual.shape[0]
    sizes = column_chunks(cols)
    sem = pltpu.SemaphoreType.DMA((len(sizes),))
    return pl.pallas_call(
        functools.partial(residual_kernel, len(acts_t), sizes),
        out_shape=jax.ShapeDtypeStruct((rows, cols), jnp.bfloat16),
        in_specs=[smem()] * 2 + [anywhere()] * (len(acts_t) + 2),
        out_specs=anywhere(),
        scratch_shapes=[
            pltpu.VMEM((rows, tokens), jnp.bfloat16),
            pltpu.VMEM((tokens, cols), jnp.bfloat16),
            pltpu.VMEM((rows, cols), jnp.bfloat16),
            pltpu.VMEM((2, rows, max(sizes)), jnp.float32),
            pltpu.SemaphoreType.DMA((len(acts_t),)),
            sem,
            sem,
            sem,
        ],
        compiler_params=params(50),
        cost_estimate=cost(2 * tokens * rows * cols, 2 * tokens * (rows + cols) + 4 * rows * cols),
        name="residual_out",
    )(here, step_size, *acts_t, cot, residual)


def finish_kernel(groups, keep, pair, col_blocks, me_ref, kept_ref, *refs):
    if pair:
        own_ref, arrived_ref, *refs = refs
    block_refs = refs[:groups]
    refs = refs[groups + 2 :]
    if pair:
        grad_ref, *refs = refs
    out_ref, res_ref, sum_ref, table_ref, scalar_ref, zero_ref, sem, table_sem, zero_sem, *refs = refs
    total = groups * keep
    me = me_ref[0]

    row = lax.broadcasted_iota(jnp.int32, (total, BLK), 0)
    lane = lax.broadcasted_iota(jnp.int32, (total, BLK), 1)
    numbers = jnp.full((total, BLK), -1, jnp.int32)
    for g, block_ref in enumerate(block_refs):
        digits = block_ref[keep * BLK :, :].astype(jnp.float32).astype(jnp.int32)
        numbers = jnp.where(lane // keep == g, digits[0:1, :] * RADIX + digits[1:2, :], numbers)
    numbers = numbers.astype(jnp.float32)
    number = jnp.sum(jnp.where(lane == row, numbers, 0.0), axis=1, keepdims=True)
    first = jnp.min(jnp.where(numbers == number, lane.astype(jnp.float32), float(BLK)), axis=1, keepdims=True)
    number = jnp.broadcast_to(number, (total, BLK)).astype(jnp.int32)
    first = jnp.broadcast_to(first, (total, BLK)).astype(jnp.int32)
    table_ref[...] = jnp.where(lane == 0, jnp.where(number % groups == me, first, -1), number // groups)
    table = pltpu.make_async_copy(table_ref, scalar_ref, table_sem)
    table.start()

    zero_ref[...] = jnp.zeros_like(zero_ref)
    zero_copies = []
    for k in range(keep):
        at = pl.multiple_of(kept_ref[k] // col_blocks * BLK, BLK)
        col = pl.multiple_of(kept_ref[k] % col_blocks * BLK, BLK)
        zero_copies.append(
            pltpu.make_async_copy(zero_ref, res_ref.at[pl.ds(at, BLK), pl.ds(col, BLK)], zero_sem.at[k])
        )
        zero_copies[k].start()
    grad_copies = []
    if pair:
        grad_buf, grad_sem = refs
        part = grad_buf.shape[0] // grad_sem.shape[0]
        for c in range(grad_sem.shape[0]):
            at = slice(c * part, (c + 1) * part)
            grad_buf[at, :] = (own_ref[at, :] + arrived_ref[at, :].astype(jnp.float32)).astype(jnp.bfloat16)
            grad_copies.append(pltpu.make_async_copy(grad_buf.at[at, :], grad_ref.at[at, :], grad_sem.at[c]))
            grad_copies[c].start()

    table.wait()

    def copy(i):
        return pltpu.make_async_copy(sum_ref.at[i], out_ref.at[scalar_ref[i, 1]], sem.at[i])

    def block(i):
        at = i % keep * BLK
        return block_refs[i // keep][at : at + BLK, :].astype(jnp.float32)

    for i in range(total):
        slot = scalar_ref[i, 0]

        @pl.when(slot == i)
        def _(i=i):
            sum_ref[i] = block(i)

        if i >= keep:

            @pl.when((slot >= 0) & (slot < i))
            def _(i=i, slot=slot):
                sum_ref[slot] += block(i)

    for i in range(total):

        @pl.when(scalar_ref[i, 0] == i)
        def _(i=i):
            copy(i).start()

    for done in zero_copies + grad_copies:
        done.wait()
    for i in range(total):

        @pl.when(scalar_ref[i, 0] == i)
        def _(i=i):
            copy(i).wait()


def finish(me, kept, parts, blocks, zeros, residual):
    groups = len(blocks)
    keep = kept.shape[0]
    out_shape = [jax.ShapeDtypeStruct(a.shape, a.dtype) for a in (zeros, residual)]
    out_specs = [anywhere(), anywhere()]
    scratch = [
        pltpu.VMEM((groups * keep, BLK, BLK), jnp.float32),
        pltpu.VMEM((groups * keep, BLK), jnp.int32),
        pltpu.SMEM((groups * keep, BLK), jnp.int32),
        pltpu.VMEM((BLK, BLK), jnp.bfloat16),
        pltpu.SemaphoreType.DMA((groups * keep,)),
        pltpu.SemaphoreType.DMA,
        pltpu.SemaphoreType.DMA((keep,)),
    ]
    if parts:
        out_shape.insert(0, jax.ShapeDtypeStruct(parts[0].shape, jnp.bfloat16))
        out_specs.insert(0, anywhere())
        scratch += [pltpu.VMEM(parts[0].shape, jnp.bfloat16), pltpu.SemaphoreType.DMA((4,))]
    first = 2 + len(parts) + groups
    return pl.pallas_call(
        functools.partial(finish_kernel, groups, keep, bool(parts), residual.shape[1] // BLK),
        out_shape=out_shape,
        in_specs=[smem(), smem()] + [vmem()] * (len(parts) + groups) + [anywhere(), anywhere()],
        out_specs=out_specs,
        scratch_shapes=scratch,
        input_output_aliases={first: len(out_shape) - 2, first + 1: len(out_shape) - 1},
        compiler_params=params(16),
        cost_estimate=cost(groups * keep * BLK * BLK, groups * keep * BLK * BLK * 8),
        name="finish",
    )(me, kept, *parts, *blocks, zeros, residual)


def swapped(x, axis, mask):
    return lax.ppermute(x, axis, [(i, i ^ mask) for i in range(lax.axis_size(axis))])


def of_all_groups(x):
    return [x] + [swapped(x, "dp", mask) for mask in range(1, lax.axis_size("dp"))]


def body(activations, cotangent, weight, residual, step_size, kept_blocks):
    rows, cols = weight.shape
    groups = lax.axis_size("dp")
    owned_count = (rows // BLK) * (cols // BLK) // groups
    kept = kept_blocks.reshape(-1)
    me = lax.axis_index("dp").astype(jnp.int32).reshape(1)
    here = lax.axis_index("tensor").astype(jnp.int32).reshape(1)
    pair = lax.axis_size("tensor") == 2
    if pair:
        act = swapped(activations, "tensor", 1)
        away, own_t, own, zeros, kept_cot, kept_res = input_grad_partials(
            here, kept, cotangent, weight, residual[0], owned_count, activations
        )
        parts = [own, swapped(away, "tensor", 1)]
    else:
        act = lax.all_gather(activations, "tensor", axis=0, tiled=True)
        own_t = None
        own, zeros, kept_cot, kept_res = input_grad_partials(
            here, kept, cotangent, weight, residual[0], owned_count, None
        )
        summed = lax.psum_scatter(own, "tensor", scatter_dimension=0, tiled=True)
        parts = []
    act_t, blocks = kept_blocks_of(here, kept, step_size, own_t, act, kept_cot, kept_res, cols // BLK)
    all_blocks = of_all_groups(blocks)
    acts_t = [own_t, act_t] if pair else [act_t]
    rounded = residual_of(here, step_size, acts_t, cotangent, residual[0])
    *grads, owned, residual_out = finish(me, kept, parts, all_blocks, zeros, rounded)
    input_grad = grads[0] if pair else summed.astype(jnp.bfloat16)
    return (input_grad, residual_out[None], owned.reshape(1, 1, 1, owned_count, BLK, BLK))


def solution(mesh):
    in_specs = (
        P(("dp", "tensor"), "fsdp"),
        P("dp", "tensor"),
        P("fsdp", "tensor"),
        P("dp", "fsdp", "tensor"),
        P(),
        P("dp", "fsdp", "tensor", None),
    )
    out_specs = (
        P(("dp", "tensor"), "fsdp"),
        P("dp", "fsdp", "tensor"),
        P("dp", "fsdp", "tensor", None, None, None),
    )
    return jax.shard_map(body, mesh=mesh, in_specs=in_specs, out_specs=out_specs, check_vma=False)
```

```python
import functools

import jax
import jax.numpy as jnp
from jax import lax
from jax.experimental import pallas as pl
from jax.experimental.pallas import tpu as pltpu
from jax.sharding import PartitionSpec as P

BLK = 128
MIB = 1024 * 1024
LABEL_ROWS = 16
RADIX = 16


def cost(flops, nbytes):
    return pl.CostEstimate(flops=flops, bytes_accessed=nbytes, transcendentals=0)


def params(mib=62):
    return pltpu.CompilerParams(vmem_limit_bytes=mib * MIB)


def dot_nt(a, b):
    return lax.dot_general(a, b, (((1,), (1,)), ((), ())), preferred_element_type=jnp.float32)


def dot_nn(a, b):
    return lax.dot_general(a, b, (((1,), (0,)), ((), ())), preferred_element_type=jnp.float32)


def hidden_chunks(cols):
    sizes = []
    for size in (512, 1536, 2048, 4096):
        if cols > sum(sizes):
            sizes.append(min(size, cols - sum(sizes)))
    while sum(sizes) < cols:
        sizes.append(min(4096, cols - sum(sizes)))
    return sizes


def smem():
    return pl.BlockSpec(memory_space=pltpu.SMEM)


def vmem():
    return pl.BlockSpec(memory_space=pltpu.VMEM)


def anywhere():
    return pl.BlockSpec(memory_space=pl.ANY)


def input_grad_kernel(split, sizes, zero_copies, here_ref, cot_ref, w_ref, *refs):
    if split:
        acts_ref, away_ref, acts_t_ref, *refs = refs
    own_ref, owned_ref, acc_ref, cot_buf, w_buf, zero_ref, cot_sem, w_sem, zero_sem, own_sem, *refs = refs
    zero_rows = zero_ref.shape[0]
    rows = w_ref.shape[0]
    width = min(256, rows)
    last = len(sizes) - 1

    def loads(i):
        part = slice(sum(sizes[:i]), sum(sizes[: i + 1]))
        return (
            pltpu.make_async_copy(cot_ref.at[:, part], cot_buf.at[:, part], cot_sem.at[i]),
            pltpu.make_async_copy(w_ref.at[:, part], w_buf.at[:, part], w_sem.at[i]),
        )

    def start(i):
        if i <= last:
            for copy in loads(i):
                copy.start()

    def zero_copy(i):
        return pltpu.make_async_copy(zero_ref, owned_ref.at[pl.ds(i * zero_rows, zero_rows)], zero_sem.at[i])

    if split:
        acts_buf, acts_t_buf, away_buf, acts_sem, acts_t_sem, away_sem = refs
        half = own_ref.shape[0]
        mine = pl.ds(pl.multiple_of(here_ref[0] * half, half), half)
        others = pl.ds(pl.multiple_of((1 - here_ref[0]) * half, half), half)
        acts_copy = pltpu.make_async_copy(acts_ref, acts_buf, acts_sem)
        acts_t_copy = pltpu.make_async_copy(acts_t_buf, acts_t_ref, acts_t_sem)
        acts_copy.start()
    else:
        mine = slice(None)
    start(0)
    if split:
        acts_copy.wait()
        acts_t_buf[...] = acts_buf[...].T
        acts_t_copy.start()
    start(1)
    zero_ref[...] = jnp.zeros_like(zero_ref)
    outputs = []
    for i in range(last + 1):
        for copy in loads(i):
            copy.wait()
        start(i + 2)
        if i == last:
            for z in range(zero_copies):
                zero_copy(z).start()
        part = slice(sum(sizes[:i]), sum(sizes[: i + 1]))
        for n, at in enumerate(range(0, rows, width)):
            cols = slice(at, at + width)
            term = dot_nt(cot_buf[:, part], w_buf[cols, part])
            if i == 0:
                acc_ref[:, cols] = term
            else:
                acc_ref[:, cols] += term
            if i == last:
                if split:
                    away_buf[:, cols] = acc_ref[others, cols].astype(jnp.bfloat16)
                    outputs.append(pltpu.make_async_copy(away_buf.at[:, cols], away_ref.at[:, cols], away_sem.at[n]))
                    outputs[-1].start()
                outputs.append(pltpu.make_async_copy(acc_ref.at[mine, cols], own_ref.at[:, cols], own_sem.at[n]))
                outputs[-1].start()
    if split:
        acts_t_copy.wait()
    for z in range(zero_copies):
        zero_copy(z).wait()
    for copy in outputs:
        copy.wait()


def input_grad_partials(here, cot, weight, owned_count, acts):
    split = acts is not None
    tokens, cols = cot.shape
    rows = weight.shape[0]
    sizes = hidden_chunks(cols)
    own_rows = tokens // 2 if split else tokens
    zero_rows = min(16, owned_count)
    zero_copies = owned_count // zero_rows
    out_shape = [
        jax.ShapeDtypeStruct((own_rows, rows), jnp.float32),
        jax.ShapeDtypeStruct((owned_count, BLK, BLK), jnp.float32),
    ]
    scratch = [
        pltpu.VMEM((tokens, rows), jnp.float32),
        pltpu.VMEM((tokens, cols), jnp.bfloat16),
        pltpu.VMEM((rows, cols), jnp.bfloat16),
        pltpu.VMEM((zero_rows, BLK, BLK), jnp.float32),
        pltpu.SemaphoreType.DMA((len(sizes),)),
        pltpu.SemaphoreType.DMA((len(sizes),)),
        pltpu.SemaphoreType.DMA((zero_copies,)),
        pltpu.SemaphoreType.DMA((4,)),
    ]
    if split:
        out_shape = [
            jax.ShapeDtypeStruct((own_rows, rows), jnp.bfloat16),
            jax.ShapeDtypeStruct((rows, own_rows), jnp.bfloat16),
        ] + out_shape
        scratch += [
            pltpu.VMEM(acts.shape, jnp.bfloat16),
            pltpu.VMEM((rows, own_rows), jnp.bfloat16),
            pltpu.VMEM((own_rows, rows), jnp.bfloat16),
            pltpu.SemaphoreType.DMA,
            pltpu.SemaphoreType.DMA,
            pltpu.SemaphoreType.DMA((4,)),
        ]
    return pl.pallas_call(
        functools.partial(input_grad_kernel, split, sizes, zero_copies),
        out_shape=out_shape,
        in_specs=[smem()] + [anywhere()] * (2 + split),
        out_specs=[anywhere()] * len(out_shape),
        scratch_shapes=scratch,
        compiler_params=params(),
        cost_estimate=cost(2 * tokens * rows * cols, 2 * cols * (tokens + rows) + 4 * owned_count * BLK * BLK),
        name="input_grad_partials",
    )(here, cot, weight, *([acts] if split else []))


def kept_kernel(pair, here_ref, kept_ref, step_ref, *refs):
    if pair:
        own_t_ref, *refs = refs
    act_ref, cot_ref, res_ref, act_t_out, out_ref, act_buf, act_t_ref, cot_buf, res_buf, *refs = refs
    act_sem, act_t_sem, cot_sem, res_sem, *refs = refs
    keep = cot_buf.shape[0]
    size = act_ref.shape[0]
    col_blocks = cot_ref.shape[1] // BLK
    rows = [pl.ds(pl.multiple_of(kept_ref[k] // col_blocks * BLK, BLK), BLK) for k in range(keep)]
    cols = [pl.ds(pl.multiple_of(kept_ref[k] % col_blocks * BLK, BLK), BLK) for k in range(keep)]

    act_copy = pltpu.make_async_copy(act_ref, act_buf, act_sem)
    act_copy.start()
    copies = []
    for k in range(keep):
        copies.append(pltpu.make_async_copy(cot_ref.at[:, cols[k]], cot_buf.at[k], cot_sem.at[k]))
        copies.append(pltpu.make_async_copy(res_ref.at[rows[k], cols[k]], res_buf.at[k], res_sem.at[k]))
    if pair:
        own_t_buf, own_t_sem = refs
        own_at = pl.ds(pl.multiple_of(here_ref[0] * size, size), size)
        act_at = pl.ds(pl.multiple_of((1 - here_ref[0]) * size, size), size)
        copies.append(pltpu.make_async_copy(own_t_ref, own_t_buf, own_t_sem))
    else:
        act_at = slice(None)
    for copy in copies:
        copy.start()
    lane = lax.broadcasted_iota(jnp.int32, (LABEL_ROWS, BLK), 1) % keep
    low = lax.broadcasted_iota(jnp.int32, (LABEL_ROWS, BLK), 0) % 2 == 1
    label = jnp.zeros((LABEL_ROWS, BLK), jnp.int32)
    for k in range(keep):
        digit = jnp.where(low, kept_ref[k] % RADIX, kept_ref[k] // RADIX)
        label = jnp.where(lane == k, digit, label)
    out_ref[keep * BLK :, :] = label.astype(jnp.float32).astype(jnp.bfloat16)
    act_copy.wait()
    act_t_ref[...] = act_buf[...].T
    act_t_copy = pltpu.make_async_copy(act_t_ref, act_t_out, act_t_sem)
    act_t_copy.start()
    for copy in copies:
        copy.wait()
    for k in range(keep):
        gradient = dot_nn(act_t_ref[rows[k], :], cot_buf[k, act_at, :])
        if pair:
            gradient += dot_nn(own_t_buf[rows[k], :], cot_buf[k, own_at, :])
        out_ref[k * BLK : (k + 1) * BLK, :] = (res_buf[k].astype(jnp.float32) + step_ref[0] * gradient).astype(
            jnp.bfloat16
        )
    act_t_copy.wait()


def kept_blocks_of(here, kept, step_size, own_t, act, cot, residual):
    size, rows = act.shape
    tokens = cot.shape[0]
    keep = kept.shape[0]
    pair = own_t is not None
    scratch = [
        pltpu.VMEM((size, rows), jnp.bfloat16),
        pltpu.VMEM((rows, size), jnp.bfloat16),
        pltpu.VMEM((keep, tokens, BLK), jnp.bfloat16),
        pltpu.VMEM((keep, BLK, BLK), jnp.bfloat16),
        pltpu.SemaphoreType.DMA,
        pltpu.SemaphoreType.DMA,
        pltpu.SemaphoreType.DMA((keep,)),
        pltpu.SemaphoreType.DMA((keep,)),
    ]
    if pair:
        scratch += [pltpu.VMEM((rows, size), jnp.bfloat16), pltpu.SemaphoreType.DMA]
    return pl.pallas_call(
        functools.partial(kept_kernel, pair),
        out_shape=[
            jax.ShapeDtypeStruct((rows, size), jnp.bfloat16),
            jax.ShapeDtypeStruct((keep * BLK + LABEL_ROWS, BLK), jnp.bfloat16),
        ],
        in_specs=[smem()] * 3 + [anywhere()] * (3 + pair),
        out_specs=[anywhere(), vmem()],
        scratch_shapes=scratch,
        compiler_params=params(),
        cost_estimate=cost(2 * tokens * BLK * BLK * keep, 4 * size * rows + 2 * keep * tokens * BLK),
        name="kept_blocks",
    )(here, kept, step_size, *([own_t] if pair else []), act, cot, residual)


def residual_kernel(pieces, here_ref, step_ref, *refs):
    act_t_refs = refs[:pieces]
    cot_ref, res_ref, out_ref, acts_t_ref, cot_buf, res_buf, acc_ref, act_sem, cot_sem, res_sem, out_sem = refs[pieces:]
    step = step_ref[0]
    chunks, _, chunk = cot_buf.shape

    def columns(j):
        return pl.ds(pl.multiple_of(j * chunk, chunk), chunk)

    def cot_copy(j):
        return pltpu.make_async_copy(cot_ref.at[:, columns(j)], cot_buf.at[j], cot_sem.at[j])

    def res_copy(j):
        return pltpu.make_async_copy(res_ref.at[:, columns(j)], res_buf.at[j], res_sem.at[j])

    def out_copy(j):
        return pltpu.make_async_copy(res_buf.at[j], out_ref.at[:, columns(j)], out_sem.at[j])

    def start_for(j):
        @pl.when(j < chunks)
        def _():
            cot_copy(j).start()

        @pl.when(j <= chunks)
        def _():
            res_copy(j - 1).start()

    def rounding(j, slot):
        res_buf[j] = (res_buf[j].astype(jnp.float32) + step * acc_ref[slot]).astype(jnp.bfloat16)

    act_copies = []
    for p, act_t_ref in enumerate(act_t_refs):
        size = act_t_ref.shape[1]
        at = here_ref[0] if p == 0 else 1 - here_ref[0]
        at = pl.ds(pl.multiple_of(at * size, size), size) if pieces > 1 else slice(None)
        act_copies.append(pltpu.make_async_copy(act_t_ref, acts_t_ref.at[:, at], act_sem.at[p]))
        act_copies[p].start()
    cot_copy(0).start()
    start_for(1)
    for copy in act_copies:
        copy.wait()
    cot_copy(0).wait()
    start_for(2)

    @pl.loop(0, chunks // 2)
    def _(pair):
        j = 2 * pair
        before = jnp.where(j > 0, j - 1, chunks)

        @pl.when(j > 0)
        def _():
            cot_copy(j).wait()
            res_copy(j - 1).wait()

        start_for(j + 3)
        acc_ref[0] = dot_nn(acts_t_ref[...], cot_buf[j])
        rounding(before, 1)

        @pl.when(j > 0)
        def _():
            out_copy(j - 1).start()

        cot_copy(j + 1).wait()
        res_copy(j).wait()
        start_for(j + 4)
        acc_ref[1] = dot_nn(acts_t_ref[...], cot_buf[j + 1])
        rounding(j, 0)
        out_copy(j).start()

    res_copy(chunks - 1).wait()
    rounding(chunks - 1, 1)
    out_copy(chunks - 1).start()
    for j in range(chunks):
        out_copy(j).wait()


def residual_of(here, step_size, acts_t, cot, residual):
    tokens, cols = cot.shape
    rows = residual.shape[0]
    chunk = min(512, cols // 2)
    chunks = cols // chunk
    sem = pltpu.SemaphoreType.DMA((chunks,))
    return pl.pallas_call(
        functools.partial(residual_kernel, len(acts_t)),
        out_shape=jax.ShapeDtypeStruct((rows, cols), jnp.bfloat16),
        in_specs=[smem()] * 2 + [anywhere()] * (len(acts_t) + 2),
        out_specs=anywhere(),
        scratch_shapes=[
            pltpu.VMEM((rows, tokens), jnp.bfloat16),
            pltpu.VMEM((chunks, tokens, chunk), jnp.bfloat16),
            pltpu.VMEM((chunks + 1, rows, chunk), jnp.bfloat16),
            pltpu.VMEM((2, rows, chunk), jnp.float32),
            pltpu.SemaphoreType.DMA((len(acts_t),)),
            sem,
            sem,
            sem,
        ],
        compiler_params=params(),
        cost_estimate=cost(2 * tokens * rows * cols, 2 * tokens * (rows + cols) + 4 * rows * cols),
        name="residual_out",
    )(here, step_size, *acts_t, cot, residual)


def finish_kernel(groups, keep, pair, col_blocks, me_ref, kept_ref, *refs):
    if pair:
        own_ref, arrived_ref, *refs = refs
    block_refs = refs[:groups]
    refs = refs[groups + 2 :]
    if pair:
        grad_ref, *refs = refs
    out_ref, res_ref, block_buf, sum_ref, table_ref, scalar_ref, zero_ref, *refs = refs
    block_sem, sem, table_sem, zero_sem, *refs = refs
    total = groups * keep
    me = me_ref[0]

    block_copies = []
    for g, block_ref in enumerate(block_refs):
        block_copies.append(pltpu.make_async_copy(block_ref, block_buf.at[g], block_sem.at[g]))
        block_copies[g].start()
    if pair:
        own_buf, arrived_buf, grad_buf, own_sem, arrived_sem, grad_sem = refs
        size = grad_buf.shape[0] // grad_sem.shape[0]
        parts = [slice(c * size, (c + 1) * size) for c in range(grad_sem.shape[0])]
        part_copies = []
        for c, part in enumerate(parts):
            part_copies.append(pltpu.make_async_copy(own_ref.at[part], own_buf.at[part], own_sem.at[c]))
            part_copies.append(pltpu.make_async_copy(arrived_ref.at[part], arrived_buf.at[part], arrived_sem.at[c]))
        for copy in part_copies:
            copy.start()
    zero_ref[...] = jnp.zeros_like(zero_ref)
    zero_copies = []
    for k in range(keep):
        at = pl.multiple_of(kept_ref[k] // col_blocks * BLK, BLK)
        col = pl.multiple_of(kept_ref[k] % col_blocks * BLK, BLK)
        zero_copies.append(
            pltpu.make_async_copy(zero_ref, res_ref.at[pl.ds(at, BLK), pl.ds(col, BLK)], zero_sem.at[k])
        )
        zero_copies[k].start()
    for copy in block_copies:
        copy.wait()

    row = lax.broadcasted_iota(jnp.int32, (total, BLK), 0)
    lane = lax.broadcasted_iota(jnp.int32, (total, BLK), 1)
    numbers = jnp.full((total, BLK), -1, jnp.int32)
    for g in range(groups):
        digits = block_buf[g, keep * BLK :, :].astype(jnp.float32).astype(jnp.int32)
        numbers = jnp.where(lane // keep == g, digits[0:1, :] * RADIX + digits[1:2, :], numbers)
    numbers = numbers.astype(jnp.float32)
    number = jnp.sum(jnp.where(lane == row, numbers, 0.0), axis=1, keepdims=True)
    first = jnp.min(jnp.where(numbers == number, lane.astype(jnp.float32), float(BLK)), axis=1, keepdims=True)
    number = jnp.broadcast_to(number, (total, BLK)).astype(jnp.int32)
    first = jnp.broadcast_to(first, (total, BLK)).astype(jnp.int32)
    table_ref[...] = jnp.where(lane == 0, jnp.where(number % groups == me, first, -1), number // groups)
    table = pltpu.make_async_copy(table_ref, scalar_ref, table_sem)
    table.start()

    grad_copies = []
    if pair:
        for c, part in enumerate(parts):
            for copy in part_copies[2 * c : 2 * c + 2]:
                copy.wait()
            grad_buf[part, :] = (own_buf[part, :] + arrived_buf[part, :].astype(jnp.float32)).astype(jnp.bfloat16)
            grad_copies.append(pltpu.make_async_copy(grad_buf.at[part, :], grad_ref.at[part, :], grad_sem.at[c]))
            grad_copies[c].start()

    table.wait()

    def copy(i):
        return pltpu.make_async_copy(sum_ref.at[i], out_ref.at[scalar_ref[i, 1]], sem.at[i])

    def block(i):
        at = i % keep * BLK
        return block_buf[i // keep, at : at + BLK, :].astype(jnp.float32)

    for i in range(total):
        slot = scalar_ref[i, 0]

        @pl.when(slot == i)
        def _(i=i):
            sum_ref[i] = block(i)

        if i >= keep:

            @pl.when((slot >= 0) & (slot < i))
            def _(i=i, slot=slot):
                sum_ref[slot] += block(i)

    for i in range(total):

        @pl.when(scalar_ref[i, 0] == i)
        def _(i=i):
            copy(i).start()

    for done in zero_copies + grad_copies:
        done.wait()
    for i in range(total):

        @pl.when(scalar_ref[i, 0] == i)
        def _(i=i):
            copy(i).wait()


def finish(me, kept, parts, blocks, zeros, residual):
    groups = len(blocks)
    keep = kept.shape[0]
    out_shape = [jax.ShapeDtypeStruct(a.shape, a.dtype) for a in (zeros, residual)]
    out_specs = [anywhere(), anywhere()]
    scratch = [
        pltpu.VMEM((groups,) + blocks[0].shape, jnp.bfloat16),
        pltpu.VMEM((groups * keep, BLK, BLK), jnp.float32),
        pltpu.VMEM((groups * keep, BLK), jnp.int32),
        pltpu.SMEM((groups * keep, BLK), jnp.int32),
        pltpu.VMEM((BLK, BLK), jnp.bfloat16),
        pltpu.SemaphoreType.DMA((groups,)),
        pltpu.SemaphoreType.DMA((groups * keep,)),
        pltpu.SemaphoreType.DMA,
        pltpu.SemaphoreType.DMA((keep,)),
    ]
    if parts:
        out_shape.insert(0, jax.ShapeDtypeStruct(parts[0].shape, jnp.bfloat16))
        out_specs.insert(0, anywhere())
        scratch += [
            pltpu.VMEM(parts[0].shape, jnp.float32),
            pltpu.VMEM(parts[0].shape, jnp.bfloat16),
            pltpu.VMEM(parts[0].shape, jnp.bfloat16),
        ] + [pltpu.SemaphoreType.DMA((4,))] * 3
    first = 2 + len(parts) + groups
    return pl.pallas_call(
        functools.partial(finish_kernel, groups, keep, bool(parts), residual.shape[1] // BLK),
        out_shape=out_shape,
        in_specs=[smem(), smem()] + [anywhere()] * (len(parts) + groups + 2),
        out_specs=out_specs,
        scratch_shapes=scratch,
        input_output_aliases={first: len(out_shape) - 2, first + 1: len(out_shape) - 1},
        compiler_params=params(24),
        cost_estimate=cost(groups * keep * BLK * BLK, groups * keep * BLK * BLK * 8),
        name="finish",
    )(me, kept, *parts, *blocks, zeros, residual)


def swapped(x, axis, mask):
    return lax.ppermute(x, axis, [(i, i ^ mask) for i in range(lax.axis_size(axis))])


def of_all_groups(x):
    return [x] + [swapped(x, "dp", mask) for mask in range(1, lax.axis_size("dp"))]


def body(activations, cotangent, weight, residual, step_size, kept_blocks):
    rows, cols = weight.shape
    groups = lax.axis_size("dp")
    owned_count = (rows // BLK) * (cols // BLK) // groups
    kept = kept_blocks.reshape(-1)
    me = lax.axis_index("dp").astype(jnp.int32).reshape(1)
    here = lax.axis_index("tensor").astype(jnp.int32).reshape(1)
    pair = lax.axis_size("tensor") == 2
    if pair:
        act = swapped(activations, "tensor", 1)
        away, own_t, own, zeros = input_grad_partials(here, cotangent, weight, owned_count, activations)
        parts = [own, swapped(away, "tensor", 1)]
    else:
        act = lax.all_gather(activations, "tensor", axis=0, tiled=True)
        own_t = None
        own, zeros = input_grad_partials(here, cotangent, weight, owned_count, None)
        summed = lax.psum_scatter(own, "tensor", scatter_dimension=0, tiled=True)
        parts = []
    act_t, blocks = kept_blocks_of(here, kept, step_size, own_t, act, cotangent, residual[0])
    all_blocks = of_all_groups(blocks)
    acts_t = [own_t, act_t] if pair else [act_t]
    rounded = residual_of(here, step_size, acts_t, cotangent, residual[0])
    *grads, owned, residual_out = finish(me, kept, parts, all_blocks, zeros, rounded)
    input_grad = grads[0] if pair else summed.astype(jnp.bfloat16)
    return (input_grad, residual_out[None], owned.reshape(1, 1, 1, owned_count, BLK, BLK))


def solution(mesh):
    in_specs = (
        P(("dp", "tensor"), "fsdp"),
        P("dp", "tensor"),
        P("fsdp", "tensor"),
        P("dp", "fsdp", "tensor"),
        P(),
        P("dp", "fsdp", "tensor", None),
    )
    out_specs = (
        P(("dp", "tensor"), "fsdp"),
        P("dp", "fsdp", "tensor"),
        P("dp", "fsdp", "tensor", None, None, None),
    )
    return jax.shard_map(body, mesh=mesh, in_specs=in_specs, out_specs=out_specs, check_vma=False)
```

```python
import functools

import jax
import jax.numpy as jnp
from jax import lax
from jax.experimental import pallas as pl
from jax.experimental.pallas import tpu as pltpu
from jax.sharding import PartitionSpec as P

BLK = 128
MIB = 1024 * 1024
LABEL_ROWS = 16
RADIX = 16


def cost(flops, nbytes):
    return pl.CostEstimate(flops=flops, bytes_accessed=nbytes, transcendentals=0)


def params(mib=62):
    return pltpu.CompilerParams(vmem_limit_bytes=mib * MIB)


def dot_nt(a, b):
    return lax.dot_general(a, b, (((1,), (1,)), ((), ())), preferred_element_type=jnp.float32)


def dot_nn(a, b):
    return lax.dot_general(a, b, (((1,), (0,)), ((), ())), preferred_element_type=jnp.float32)


def hidden_chunks(cols):
    sizes = []
    for size in (512, 1536, 2048, 4096):
        if cols > sum(sizes):
            sizes.append(min(size, cols - sum(sizes)))
    while sum(sizes) < cols:
        sizes.append(min(4096, cols - sum(sizes)))
    return sizes


def smem():
    return pl.BlockSpec(memory_space=pltpu.SMEM)


def vmem():
    return pl.BlockSpec(memory_space=pltpu.VMEM)


def hbm():
    return pl.BlockSpec(memory_space=pltpu.HBM)


def in_hbm(x):
    return pltpu.with_memory_space_constraint(x, pltpu.HBM)


def in_vmem(x):
    return pltpu.with_memory_space_constraint(x, pltpu.VMEM)


def cot_copies(here_ref, split, cot_ref, buf_ref, sems):
    if not split:
        return [pltpu.make_async_copy(cot_ref, buf_ref, sems.at[0])]
    half = buf_ref.shape[0] // 2
    copies = []
    for i, at in enumerate((here_ref[0], 1 - here_ref[0])):
        rows = pl.ds(pl.multiple_of(at * half, half), half)
        copies.append(pltpu.make_async_copy(cot_ref.at[rows], buf_ref.at[pl.ds(i * half, half)], sems.at[i]))
    return copies


def input_grad_kernel(split, sizes, zero_copies, here_ref, kept_ref, cot_ref, w_ref, res_ref, *refs):
    if split:
        acts_ref, away_ref, acts_t_ref, *refs = refs
    own_ref, owned_ref, kept_cot_ref, kept_res_ref, *refs = refs
    acc_ref, cot_buf, w_buf, zero_ref, cot_sem, w_sem, zero_sem, kept_cot_sem, kept_res_sem, *refs = refs
    zero_rows = zero_ref.shape[0]
    rows, hidden = w_ref.shape
    width = min(256, rows)
    last = len(sizes) - 1
    keep = kept_cot_ref.shape[0]
    half = own_ref.shape[0]

    def loads(i):
        part = pl.ds(sum(sizes[:i]), sizes[i])
        return cot_copies(here_ref, split, cot_ref.at[:, part], cot_buf.at[:, part], cot_sem.at[i]) + [
            pltpu.make_async_copy(w_ref.at[:, part], w_buf.at[:, part], w_sem.at[i])
        ]

    def start(i):
        if i <= last:
            for copy in loads(i):
                copy.start()

    def zero_copy(i):
        return pltpu.make_async_copy(zero_ref, owned_ref.at[pl.ds(i * zero_rows, zero_rows)], zero_sem.at[i])

    def kept_copies(k):
        col_blocks = hidden // BLK
        row = pl.ds(pl.multiple_of(kept_ref[k] // col_blocks * BLK, BLK), BLK)
        col = pl.ds(pl.multiple_of(kept_ref[k] % col_blocks * BLK, BLK), BLK)
        return (
            pltpu.make_async_copy(cot_buf.at[:, col], kept_cot_ref.at[k], kept_cot_sem.at[k]),
            pltpu.make_async_copy(res_ref.at[row, col], kept_res_ref.at[k], kept_res_sem.at[k]),
        )

    if split:
        acts_buf, acts_sem = refs
        acts_copy = pltpu.make_async_copy(acts_ref, acts_buf, acts_sem)
        acts_copy.start()
    start(0)
    if split:
        acts_copy.wait()
        acts_t_ref[:, :half] = acts_buf[...].T
    start(1)
    zero_ref[...] = jnp.zeros_like(zero_ref)
    for i in range(last + 1):
        for copy in loads(i):
            copy.wait()
        start(i + 2)
        if i == last:
            for z in range(zero_copies):
                zero_copy(z).start()
            for k in range(keep):
                for copy in kept_copies(k):
                    copy.start()
        part = slice(sum(sizes[:i]), sum(sizes[: i + 1]))
        for at in range(0, rows, width):
            cols = slice(at, at + width)
            total = dot_nt(cot_buf[:, part], w_buf[cols, part])
            if i > 0:
                total += acc_ref[:, cols]
            if i < last:
                acc_ref[:, cols] = total
            else:
                own_ref[:, cols] = total[:half]
                if split:
                    away_ref[:, cols] = total[half:].astype(jnp.bfloat16)
    for z in range(zero_copies):
        zero_copy(z).wait()
    for k in range(keep):
        for copy in kept_copies(k):
            copy.wait()


def input_grad_partials(here, kept, cot, weight, residual, owned_count, acts):
    split = acts is not None
    tokens, cols = cot.shape
    rows = weight.shape[0]
    sizes = hidden_chunks(cols)
    keep = kept.shape[0]
    own_rows = tokens // 2 if split else tokens
    zero_rows = min(16, owned_count)
    zero_copies = owned_count // zero_rows
    out_shape = [
        pltpu.VMEM((own_rows, rows), jnp.float32) if split else jax.ShapeDtypeStruct((own_rows, rows), jnp.float32),
        pltpu.HBM((owned_count, BLK, BLK), jnp.float32),
        pltpu.VMEM((keep, tokens, BLK), jnp.bfloat16),
        pltpu.VMEM((keep, BLK, BLK), jnp.bfloat16),
    ]
    out_specs = [vmem(), hbm(), vmem(), vmem()]
    scratch = [
        pltpu.VMEM((tokens, rows), jnp.float32),
        pltpu.VMEM((tokens, cols), jnp.bfloat16),
        pltpu.VMEM((rows, cols), jnp.bfloat16),
        pltpu.VMEM((zero_rows, BLK, BLK), jnp.float32),
        pltpu.SemaphoreType.DMA((len(sizes), 2)),
        pltpu.SemaphoreType.DMA((len(sizes),)),
        pltpu.SemaphoreType.DMA((zero_copies,)),
        pltpu.SemaphoreType.DMA((keep,)),
        pltpu.SemaphoreType.DMA((keep,)),
    ]
    if split:
        out_shape = [
            jax.ShapeDtypeStruct((own_rows, rows), jnp.bfloat16),
            pltpu.VMEM((rows, tokens), jnp.bfloat16),
        ] + out_shape
        out_specs = [vmem(), vmem()] + out_specs
        scratch += [pltpu.VMEM(acts.shape, jnp.bfloat16), pltpu.SemaphoreType.DMA]
    return pl.pallas_call(
        functools.partial(input_grad_kernel, split, sizes, zero_copies),
        out_shape=out_shape,
        in_specs=[smem(), smem()] + [hbm()] * (3 + split),
        out_specs=out_specs,
        scratch_shapes=scratch,
        compiler_params=params(52),
        cost_estimate=cost(2 * tokens * rows * cols, 2 * cols * (tokens + rows) + 4 * owned_count * BLK * BLK),
        name="input_grad_partials",
    )(here, kept, in_hbm(cot), in_hbm(weight), in_hbm(residual), *([in_hbm(acts)] if split else []))


def kept_kernel(pair, col_blocks, kept_ref, step_ref, *refs):
    if pair:
        _, *refs = refs
    act_ref, cot_ref, res_ref, acts_t_ref, out_ref = refs
    keep = cot_ref.shape[0]
    acts_t_ref[:, acts_t_ref.shape[1] - act_ref.shape[0] :] = act_ref[...].T
    for k in range(keep):
        row = pl.ds(pl.multiple_of(kept_ref[k] // col_blocks * BLK, BLK), BLK)
        gradient = dot_nn(acts_t_ref[row, :], cot_ref[k])
        out_ref[k * BLK : (k + 1) * BLK, :] = (res_ref[k].astype(jnp.float32) + step_ref[0] * gradient).astype(
            jnp.bfloat16
        )
    lane = lax.broadcasted_iota(jnp.int32, (LABEL_ROWS, BLK), 1) % keep
    low = lax.broadcasted_iota(jnp.int32, (LABEL_ROWS, BLK), 0) % 2 == 1
    label = jnp.zeros((LABEL_ROWS, BLK), jnp.int32)
    for k in range(keep):
        digit = jnp.where(low, kept_ref[k] % RADIX, kept_ref[k] // RADIX)
        label = jnp.where(lane == k, digit, label)
    out_ref[keep * BLK :, :] = label.astype(jnp.float32).astype(jnp.bfloat16)


def kept_blocks_of(kept, step_size, acts_t, act, kept_cot, kept_res, col_blocks):
    rows = act.shape[1]
    keep, tokens = kept_cot.shape[:2]
    pair = acts_t is not None
    return pl.pallas_call(
        functools.partial(kept_kernel, pair, col_blocks),
        out_shape=[
            pltpu.VMEM((rows, tokens), jnp.bfloat16),
            jax.ShapeDtypeStruct((keep * BLK + LABEL_ROWS, BLK), jnp.bfloat16),
        ],
        in_specs=[smem()] * 2 + [vmem()] * (3 + pair),
        out_specs=[vmem(), vmem()],
        input_output_aliases={2: 0} if pair else {},
        compiler_params=params(16),
        cost_estimate=cost(2 * tokens * BLK * BLK * keep, 4 * tokens * rows + 2 * keep * tokens * BLK),
        name="kept_blocks",
    )(kept, step_size, *([in_vmem(acts_t)] if pair else []), act, in_vmem(kept_cot), in_vmem(kept_res))


def residual_kernel(split, here_ref, step_ref, acts_t_ref, cot_ref, res_ref, out_ref, cot_buf, res_buf, *sems):
    cot_sem, res_sem, out_sem = sems
    step = step_ref[0]
    chunks, _, chunk = cot_buf.shape
    width = min(256, chunk)

    def columns(j):
        return pl.ds(pl.multiple_of(j * chunk, chunk), chunk)

    def loads(j):
        return cot_copies(here_ref, split, cot_ref.at[:, columns(j)], cot_buf.at[j], cot_sem.at[j]) + [
            pltpu.make_async_copy(res_ref.at[:, columns(j)], res_buf.at[j], res_sem.at[j])
        ]

    def store(j):
        return pltpu.make_async_copy(res_buf.at[j], out_ref.at[:, columns(j)], out_sem.at[j])

    def start(j):
        @pl.when(j < chunks)
        def _():
            for copy in loads(j):
                copy.start()

    start(0)
    start(1)

    @pl.loop(0, chunks)
    def _(j):
        for copy in loads(j):
            copy.wait()
        start(j + 2)
        for at in range(0, chunk, width):
            part = slice(at, at + width)
            gradient = dot_nn(acts_t_ref[...], cot_buf[j, :, part])
            res_buf[j, :, part] = (res_buf[j, :, part].astype(jnp.float32) + step * gradient).astype(jnp.bfloat16)
        store(j).start()

    for j in range(chunks):
        store(j).wait()


def residual_of(here, step_size, acts_t, cot, residual, split):
    tokens, cols = cot.shape
    rows = residual.shape[0]
    chunk = min(1024, cols)
    chunks = cols // chunk
    sem = pltpu.SemaphoreType.DMA((chunks,))
    return pl.pallas_call(
        functools.partial(residual_kernel, split),
        out_shape=pltpu.HBM((rows, cols), jnp.bfloat16),
        in_specs=[smem()] * 2 + [vmem(), hbm(), hbm()],
        out_specs=hbm(),
        scratch_shapes=[
            pltpu.VMEM((chunks, tokens, chunk), jnp.bfloat16),
            pltpu.VMEM((chunks, rows, chunk), jnp.bfloat16),
            pltpu.SemaphoreType.DMA((chunks, 2)),
            sem,
            sem,
        ],
        compiler_params=params(44),
        cost_estimate=cost(2 * tokens * rows * cols, 2 * tokens * (rows + cols) + 4 * rows * cols),
        name="residual_out",
    )(here, step_size, in_vmem(acts_t), in_hbm(cot), in_hbm(residual))


def finish_kernel(groups, keep, pair, col_blocks, me_ref, kept_ref, *refs):
    if pair:
        own_ref, arrived_ref, *refs = refs
    block_refs = refs[:groups]
    refs = refs[groups + 2 :]
    if pair:
        grad_ref, *refs = refs
    out_ref, res_ref, sum_ref, table_ref, scalar_ref, zero_ref, sem, table_sem, zero_sem, *refs = refs
    total = groups * keep
    me = me_ref[0]

    zero_ref[...] = jnp.zeros_like(zero_ref)
    zero_copies = []
    for k in range(keep):
        at = pl.multiple_of(kept_ref[k] // col_blocks * BLK, BLK)
        col = pl.multiple_of(kept_ref[k] % col_blocks * BLK, BLK)
        zero_copies.append(
            pltpu.make_async_copy(zero_ref, res_ref.at[pl.ds(at, BLK), pl.ds(col, BLK)], zero_sem.at[k])
        )
        zero_copies[k].start()

    row = lax.broadcasted_iota(jnp.int32, (total, BLK), 0)
    lane = lax.broadcasted_iota(jnp.int32, (total, BLK), 1)
    numbers = jnp.full((total, BLK), -1, jnp.int32)
    for g, block_ref in enumerate(block_refs):
        digits = block_ref[keep * BLK :, :].astype(jnp.float32).astype(jnp.int32)
        numbers = jnp.where(lane // keep == g, digits[0:1, :] * RADIX + digits[1:2, :], numbers)
    numbers = numbers.astype(jnp.float32)
    number = jnp.sum(jnp.where(lane == row, numbers, 0.0), axis=1, keepdims=True)
    first = jnp.min(jnp.where(numbers == number, lane.astype(jnp.float32), float(BLK)), axis=1, keepdims=True)
    number = jnp.broadcast_to(number, (total, BLK)).astype(jnp.int32)
    first = jnp.broadcast_to(first, (total, BLK)).astype(jnp.int32)
    table_ref[...] = jnp.where(lane == 0, jnp.where(number % groups == me, first, -1), number // groups)
    table = pltpu.make_async_copy(table_ref, scalar_ref, table_sem)
    table.start()

    grad_copies = []
    if pair:
        grad_buf, grad_sem = refs
        size = grad_buf.shape[0] // grad_sem.shape[0]
        for c in range(grad_sem.shape[0]):
            part = slice(c * size, (c + 1) * size)
            grad_buf[part, :] = (own_ref[part, :] + arrived_ref[part, :].astype(jnp.float32)).astype(jnp.bfloat16)
            grad_copies.append(pltpu.make_async_copy(grad_buf.at[part, :], grad_ref.at[part, :], grad_sem.at[c]))
            grad_copies[c].start()

    table.wait()

    def copy(i):
        return pltpu.make_async_copy(sum_ref.at[i], out_ref.at[scalar_ref[i, 1]], sem.at[i])

    def block(i):
        at = i % keep * BLK
        return block_refs[i // keep][at : at + BLK, :].astype(jnp.float32)

    for i in range(total):
        slot = scalar_ref[i, 0]

        @pl.when(slot == i)
        def _(i=i):
            sum_ref[i] = block(i)

        if i >= keep:

            @pl.when((slot >= 0) & (slot < i))
            def _(i=i, slot=slot):
                sum_ref[slot] += block(i)

    for i in range(total):

        @pl.when(scalar_ref[i, 0] == i)
        def _(i=i):
            copy(i).start()

    for done in zero_copies + grad_copies:
        done.wait()
    for i in range(total):

        @pl.when(scalar_ref[i, 0] == i)
        def _(i=i):
            copy(i).wait()


def finish(me, kept, parts, blocks, zeros, residual):
    groups = len(blocks)
    keep = kept.shape[0]
    out_shape = [pltpu.HBM(a.shape, a.dtype) for a in (zeros, residual)]
    out_specs = [hbm(), hbm()]
    scratch = [
        pltpu.VMEM((groups * keep, BLK, BLK), jnp.float32),
        pltpu.VMEM((groups * keep, BLK), jnp.int32),
        pltpu.SMEM((groups * keep, BLK), jnp.int32),
        pltpu.VMEM((BLK, BLK), jnp.bfloat16),
        pltpu.SemaphoreType.DMA((groups * keep,)),
        pltpu.SemaphoreType.DMA,
        pltpu.SemaphoreType.DMA((keep,)),
    ]
    if parts:
        out_shape.insert(0, pltpu.HBM(parts[0].shape, jnp.bfloat16))
        out_specs.insert(0, hbm())
        scratch += [pltpu.VMEM(parts[0].shape, jnp.bfloat16), pltpu.SemaphoreType.DMA((4,))]
        parts = [in_vmem(parts[0]), parts[1]]
    first = 2 + len(parts) + groups
    return pl.pallas_call(
        functools.partial(finish_kernel, groups, keep, bool(parts), residual.shape[1] // BLK),
        out_shape=out_shape,
        in_specs=[smem(), smem()] + [vmem()] * (len(parts) + groups) + [hbm(), hbm()],
        out_specs=out_specs,
        scratch_shapes=scratch,
        input_output_aliases={first: len(out_shape) - 2, first + 1: len(out_shape) - 1},
        compiler_params=params(24),
        cost_estimate=cost(groups * keep * BLK * BLK, groups * keep * BLK * BLK * 8),
        name="finish",
    )(me, kept, *parts, *blocks, in_hbm(zeros), in_hbm(residual))


def swapped(x, axis, mask):
    return lax.ppermute(x, axis, [(i, i ^ mask) for i in range(lax.axis_size(axis))])


def of_all_groups(x):
    return [x] + [swapped(x, "dp", mask) for mask in range(1, lax.axis_size("dp"))]


def body(activations, cotangent, weight, residual, step_size, kept_blocks):
    rows, cols = weight.shape
    groups = lax.axis_size("dp")
    owned_count = (rows // BLK) * (cols // BLK) // groups
    kept = kept_blocks.reshape(-1)
    me = lax.axis_index("dp").astype(jnp.int32).reshape(1)
    here = lax.axis_index("tensor").astype(jnp.int32).reshape(1)
    pair = lax.axis_size("tensor") == 2
    if pair:
        act = swapped(activations, "tensor", 1)
        away, acts_t, own, zeros, kept_cot, kept_res = input_grad_partials(
            here, kept, cotangent, weight, residual[0], owned_count, activations
        )
        parts = [own, swapped(away, "tensor", 1)]
    else:
        act = lax.all_gather(activations, "tensor", axis=0, tiled=True)
        acts_t = None
        own, zeros, kept_cot, kept_res = input_grad_partials(
            here, kept, cotangent, weight, residual[0], owned_count, None
        )
        summed = lax.psum_scatter(own, "tensor", scatter_dimension=0, tiled=True)
        parts = []
    acts_t, blocks = kept_blocks_of(kept, step_size, acts_t, act, kept_cot, kept_res, cols // BLK)
    all_blocks = of_all_groups(blocks)
    rounded = residual_of(here, step_size, acts_t, cotangent, residual[0], pair)
    *grads, owned, residual_out = finish(me, kept, parts, all_blocks, zeros, rounded)
    input_grad = grads[0] if pair else summed.astype(jnp.bfloat16)
    return (input_grad, residual_out[None], owned.reshape(1, 1, 1, owned_count, BLK, BLK))


def solution(mesh):
    in_specs = (
        P(("dp", "tensor"), "fsdp"),
        P("dp", "tensor"),
        P("fsdp", "tensor"),
        P("dp", "fsdp", "tensor"),
        P(),
        P("dp", "fsdp", "tensor", None),
    )
    out_specs = (
        P(("dp", "tensor"), "fsdp"),
        P("dp", "fsdp", "tensor"),
        P("dp", "fsdp", "tensor", None, None, None),
    )
    return jax.shard_map(body, mesh=mesh, in_specs=in_specs, out_specs=out_specs, check_vma=False)
```

```python
import functools

import jax
import jax.numpy as jnp
from jax import lax
from jax.experimental import pallas as pl
from jax.experimental.pallas import tpu as pltpu
from jax.sharding import PartitionSpec as P

BLK = 128
MIB = 1024 * 1024
LABEL_ROWS = 16
RADIX = 16


def cost(flops, nbytes):
    return pl.CostEstimate(flops=flops, bytes_accessed=nbytes, transcendentals=0)


def params(mib=62):
    return pltpu.CompilerParams(vmem_limit_bytes=mib * MIB)


def dot_nt(a, b):
    return lax.dot_general(a, b, (((1,), (1,)), ((), ())), preferred_element_type=jnp.float32)


def dot_nn(a, b):
    return lax.dot_general(a, b, (((1,), (0,)), ((), ())), preferred_element_type=jnp.float32)


def hidden_chunks(cols):
    sizes = []
    for size in (512, 1024, 2048, 4608):
        if cols > sum(sizes):
            sizes.append(min(size, cols - sum(sizes)))
    while sum(sizes) < cols:
        sizes.append(min(4608, cols - sum(sizes)))
    return sizes


def smem():
    return pl.BlockSpec(memory_space=pltpu.SMEM)


def vmem():
    return pl.BlockSpec(memory_space=pltpu.VMEM)


def hbm():
    return pl.BlockSpec(memory_space=pltpu.HBM)


def in_hbm(x):
    return pltpu.with_memory_space_constraint(x, pltpu.HBM)


def in_vmem(x):
    return pltpu.with_memory_space_constraint(x, pltpu.VMEM)


def cot_copies(here_ref, split, cot_ref, buf_ref, sems):
    if not split:
        return [pltpu.make_async_copy(cot_ref, buf_ref, sems.at[0])]
    half = buf_ref.shape[0] // 2
    copies = []
    for i, at in enumerate((here_ref[0], 1 - here_ref[0])):
        rows = pl.ds(pl.multiple_of(at * half, half), half)
        copies.append(pltpu.make_async_copy(cot_ref.at[rows], buf_ref.at[pl.ds(i * half, half)], sems.at[i]))
    return copies


def input_grad_kernel(split, sizes, zero_copies, here_ref, _, kept_ref, cot_ref, w_ref, res_ref, *refs):
    if split:
        acts_ref, away_ref, acts_t_ref, *refs = refs
    own_ref, owned_ref, cot_buf, kept_res_ref, *refs = refs
    acc_ref, w_buf, zero_ref, cot_sem, w_sem, zero_sem, kept_res_sem, *refs = refs
    zero_rows = zero_ref.shape[0]
    rows, hidden = w_ref.shape
    width = min(256, rows)
    last = len(sizes) - 1
    keep = kept_res_ref.shape[0]
    half = own_ref.shape[0]

    def loads(i):
        part = pl.ds(sum(sizes[:i]), sizes[i])
        return cot_copies(here_ref, split, cot_ref.at[:, part], cot_buf.at[:, part], cot_sem.at[i]) + [
            pltpu.make_async_copy(w_ref.at[:, part], w_buf.at[:, part], w_sem.at[i])
        ]

    def start(i):
        if i <= last:
            for copy in loads(i):
                copy.start()

    def zero_copy(i):
        return pltpu.make_async_copy(zero_ref, owned_ref.at[pl.ds(i * zero_rows, zero_rows)], zero_sem.at[i])

    def kept_copy(k):
        col_blocks = hidden // BLK
        row = pl.ds(pl.multiple_of(kept_ref[k] // col_blocks * BLK, BLK), BLK)
        col = pl.ds(pl.multiple_of(kept_ref[k] % col_blocks * BLK, BLK), BLK)
        return pltpu.make_async_copy(res_ref.at[row, col], kept_res_ref.at[k], kept_res_sem.at[k])

    start(0)
    start(1)
    if split:
        acts_buf, acts_sem = refs
        acts_copy = pltpu.make_async_copy(acts_ref, acts_buf, acts_sem)
        acts_copy.start()
    zero_ref[...] = jnp.zeros_like(zero_ref)
    turned = min(1, last)
    for i in range(last + 1):
        for copy in loads(i):
            copy.wait()
        if split and i == turned:
            acts_copy.wait()
        start(i + 2)
        if i == last:
            for z in range(zero_copies):
                zero_copy(z).start()
            for k in range(keep):
                kept_copy(k).start()
        part = slice(sum(sizes[:i]), sum(sizes[: i + 1]))
        for at in range(0, rows, width):
            cols = slice(at, at + width)
            total = dot_nt(cot_buf[:, part], w_buf[cols, part])
            if split and i == turned:
                acts_t_ref[cols, :half] = acts_buf[:, cols].T
            if i > 0:
                total += acc_ref[:, cols]
            if i < last:
                acc_ref[:, cols] = total
            else:
                own_ref[:, cols] = total[:half]
                if split:
                    away_ref[:, cols] = total[half:].astype(jnp.bfloat16)
    for z in range(zero_copies):
        zero_copy(z).wait()
    for k in range(keep):
        kept_copy(k).wait()


def input_grad_partials(here, me, kept, cot, weight, residual, owned_count, acts):
    split = acts is not None
    tokens, cols = cot.shape
    rows = weight.shape[0]
    sizes = hidden_chunks(cols)
    keep = kept.shape[0]
    own_rows = tokens // 2 if split else tokens
    zero_rows = min(16, owned_count)
    zero_copies = owned_count // zero_rows
    out_shape = [
        pltpu.VMEM((own_rows, rows), jnp.float32) if split else jax.ShapeDtypeStruct((own_rows, rows), jnp.float32),
        pltpu.HBM((owned_count, BLK, BLK), jnp.float32),
        pltpu.VMEM((tokens, cols), jnp.bfloat16),
        pltpu.VMEM((keep, BLK, BLK), jnp.bfloat16),
    ]
    out_specs = [vmem(), hbm(), vmem(), vmem()]
    scratch = [
        pltpu.VMEM((tokens, rows), jnp.float32),
        pltpu.VMEM((rows, cols), jnp.bfloat16),
        pltpu.VMEM((zero_rows, BLK, BLK), jnp.float32),
        pltpu.SemaphoreType.DMA((len(sizes), 2)),
        pltpu.SemaphoreType.DMA((len(sizes),)),
        pltpu.SemaphoreType.DMA((zero_copies,)),
        pltpu.SemaphoreType.DMA((keep,)),
    ]
    if split:
        out_shape = [
            jax.ShapeDtypeStruct((own_rows, rows), jnp.bfloat16),
            pltpu.VMEM((rows, tokens), jnp.bfloat16),
        ] + out_shape
        out_specs = [vmem(), vmem()] + out_specs
        scratch += [pltpu.VMEM(acts.shape, jnp.bfloat16), pltpu.SemaphoreType.DMA]
    return pl.pallas_call(
        functools.partial(input_grad_kernel, split, sizes, zero_copies),
        out_shape=out_shape,
        in_specs=[smem()] * 3 + [hbm()] * (3 + split),
        out_specs=out_specs,
        scratch_shapes=scratch,
        compiler_params=params(34),
        cost_estimate=cost(2 * tokens * rows * cols, 2 * cols * (tokens + rows) + 4 * owned_count * BLK * BLK),
        name="input_grad_partials",
    )(here, me, kept, in_hbm(cot), in_hbm(weight), in_hbm(residual), *([in_hbm(acts)] if split else []))


def kept_kernel(pair, kept_ref, step_in, *refs):
    if pair:
        _, *refs = refs
    act_ref, cot_ref, kept_res_ref, acts_t_ref, out_ref, step_ref, step_sem = refs
    keep = kept_res_ref.shape[0]
    col_blocks = cot_ref.shape[1] // BLK
    step_copy = pltpu.make_async_copy(step_in, step_ref, step_sem)
    step_copy.start()
    acts_t_ref[:, acts_t_ref.shape[1] - act_ref.shape[0] :] = act_ref[...].T
    step_copy.wait()
    step = step_ref[0]
    for k in range(keep):
        row = pl.ds(pl.multiple_of(kept_ref[k] // col_blocks * BLK, BLK), BLK)
        col = pl.ds(pl.multiple_of(kept_ref[k] % col_blocks * BLK, BLK), BLK)
        gradient = dot_nn(acts_t_ref[row, :], cot_ref[:, col])
        out_ref[k * BLK : (k + 1) * BLK, :] = (kept_res_ref[k].astype(jnp.float32) + step * gradient).astype(
            jnp.bfloat16
        )
    lane = lax.broadcasted_iota(jnp.int32, (LABEL_ROWS, BLK), 1) % keep
    low = lax.broadcasted_iota(jnp.int32, (LABEL_ROWS, BLK), 0) % 2 == 1
    label = jnp.zeros((LABEL_ROWS, BLK), jnp.int32)
    for k in range(keep):
        digit = jnp.where(low, kept_ref[k] % RADIX, kept_ref[k] // RADIX)
        label = jnp.where(lane == k, digit, label)
    out_ref[keep * BLK :, :] = label.astype(jnp.float32).astype(jnp.bfloat16)


def kept_blocks_of(kept, step_size, acts_t, act, cot, kept_res):
    rows = act.shape[1]
    tokens, cols = cot.shape
    keep = kept_res.shape[0]
    pair = acts_t is not None
    return pl.pallas_call(
        functools.partial(kept_kernel, pair),
        out_shape=[
            pltpu.VMEM((rows, tokens), jnp.bfloat16),
            jax.ShapeDtypeStruct((keep * BLK + LABEL_ROWS, BLK), jnp.bfloat16),
        ],
        in_specs=[smem(), pl.BlockSpec(memory_space=pl.ANY)] + [vmem()] * (3 + pair),
        out_specs=[vmem()] * 2,
        scratch_shapes=[pltpu.SMEM((1,), jnp.float32), pltpu.SemaphoreType.DMA],
        input_output_aliases={2: 0} if pair else {},
        compiler_params=params(4),
        cost_estimate=cost(2 * tokens * BLK * BLK * keep, 4 * tokens * rows + 2 * keep * tokens * BLK),
        name="kept_blocks",
    )(
        kept,
        step_size,
        *([in_vmem(acts_t)] if pair else []),
        act,
        in_vmem(cot),
        in_vmem(kept_res),
    )


def residual_kernel(step_in, acts_t_ref, cot_ref, res_ref, out_ref, res_buf, step_ref, step_sem, res_sem, out_sem):
    chunks, _, chunk = res_buf.shape
    width = min(256, chunk)
    pieces = chunk // width

    def load(j):
        cols = pl.ds(pl.multiple_of(j * chunk, chunk), chunk)
        return pltpu.make_async_copy(res_ref.at[:, cols], res_buf.at[j], res_sem.at[j])

    def store(j, n):
        cols = pl.ds(pl.multiple_of(j * chunk + n * width, width), width)
        return pltpu.make_async_copy(
            res_buf.at[j, :, pl.ds(n * width, width)], out_ref.at[:, cols], out_sem.at[j, n]
        )

    def start(j):
        @pl.when(j < chunks)
        def _():
            load(j).start()

    step_copy = pltpu.make_async_copy(step_in, step_ref, step_sem)
    step_copy.start()
    start(0)
    start(1)
    step_copy.wait()
    step = step_ref[0]

    @pl.loop(0, chunks)
    def _(j):
        load(j).wait()
        start(j + 2)
        for n in range(pieces):
            part = slice(n * width, (n + 1) * width)
            cols = pl.ds(pl.multiple_of(j * chunk + n * width, width), width)
            gradient = dot_nn(acts_t_ref[...], cot_ref[:, cols])
            res_buf[j, :, part] = (res_buf[j, :, part].astype(jnp.float32) + step * gradient).astype(jnp.bfloat16)
            store(j, n).start()

    @pl.loop(0, chunks)
    def _(j):
        for n in range(pieces):
            store(j, n).wait()


def residual_of(step_size, acts_t, cot, residual):
    tokens, cols = cot.shape
    rows = residual.shape[0]
    chunk = min(1024, cols)
    chunks = cols // chunk
    return pl.pallas_call(
        residual_kernel,
        out_shape=pltpu.HBM((rows, cols), jnp.bfloat16),
        in_specs=[pl.BlockSpec(memory_space=pl.ANY), vmem(), vmem(), hbm()],
        out_specs=hbm(),
        scratch_shapes=[
            pltpu.VMEM((chunks, rows, chunk), jnp.bfloat16),
            pltpu.SMEM((1,), jnp.float32),
            pltpu.SemaphoreType.DMA,
            pltpu.SemaphoreType.DMA((chunks,)),
            pltpu.SemaphoreType.DMA((chunks, chunk // min(256, chunk))),
        ],
        compiler_params=params(20),
        cost_estimate=cost(2 * tokens * rows * cols, 2 * tokens * rows + 4 * rows * cols),
        name="residual_out",
    )(step_size, in_vmem(acts_t), in_vmem(cot), in_hbm(residual))


def finish_kernel(groups, keep, pair, col_blocks, me_ref, kept_ref, *refs):
    if pair:
        own_ref, arrived_ref, *refs = refs
    block_refs = refs[:groups]
    refs = refs[groups + 2 :]
    if pair:
        grad_ref, *refs = refs
    out_ref, res_ref, sum_ref, table_ref, scalar_ref, zero_ref, sem, table_sem, zero_sem, *refs = refs
    total = groups * keep
    me = me_ref[0]

    zero_ref[...] = jnp.zeros_like(zero_ref)
    zero_copies = []
    for k in range(keep):
        at = pl.multiple_of(kept_ref[k] // col_blocks * BLK, BLK)
        col = pl.multiple_of(kept_ref[k] % col_blocks * BLK, BLK)
        zero_copies.append(
            pltpu.make_async_copy(zero_ref, res_ref.at[pl.ds(at, BLK), pl.ds(col, BLK)], zero_sem.at[k])
        )
        zero_copies[k].start()

    row = lax.broadcasted_iota(jnp.int32, (total, BLK), 0)
    lane = lax.broadcasted_iota(jnp.int32, (total, BLK), 1)
    numbers = jnp.full((total, BLK), -1, jnp.int32)
    for g, block_ref in enumerate(block_refs):
        digits = block_ref[keep * BLK :, :].astype(jnp.float32).astype(jnp.int32)
        numbers = jnp.where(lane // keep == g, digits[0:1, :] * RADIX + digits[1:2, :], numbers)
    numbers = numbers.astype(jnp.float32)
    number = jnp.sum(jnp.where(lane == row, numbers, 0.0), axis=1, keepdims=True)
    first = jnp.min(jnp.where(numbers == number, lane.astype(jnp.float32), float(BLK)), axis=1, keepdims=True)
    number = jnp.broadcast_to(number, (total, BLK)).astype(jnp.int32)
    first = jnp.broadcast_to(first, (total, BLK)).astype(jnp.int32)
    table_ref[...] = jnp.where(lane == 0, jnp.where(number % groups == me, first, -1), number // groups)
    table = pltpu.make_async_copy(table_ref, scalar_ref, table_sem)
    table.start()

    grad_copies = []
    if pair:
        grad_buf, grad_sem = refs
        size = grad_buf.shape[0] // grad_sem.shape[0]
        for c in range(grad_sem.shape[0]):
            part = slice(c * size, (c + 1) * size)
            grad_buf[part, :] = (own_ref[part, :] + arrived_ref[part, :].astype(jnp.float32)).astype(jnp.bfloat16)
            grad_copies.append(pltpu.make_async_copy(grad_buf.at[part, :], grad_ref.at[part, :], grad_sem.at[c]))
            grad_copies[c].start()

    table.wait()

    def copy(i):
        return pltpu.make_async_copy(sum_ref.at[i], out_ref.at[scalar_ref[i, 1]], sem.at[i])

    def block(i):
        at = i % keep * BLK
        return block_refs[i // keep][at : at + BLK, :].astype(jnp.float32)

    for i in range(total):
        slot = scalar_ref[i, 0]

        @pl.when(slot == i)
        def _(i=i):
            sum_ref[i] = block(i)

        if i >= keep:

            @pl.when((slot >= 0) & (slot < i))
            def _(i=i, slot=slot):
                sum_ref[slot] += block(i)

    for i in range(total):

        @pl.when(scalar_ref[i, 0] == i)
        def _(i=i):
            copy(i).start()

    for done in zero_copies + grad_copies:
        done.wait()
    for i in range(total):

        @pl.when(scalar_ref[i, 0] == i)
        def _(i=i):
            copy(i).wait()


def finish(me, kept, parts, blocks, zeros, residual):
    groups = len(blocks)
    keep = kept.shape[0]
    out_shape = [pltpu.HBM(a.shape, a.dtype) for a in (zeros, residual)]
    out_specs = [hbm(), hbm()]
    scratch = [
        pltpu.VMEM((groups * keep, BLK, BLK), jnp.float32),
        pltpu.VMEM((groups * keep, BLK), jnp.int32),
        pltpu.SMEM((groups * keep, BLK), jnp.int32),
        pltpu.VMEM((BLK, BLK), jnp.bfloat16),
        pltpu.SemaphoreType.DMA((groups * keep,)),
        pltpu.SemaphoreType.DMA,
        pltpu.SemaphoreType.DMA((keep,)),
    ]
    if parts:
        out_shape.insert(0, pltpu.HBM(parts[0].shape, jnp.bfloat16))
        out_specs.insert(0, hbm())
        scratch += [pltpu.VMEM(parts[0].shape, jnp.bfloat16), pltpu.SemaphoreType.DMA((4,))]
        parts = [in_vmem(parts[0]), parts[1]]
    first = 2 + len(parts) + groups
    return pl.pallas_call(
        functools.partial(finish_kernel, groups, keep, bool(parts), residual.shape[1] // BLK),
        out_shape=out_shape,
        in_specs=[smem(), smem()] + [vmem()] * (len(parts) + groups) + [hbm(), hbm()],
        out_specs=out_specs,
        scratch_shapes=scratch,
        input_output_aliases={first: len(out_shape) - 2, first + 1: len(out_shape) - 1},
        compiler_params=params(10),
        cost_estimate=cost(groups * keep * BLK * BLK, groups * keep * BLK * BLK * 8),
        name="finish",
    )(me, kept, *parts, *blocks, in_hbm(zeros), in_hbm(residual))


def swapped(x, axis, mask):
    return lax.ppermute(x, axis, [(i, i ^ mask) for i in range(lax.axis_size(axis))])


def of_all_groups(x):
    return [x] + [swapped(x, "dp", mask) for mask in range(1, lax.axis_size("dp"))]


def body(activations, cotangent, weight, residual, step_size, kept_blocks):
    rows, cols = weight.shape
    groups = lax.axis_size("dp")
    owned_count = (rows // BLK) * (cols // BLK) // groups
    kept = kept_blocks.reshape(-1)
    me = lax.axis_index("dp").astype(jnp.int32).reshape(1)
    here = lax.axis_index("tensor").astype(jnp.int32).reshape(1)
    pair = lax.axis_size("tensor") == 2
    if pair:
        act = swapped(activations, "tensor", 1)
        away, acts_t, own, zeros, cot, kept_res = input_grad_partials(
            here, me, kept, cotangent, weight, residual[0], owned_count, activations
        )
        parts = [own, swapped(away, "tensor", 1)]
    else:
        act = lax.all_gather(activations, "tensor", axis=0, tiled=True)
        acts_t = None
        own, zeros, cot, kept_res = input_grad_partials(
            here, me, kept, cotangent, weight, residual[0], owned_count, None
        )
        summed = lax.psum_scatter(own, "tensor", scatter_dimension=0, tiled=True)
        parts = []
    acts_t, blocks = kept_blocks_of(kept, step_size, acts_t, act, cot, kept_res)
    all_blocks = of_all_groups(blocks)
    rounded = residual_of(step_size, acts_t, cot, residual[0])
    *grads, owned, residual_out = finish(me, kept, parts, all_blocks, zeros, rounded)
    input_grad = grads[0] if pair else summed.astype(jnp.bfloat16)
    return (input_grad, residual_out[None], owned.reshape(1, 1, 1, owned_count, BLK, BLK))


def solution(mesh):
    in_specs = (
        P(("dp", "tensor"), "fsdp"),
        P("dp", "tensor"),
        P("fsdp", "tensor"),
        P("dp", "fsdp", "tensor"),
        P(),
        P("dp", "fsdp", "tensor", None),
    )
    out_specs = (
        P(("dp", "tensor"), "fsdp"),
        P("dp", "fsdp", "tensor"),
        P("dp", "fsdp", "tensor", None, None, None),
    )
    return jax.shard_map(body, mesh=mesh, in_specs=in_specs, out_specs=out_specs, check_vma=False)
```

```python
import functools

import jax
import jax.numpy as jnp
from jax import lax
from jax.experimental import pallas as pl
from jax.experimental.pallas import tpu as pltpu
from jax.sharding import PartitionSpec as P

BLK = 128
MIB = 1024 * 1024
LABEL_ROWS = 16
RADIX = 16


def cost(flops, nbytes):
    return pl.CostEstimate(flops=flops, bytes_accessed=nbytes, transcendentals=0)


def params(mib=62):
    return pltpu.CompilerParams(vmem_limit_bytes=mib * MIB)


def dot_nt(a, b):
    return lax.dot_general(a, b, (((1,), (1,)), ((), ())), preferred_element_type=jnp.float32)


def dot_nn(a, b):
    return lax.dot_general(a, b, (((1,), (0,)), ((), ())), preferred_element_type=jnp.float32)


def hidden_chunks(cols):
    sizes = []
    for size in (512, 1024, 2048, 4608):
        if cols > sum(sizes):
            sizes.append(min(size, cols - sum(sizes)))
    while sum(sizes) < cols:
        sizes.append(min(4608, cols - sum(sizes)))
    return sizes


def smem():
    return pl.BlockSpec(memory_space=pltpu.SMEM)


def vmem():
    return pl.BlockSpec(memory_space=pltpu.VMEM)


def hbm():
    return pl.BlockSpec(memory_space=pltpu.HBM)


def anywhere():
    return pl.BlockSpec(memory_space=pl.ANY)


def in_hbm(x):
    return pltpu.with_memory_space_constraint(x, pltpu.HBM)


def in_vmem(x):
    return pltpu.with_memory_space_constraint(x, pltpu.VMEM)


def cot_copies(here_ref, split, cot_ref, buf_ref, sems):
    if not split:
        return [pltpu.make_async_copy(cot_ref, buf_ref, sems.at[0])]
    half = buf_ref.shape[0] // 2
    copies = []
    for i, at in enumerate((here_ref[0], 1 - here_ref[0])):
        rows = pl.ds(pl.multiple_of(at * half, half), half)
        copies.append(pltpu.make_async_copy(cot_ref.at[rows], buf_ref.at[pl.ds(i * half, half)], sems.at[i]))
    return copies


def input_grad_kernel(split, sizes, zero_copies, here_ref, _, kept_ref, cot_ref, w_ref, res_ref, *refs):
    if split:
        acts_ref, away_ref, acts_t_ref, *refs = refs
    own_ref, owned_ref, kept_cot_ref, kept_res_ref, *refs = refs
    acc_ref, cot_buf, w_buf, zero_ref, cot_sem, w_sem, zero_sem, kept_cot_sem, kept_res_sem, own_sem, *refs = refs
    zero_rows = zero_ref.shape[0]
    rows, hidden = w_ref.shape
    width = min(256, rows)
    last = len(sizes) - 1
    keep = kept_cot_ref.shape[0]
    half = own_ref.shape[0]

    def loads(i):
        part = pl.ds(sum(sizes[:i]), sizes[i])
        return cot_copies(here_ref, split, cot_ref.at[:, part], cot_buf.at[:, part], cot_sem.at[i]) + [
            pltpu.make_async_copy(w_ref.at[:, part], w_buf.at[:, part], w_sem.at[i])
        ]

    def start(i):
        if i <= last:
            for copy in loads(i):
                copy.start()

    def zero_copy(i):
        return pltpu.make_async_copy(zero_ref, owned_ref.at[pl.ds(i * zero_rows, zero_rows)], zero_sem.at[i])

    def kept_copies(k):
        col_blocks = hidden // BLK
        row = pl.ds(pl.multiple_of(kept_ref[k] // col_blocks * BLK, BLK), BLK)
        col = pl.ds(pl.multiple_of(kept_ref[k] % col_blocks * BLK, BLK), BLK)
        return (
            pltpu.make_async_copy(cot_buf.at[:, col], kept_cot_ref.at[k], kept_cot_sem.at[k]),
            pltpu.make_async_copy(res_ref.at[row, col], kept_res_ref.at[k], kept_res_sem.at[k]),
        )

    if split:
        acts_buf, acts_t_buf, away_buf, acts_sem, acts_t_sem, away_sem = refs
        acts_copy = pltpu.make_async_copy(acts_ref, acts_buf, acts_sem)
        acts_t_copy = pltpu.make_async_copy(acts_t_buf, acts_t_ref.at[:, pl.ds(0, half)], acts_t_sem)
        acts_copy.start()
    start(0)
    start(1)
    zero_ref[...] = jnp.zeros_like(zero_ref)
    if split:
        acts_copy.wait()
        acts_t_buf[...] = acts_buf[...].T
        acts_t_copy.start()
    outputs = []
    for i in range(last + 1):
        for copy in loads(i):
            copy.wait()
        start(i + 2)
        if i == last:
            for z in range(zero_copies):
                zero_copy(z).start()
            for k in range(keep):
                for copy in kept_copies(k):
                    copy.start()
        part = slice(sum(sizes[:i]), sum(sizes[: i + 1]))
        for n, at in enumerate(range(0, rows, width)):
            cols = slice(at, at + width)
            total = dot_nt(cot_buf[:, part], w_buf[cols, part])
            if i > 0:
                total += acc_ref[:, cols]
            if i < last or not split:
                acc_ref[:, cols] = total
            else:
                acc_ref[:half, cols] = total[:half]
                away_buf[:, cols] = total[half:].astype(jnp.bfloat16)
                outputs.append(pltpu.make_async_copy(away_buf.at[:, cols], away_ref.at[:, cols], away_sem.at[n]))
                outputs[-1].start()
            if i == last:
                outputs.append(pltpu.make_async_copy(acc_ref.at[:half, cols], own_ref.at[:, cols], own_sem.at[n]))
                outputs[-1].start()
    if split:
        acts_t_copy.wait()
    for z in range(zero_copies):
        zero_copy(z).wait()
    for k in range(keep):
        for copy in kept_copies(k):
            copy.wait()
    for copy in outputs:
        copy.wait()


def input_grad_partials(here, me, kept, cot, weight, residual, owned_count, acts):
    split = acts is not None
    tokens, cols = cot.shape
    rows = weight.shape[0]
    sizes = hidden_chunks(cols)
    keep = kept.shape[0]
    own_rows = tokens // 2 if split else tokens
    zero_rows = min(16, owned_count)
    zero_copies = owned_count // zero_rows
    out_shape = [
        pltpu.VMEM((own_rows, rows), jnp.float32) if split else jax.ShapeDtypeStruct((own_rows, rows), jnp.float32),
        pltpu.HBM((owned_count, BLK, BLK), jnp.float32),
        pltpu.VMEM((keep, tokens, BLK), jnp.bfloat16),
        pltpu.VMEM((keep, BLK, BLK), jnp.bfloat16),
    ]
    out_specs = [vmem() if split else anywhere(), hbm(), vmem(), vmem()]
    scratch = [
        pltpu.VMEM((tokens, rows), jnp.float32),
        pltpu.VMEM((tokens, cols), jnp.bfloat16),
        pltpu.VMEM((rows, cols), jnp.bfloat16),
        pltpu.VMEM((zero_rows, BLK, BLK), jnp.float32),
        pltpu.SemaphoreType.DMA((len(sizes), 2)),
        pltpu.SemaphoreType.DMA((len(sizes),)),
        pltpu.SemaphoreType.DMA((zero_copies,)),
        pltpu.SemaphoreType.DMA((keep,)),
        pltpu.SemaphoreType.DMA((keep,)),
        pltpu.SemaphoreType.DMA((4,)),
    ]
    if split:
        out_shape = [
            jax.ShapeDtypeStruct((own_rows, rows), jnp.bfloat16),
            pltpu.VMEM((rows, tokens), jnp.bfloat16),
        ] + out_shape
        out_specs = [anywhere(), vmem()] + out_specs
        scratch += [
            pltpu.VMEM(acts.shape, jnp.bfloat16),
            pltpu.VMEM((rows, own_rows), jnp.bfloat16),
            pltpu.VMEM((own_rows, rows), jnp.bfloat16),
            pltpu.SemaphoreType.DMA,
            pltpu.SemaphoreType.DMA,
            pltpu.SemaphoreType.DMA((4,)),
        ]
    return pl.pallas_call(
        functools.partial(input_grad_kernel, split, sizes, zero_copies),
        out_shape=out_shape,
        in_specs=[smem()] * 3 + [hbm()] * (3 + split),
        out_specs=out_specs,
        scratch_shapes=scratch,
        compiler_params=params(53),
        cost_estimate=cost(2 * tokens * rows * cols, 2 * cols * (tokens + rows) + 4 * owned_count * BLK * BLK),
        name="input_grad_partials",
    )(here, me, kept, in_hbm(cot), in_hbm(weight), in_hbm(residual), *([in_hbm(acts)] if split else []))


def kept_kernel(pair, col_blocks, kept_ref, step_ref, *refs):
    if pair:
        _, *refs = refs
    act_ref, cot_ref, res_ref, acts_t_ref, out_ref = refs
    keep = cot_ref.shape[0]
    acts_t_ref[:, acts_t_ref.shape[1] - act_ref.shape[0] :] = act_ref[...].T
    for k in range(keep):
        row = pl.ds(pl.multiple_of(kept_ref[k] // col_blocks * BLK, BLK), BLK)
        gradient = dot_nn(acts_t_ref[row, :], cot_ref[k])
        out_ref[k * BLK : (k + 1) * BLK, :] = (res_ref[k].astype(jnp.float32) + step_ref[0] * gradient).astype(
            jnp.bfloat16
        )
    lane = lax.broadcasted_iota(jnp.int32, (LABEL_ROWS, BLK), 1) % keep
    low = lax.broadcasted_iota(jnp.int32, (LABEL_ROWS, BLK), 0) % 2 == 1
    label = jnp.zeros((LABEL_ROWS, BLK), jnp.int32)
    for k in range(keep):
        digit = jnp.where(low, kept_ref[k] % RADIX, kept_ref[k] // RADIX)
        label = jnp.where(lane == k, digit, label)
    out_ref[keep * BLK :, :] = label.astype(jnp.float32).astype(jnp.bfloat16)


def kept_blocks_of(kept, step_size, acts_t, act, kept_cot, kept_res, col_blocks):
    rows = act.shape[1]
    keep, tokens = kept_cot.shape[:2]
    pair = acts_t is not None
    return pl.pallas_call(
        functools.partial(kept_kernel, pair, col_blocks),
        out_shape=[
            pltpu.VMEM((rows, tokens), jnp.bfloat16),
            jax.ShapeDtypeStruct((keep * BLK + LABEL_ROWS, BLK), jnp.bfloat16),
        ],
        in_specs=[smem()] * 2 + [vmem()] * (3 + pair),
        out_specs=[vmem(), vmem()],
        input_output_aliases={2: 0} if pair else {},
        compiler_params=params(4),
        cost_estimate=cost(2 * tokens * BLK * BLK * keep, 4 * tokens * rows + 2 * keep * tokens * BLK),
        name="kept_blocks",
    )(kept, step_size, *([in_vmem(acts_t)] if pair else []), act, in_vmem(kept_cot), in_vmem(kept_res))


def residual_kernel(split, here_ref, step_ref, acts_t_ref, cot_ref, res_ref, out_ref, cot_buf, res_buf, *sems):
    cot_sem, res_sem, out_sem = sems
    step = step_ref[0]
    chunks, _, chunk = cot_buf.shape
    width = min(256, chunk)

    def columns(j):
        return pl.ds(pl.multiple_of(j * chunk, chunk), chunk)

    def loads(j):
        return cot_copies(here_ref, split, cot_ref.at[:, columns(j)], cot_buf.at[j], cot_sem.at[j]) + [
            pltpu.make_async_copy(res_ref.at[:, columns(j)], res_buf.at[j], res_sem.at[j])
        ]

    def store(j):
        return pltpu.make_async_copy(res_buf.at[j], out_ref.at[:, columns(j)], out_sem.at[j])

    def start(j):
        @pl.when(j < chunks)
        def _():
            for copy in loads(j):
                copy.start()

    start(0)
    start(1)

    @pl.loop(0, chunks)
    def _(j):
        for copy in loads(j):
            copy.wait()
        start(j + 2)
        for at in range(0, chunk, width):
            part = slice(at, at + width)
            gradient = dot_nn(acts_t_ref[...], cot_buf[j, :, part])
            res_buf[j, :, part] = (res_buf[j, :, part].astype(jnp.float32) + step * gradient).astype(jnp.bfloat16)
        store(j).start()

    for j in range(chunks):
        store(j).wait()


def residual_of(here, step_size, acts_t, cot, residual, split):
    tokens, cols = cot.shape
    rows = residual.shape[0]
    chunk = min(1024, cols)
    chunks = cols // chunk
    sem = pltpu.SemaphoreType.DMA((chunks,))
    return pl.pallas_call(
        functools.partial(residual_kernel, split),
        out_shape=pltpu.HBM((rows, cols), jnp.bfloat16),
        in_specs=[smem()] * 2 + [vmem(), hbm(), hbm()],
        out_specs=hbm(),
        scratch_shapes=[
            pltpu.VMEM((chunks, tokens, chunk), jnp.bfloat16),
            pltpu.VMEM((chunks, rows, chunk), jnp.bfloat16),
            pltpu.SemaphoreType.DMA((chunks, 2)),
            sem,
            sem,
        ],
        compiler_params=params(38),
        cost_estimate=cost(2 * tokens * rows * cols, 2 * tokens * (rows + cols) + 4 * rows * cols),
        name="residual_out",
    )(here, step_size, in_vmem(acts_t), in_hbm(cot), in_hbm(residual))


def finish_kernel(groups, keep, pair, col_blocks, me_ref, kept_ref, *refs):
    if pair:
        own_ref, arrived_ref, *refs = refs
    block_refs = refs[:groups]
    refs = refs[groups + 2 :]
    if pair:
        grad_ref, *refs = refs
    out_ref, res_ref, sum_ref, table_ref, scalar_ref, zero_ref, sem, table_sem, zero_sem, *refs = refs
    total = groups * keep
    me = me_ref[0]

    zero_ref[...] = jnp.zeros_like(zero_ref)
    zero_copies = []
    for k in range(keep):
        at = pl.multiple_of(kept_ref[k] // col_blocks * BLK, BLK)
        col = pl.multiple_of(kept_ref[k] % col_blocks * BLK, BLK)
        zero_copies.append(
            pltpu.make_async_copy(zero_ref, res_ref.at[pl.ds(at, BLK), pl.ds(col, BLK)], zero_sem.at[k])
        )
        zero_copies[k].start()

    row = lax.broadcasted_iota(jnp.int32, (total, BLK), 0)
    lane = lax.broadcasted_iota(jnp.int32, (total, BLK), 1)
    numbers = jnp.full((total, BLK), -1, jnp.int32)
    for g, block_ref in enumerate(block_refs):
        digits = block_ref[keep * BLK :, :].astype(jnp.float32).astype(jnp.int32)
        numbers = jnp.where(lane // keep == g, digits[0:1, :] * RADIX + digits[1:2, :], numbers)
    numbers = numbers.astype(jnp.float32)
    number = jnp.sum(jnp.where(lane == row, numbers, 0.0), axis=1, keepdims=True)
    first = jnp.min(jnp.where(numbers == number, lane.astype(jnp.float32), float(BLK)), axis=1, keepdims=True)
    number = jnp.broadcast_to(number, (total, BLK)).astype(jnp.int32)
    first = jnp.broadcast_to(first, (total, BLK)).astype(jnp.int32)
    table_ref[...] = jnp.where(lane == 0, jnp.where(number % groups == me, first, -1), number // groups)
    table = pltpu.make_async_copy(table_ref, scalar_ref, table_sem)
    table.start()

    grad_copies = []
    if pair:
        grad_buf, grad_sem = refs
        size = grad_buf.shape[0] // grad_sem.shape[0]
        for c in range(grad_sem.shape[0]):
            part = slice(c * size, (c + 1) * size)
            grad_buf[part, :] = (own_ref[part, :] + arrived_ref[part, :].astype(jnp.float32)).astype(jnp.bfloat16)
            grad_copies.append(pltpu.make_async_copy(grad_buf.at[part, :], grad_ref.at[part, :], grad_sem.at[c]))
            grad_copies[c].start()

    table.wait()

    def copy(i):
        return pltpu.make_async_copy(sum_ref.at[i], out_ref.at[scalar_ref[i, 1]], sem.at[i])

    def block(i):
        at = i % keep * BLK
        return block_refs[i // keep][at : at + BLK, :].astype(jnp.float32)

    for i in range(total):
        slot = scalar_ref[i, 0]

        @pl.when(slot == i)
        def _(i=i):
            sum_ref[i] = block(i)

        if i >= keep:

            @pl.when((slot >= 0) & (slot < i))
            def _(i=i, slot=slot):
                sum_ref[slot] += block(i)

    for i in range(total):

        @pl.when(scalar_ref[i, 0] == i)
        def _(i=i):
            copy(i).start()

    for done in zero_copies + grad_copies:
        done.wait()
    for i in range(total):

        @pl.when(scalar_ref[i, 0] == i)
        def _(i=i):
            copy(i).wait()


def finish(me, kept, parts, blocks, zeros, residual):
    groups = len(blocks)
    keep = kept.shape[0]
    out_shape = [pltpu.HBM(a.shape, a.dtype) for a in (zeros, residual)]
    out_specs = [hbm(), hbm()]
    scratch = [
        pltpu.VMEM((groups * keep, BLK, BLK), jnp.float32),
        pltpu.VMEM((groups * keep, BLK), jnp.int32),
        pltpu.SMEM((groups * keep, BLK), jnp.int32),
        pltpu.VMEM((BLK, BLK), jnp.bfloat16),
        pltpu.SemaphoreType.DMA((groups * keep,)),
        pltpu.SemaphoreType.DMA,
        pltpu.SemaphoreType.DMA((keep,)),
    ]
    if parts:
        out_shape.insert(0, pltpu.HBM(parts[0].shape, jnp.bfloat16))
        out_specs.insert(0, hbm())
        scratch += [pltpu.VMEM(parts[0].shape, jnp.bfloat16), pltpu.SemaphoreType.DMA((4,))]
        parts = [in_vmem(parts[0]), parts[1]]
    first = 2 + len(parts) + groups
    return pl.pallas_call(
        functools.partial(finish_kernel, groups, keep, bool(parts), residual.shape[1] // BLK),
        out_shape=out_shape,
        in_specs=[smem(), smem()] + [vmem()] * (len(parts) + groups) + [hbm(), hbm()],
        out_specs=out_specs,
        scratch_shapes=scratch,
        input_output_aliases={first: len(out_shape) - 2, first + 1: len(out_shape) - 1},
        compiler_params=params(10),
        cost_estimate=cost(groups * keep * BLK * BLK, groups * keep * BLK * BLK * 8),
        name="finish",
    )(me, kept, *parts, *blocks, in_hbm(zeros), in_hbm(residual))


def swapped(x, axis, mask):
    return lax.ppermute(x, axis, [(i, i ^ mask) for i in range(lax.axis_size(axis))])


def of_all_groups(x):
    return [x] + [swapped(x, "dp", mask) for mask in range(1, lax.axis_size("dp"))]


def body(activations, cotangent, weight, residual, step_size, kept_blocks):
    rows, cols = weight.shape
    groups = lax.axis_size("dp")
    owned_count = (rows // BLK) * (cols // BLK) // groups
    kept = kept_blocks.reshape(-1)
    me = lax.axis_index("dp").astype(jnp.int32).reshape(1)
    here = lax.axis_index("tensor").astype(jnp.int32).reshape(1)
    pair = lax.axis_size("tensor") == 2
    if pair:
        act = swapped(activations, "tensor", 1)
        away, acts_t, own, zeros, kept_cot, kept_res = input_grad_partials(
            here, me, kept, cotangent, weight, residual[0], owned_count, activations
        )
        parts = [own, swapped(away, "tensor", 1)]
    else:
        act = lax.all_gather(activations, "tensor", axis=0, tiled=True)
        acts_t = None
        own, zeros, kept_cot, kept_res = input_grad_partials(
            here, me, kept, cotangent, weight, residual[0], owned_count, None
        )
        summed = lax.psum_scatter(own, "tensor", scatter_dimension=0, tiled=True)
        parts = []
    acts_t, blocks = kept_blocks_of(kept, step_size, acts_t, act, kept_cot, kept_res, cols // BLK)
    all_blocks = of_all_groups(blocks)
    rounded = residual_of(here, step_size, acts_t, cotangent, residual[0], pair)
    *grads, owned, residual_out = finish(me, kept, parts, all_blocks, zeros, rounded)
    input_grad = grads[0] if pair else summed.astype(jnp.bfloat16)
    return (input_grad, residual_out[None], owned.reshape(1, 1, 1, owned_count, BLK, BLK))


def solution(mesh):
    in_specs = (
        P(("dp", "tensor"), "fsdp"),
        P("dp", "tensor"),
        P("fsdp", "tensor"),
        P("dp", "fsdp", "tensor"),
        P(),
        P("dp", "fsdp", "tensor", None),
    )
    out_specs = (
        P(("dp", "tensor"), "fsdp"),
        P("dp", "fsdp", "tensor"),
        P("dp", "fsdp", "tensor", None, None, None),
    )
    return jax.shard_map(body, mesh=mesh, in_specs=in_specs, out_specs=out_specs, check_vma=False)
```

```python
import functools

import jax
import jax.numpy as jnp
from jax import lax
from jax.experimental import pallas as pl
from jax.experimental.pallas import tpu as pltpu
from jax.sharding import PartitionSpec as P

BLK = 128
MIB = 1024 * 1024
LABEL_ROWS = 16
RADIX = 16


def cost(flops, nbytes):
    return pl.CostEstimate(flops=flops, bytes_accessed=nbytes, transcendentals=0)


def params(mib=62):
    return pltpu.CompilerParams(vmem_limit_bytes=mib * MIB)


def dot_nt(a, b):
    return lax.dot_general(a, b, (((1,), (1,)), ((), ())), preferred_element_type=jnp.float32)


def dot_nn(a, b):
    return lax.dot_general(a, b, (((1,), (0,)), ((), ())), preferred_element_type=jnp.float32)


def chunking(cols):
    if cols < 2048:
        return cols // 2, 0, cols // 2
    return 512, cols // 1024 - 1, 1024


def smem():
    return pl.BlockSpec(memory_space=pltpu.SMEM)


def vmem():
    return pl.BlockSpec(memory_space=pltpu.VMEM)


def hbm():
    return pl.BlockSpec(memory_space=pltpu.HBM)


def anywhere():
    return pl.BlockSpec(memory_space=pl.ANY)


def in_hbm(x):
    return pltpu.with_memory_space_constraint(x, pltpu.HBM)


def in_vmem(x):
    return pltpu.with_memory_space_constraint(x, pltpu.VMEM)


def cot_copies(here_ref, split, cot_ref, buf_ref, sems):
    if not split:
        return [pltpu.make_async_copy(cot_ref, buf_ref, sems.at[0])]
    half = buf_ref.shape[0] // 2
    copies = []
    for i, at in enumerate((here_ref[0], 1 - here_ref[0])):
        rows = pl.ds(pl.multiple_of(at * half, half), half)
        copies.append(pltpu.make_async_copy(cot_ref.at[rows], buf_ref.at[pl.ds(i * half, half)], sems.at[i]))
    return copies


def input_grad_kernel(split, zero_copies, here_ref, _, kept_ref, cot_ref, w_ref, res_ref, *refs):
    if split:
        acts_ref, away_ref, acts_t_ref, *refs = refs
    own_ref, owned_ref, kept_cot_ref, kept_res_ref, *refs = refs
    acc_ref, cot_head, w_head, cot_body, w_body, cot_tail, w_tail, zero_ref, *refs = refs
    cot_sem, w_sem, zero_sem, kept_cot_sem, kept_res_sem, own_sem, *refs = refs
    zero_rows = zero_ref.shape[0]
    rows, hidden = w_ref.shape
    width = min(256, rows)
    keep = kept_cot_ref.shape[0]
    half = own_ref.shape[0]
    head, chunks, chunk = chunking(hidden)

    def loads(at, size, cot_buf, w_buf, i):
        part = pl.ds(at, size)
        return cot_copies(here_ref, split, cot_ref.at[:, part], cot_buf, cot_sem.at[i]) + [
            pltpu.make_async_copy(w_ref.at[:, part], w_buf, w_sem.at[i])
        ]

    def head_loads():
        return loads(0, head, cot_head, w_head, 0)

    def tail_loads():
        return loads(hidden - head, head, cot_tail, w_tail, 1)

    def body_loads(j):
        return loads(pl.multiple_of(head + j * chunk, BLK), chunk, cot_body.at[j], w_body.at[j], 2 + j)

    def start(copies):
        for copy in copies:
            copy.start()

    def wait(copies):
        for copy in copies:
            copy.wait()

    def side_copies():
        copies = []
        for z in range(zero_copies):
            part = pl.ds(z * zero_rows, zero_rows)
            copies.append(pltpu.make_async_copy(zero_ref, owned_ref.at[part], zero_sem.at[z]))
        for k in range(keep):
            col_blocks = hidden // BLK
            row = pl.ds(pl.multiple_of(kept_ref[k] // col_blocks * BLK, BLK), BLK)
            col = pl.ds(pl.multiple_of(kept_ref[k] % col_blocks * BLK, BLK), BLK)
            copies += cot_copies(here_ref, split, cot_ref.at[:, col], kept_cot_ref.at[k], kept_cot_sem.at[k])
            copies.append(pltpu.make_async_copy(res_ref.at[row, col], kept_res_ref.at[k], kept_res_sem.at[k]))
        return copies

    if split:
        acts_buf, acts_t_buf, away_buf, acts_sem, acts_t_sem, away_sem = refs
        acts_copy = pltpu.make_async_copy(acts_ref, acts_buf, acts_sem)
        acts_t_copy = pltpu.make_async_copy(acts_t_buf, acts_t_ref.at[:, pl.ds(0, half)], acts_t_sem)
        acts_copy.start()
    start(head_loads())
    start(body_loads(0) if chunks else tail_loads())
    zero_ref[...] = jnp.zeros_like(zero_ref)
    if split:
        acts_copy.wait()
        acts_t_buf[...] = acts_buf[...].T
        acts_t_copy.start()
    wait(head_loads())
    if chunks:
        start(body_loads(1))
    for at in range(0, rows, width):
        cols = slice(at, at + width)
        acc_ref[:, cols] = dot_nt(cot_head[...], w_head[cols, :])

    if chunks:

        @pl.loop(0, chunks)
        def _(j):
            wait(body_loads(j))

            @pl.when(j + 2 < chunks)
            def _():
                start(body_loads(j + 2))

            @pl.when(j + 2 == chunks)
            def _():
                start(tail_loads())
                start(side_copies())

            for at in range(0, rows, width):
                cols = slice(at, at + width)
                acc_ref[:, cols] += dot_nt(cot_body[j], w_body[j, cols, :])

    else:
        start(side_copies())
    wait(tail_loads())
    outputs = []
    for n, at in enumerate(range(0, rows, width)):
        cols = slice(at, at + width)
        total = acc_ref[:, cols] + dot_nt(cot_tail[...], w_tail[cols, :])
        acc_ref[:half, cols] = total[:half]
        outputs.append(pltpu.make_async_copy(acc_ref.at[:half, cols], own_ref.at[:, cols], own_sem.at[n]))
        if split:
            away_buf[:, cols] = total[half:].astype(jnp.bfloat16)
            outputs.append(pltpu.make_async_copy(away_buf.at[:, cols], away_ref.at[:, cols], away_sem.at[n]))
    start(outputs)
    if split:
        acts_t_copy.wait()
    wait(side_copies())
    wait(outputs)


def input_grad_partials(here, me, kept, cot, weight, residual, owned_count, acts):
    split = acts is not None
    tokens, cols = cot.shape
    rows = weight.shape[0]
    head, chunks, chunk = chunking(cols)
    keep = kept.shape[0]
    own_rows = tokens // 2 if split else tokens
    zero_rows = min(16, owned_count)
    zero_copies = owned_count // zero_rows
    out_shape = [
        pltpu.VMEM((own_rows, rows), jnp.float32) if split else jax.ShapeDtypeStruct((own_rows, rows), jnp.float32),
        pltpu.HBM((owned_count, BLK, BLK), jnp.float32),
        pltpu.VMEM((keep, tokens, BLK), jnp.bfloat16),
        pltpu.VMEM((keep, BLK, BLK), jnp.bfloat16),
    ]
    out_specs = [vmem() if split else anywhere(), hbm(), vmem(), vmem()]
    scratch = [
        pltpu.VMEM((tokens, rows), jnp.float32),
        pltpu.VMEM((tokens, head), jnp.bfloat16),
        pltpu.VMEM((rows, head), jnp.bfloat16),
        pltpu.VMEM((max(chunks, 1), tokens, chunk), jnp.bfloat16),
        pltpu.VMEM((max(chunks, 1), rows, chunk), jnp.bfloat16),
        pltpu.VMEM((tokens, head), jnp.bfloat16),
        pltpu.VMEM((rows, head), jnp.bfloat16),
        pltpu.VMEM((zero_rows, BLK, BLK), jnp.float32),
        pltpu.SemaphoreType.DMA((chunks + 2, 2)),
        pltpu.SemaphoreType.DMA((chunks + 2,)),
        pltpu.SemaphoreType.DMA((zero_copies,)),
        pltpu.SemaphoreType.DMA((keep, 2)),
        pltpu.SemaphoreType.DMA((keep,)),
        pltpu.SemaphoreType.DMA((4,)),
    ]
    if split:
        out_shape = [
            jax.ShapeDtypeStruct((own_rows, rows), jnp.bfloat16),
            pltpu.VMEM((rows, tokens), jnp.bfloat16),
        ] + out_shape
        out_specs = [anywhere(), vmem()] + out_specs
        scratch += [
            pltpu.VMEM(acts.shape, jnp.bfloat16),
            pltpu.VMEM((rows, own_rows), jnp.bfloat16),
            pltpu.VMEM((own_rows, rows), jnp.bfloat16),
            pltpu.SemaphoreType.DMA,
            pltpu.SemaphoreType.DMA,
            pltpu.SemaphoreType.DMA((4,)),
        ]
    return pl.pallas_call(
        functools.partial(input_grad_kernel, split, zero_copies),
        out_shape=out_shape,
        in_specs=[smem()] * 3 + [hbm()] * (3 + split),
        out_specs=out_specs,
        scratch_shapes=scratch,
        compiler_params=params(46),
        cost_estimate=cost(2 * tokens * rows * cols, 2 * cols * (tokens + rows) + 4 * owned_count * BLK * BLK),
        name="input_grad_partials",
    )(here, me, kept, in_hbm(cot), in_hbm(weight), in_hbm(residual), *([in_hbm(acts)] if split else []))


def kept_kernel(pair, col_blocks, kept_ref, step_ref, *refs):
    if pair:
        _, *refs = refs
    act_ref, cot_ref, res_ref, acts_t_ref, out_ref = refs
    keep = cot_ref.shape[0]
    acts_t_ref[:, acts_t_ref.shape[1] - act_ref.shape[0] :] = act_ref[...].T
    for k in range(keep):
        row = pl.ds(pl.multiple_of(kept_ref[k] // col_blocks * BLK, BLK), BLK)
        gradient = dot_nn(acts_t_ref[row, :], cot_ref[k])
        out_ref[k * BLK : (k + 1) * BLK, :] = (res_ref[k].astype(jnp.float32) + step_ref[0] * gradient).astype(
            jnp.bfloat16
        )
    lane = lax.broadcasted_iota(jnp.int32, (LABEL_ROWS, BLK), 1) % keep
    low = lax.broadcasted_iota(jnp.int32, (LABEL_ROWS, BLK), 0) % 2 == 1
    label = jnp.zeros((LABEL_ROWS, BLK), jnp.int32)
    for k in range(keep):
        digit = jnp.where(low, kept_ref[k] % RADIX, kept_ref[k] // RADIX)
        label = jnp.where(lane == k, digit, label)
    out_ref[keep * BLK :, :] = label.astype(jnp.float32).astype(jnp.bfloat16)


def kept_blocks_of(kept, step_size, acts_t, act, kept_cot, kept_res, col_blocks):
    rows = act.shape[1]
    keep, tokens = kept_cot.shape[:2]
    pair = acts_t is not None
    return pl.pallas_call(
        functools.partial(kept_kernel, pair, col_blocks),
        out_shape=[
            pltpu.VMEM((rows, tokens), jnp.bfloat16),
            jax.ShapeDtypeStruct((keep * BLK + LABEL_ROWS, BLK), jnp.bfloat16),
        ],
        in_specs=[smem()] * 2 + [vmem()] * (3 + pair),
        out_specs=[vmem(), vmem()],
        input_output_aliases={2: 0} if pair else {},
        compiler_params=params(4),
        cost_estimate=cost(2 * tokens * BLK * BLK * keep, 4 * tokens * rows + 2 * keep * tokens * BLK),
        name="kept_blocks",
    )(kept, step_size, *([in_vmem(acts_t)] if pair else []), act, in_vmem(kept_cot), in_vmem(kept_res))


def residual_kernel(split, here_ref, step_ref, acts_t_ref, cot_ref, res_ref, out_ref, *refs):
    cot_head, res_head, cot_body, res_body, cot_tail, res_tail, cot_sem, res_sem, out_sem = refs
    step = step_ref[0]
    hidden = cot_ref.shape[1]
    head, chunks, chunk = chunking(hidden)

    def loads(at, size, cot_buf, res_buf, i):
        part = pl.ds(at, size)
        return cot_copies(here_ref, split, cot_ref.at[:, part], cot_buf, cot_sem.at[i]) + [
            pltpu.make_async_copy(res_ref.at[:, part], res_buf, res_sem.at[i])
        ]

    def head_loads():
        return loads(0, head, cot_head, res_head, 0)

    def tail_loads():
        return loads(hidden - head, head, cot_tail, res_tail, 1)

    def body_loads(j):
        return loads(pl.multiple_of(head + j * chunk, BLK), chunk, cot_body.at[j], res_body.at[j], 2 + j)

    def store(at, size, res_buf, i):
        return pltpu.make_async_copy(res_buf, out_ref.at[:, pl.ds(at, size)], out_sem.at[i])

    def head_store():
        return store(0, head, res_head, 0)

    def tail_store():
        return store(hidden - head, head, res_tail, 1)

    def body_store(j):
        return store(pl.multiple_of(head + j * chunk, BLK), chunk, res_body.at[j], 2 + j)

    def start(copies):
        for copy in copies:
            copy.start()

    def wait(copies):
        for copy in copies:
            copy.wait()

    def work(cot_buf, res_buf):
        size = cot_buf.shape[1]
        width = min(256, size)
        for at in range(0, size, width):
            part = slice(at, at + width)
            gradient = dot_nn(acts_t_ref[...], cot_buf[:, part])
            res_buf[:, part] = (res_buf[:, part].astype(jnp.float32) + step * gradient).astype(jnp.bfloat16)

    start(head_loads())
    start(body_loads(0) if chunks else tail_loads())
    wait(head_loads())
    if chunks:
        start(body_loads(1))
    work(cot_head, res_head)
    head_store().start()

    if chunks:

        @pl.loop(0, chunks)
        def _(j):
            wait(body_loads(j))

            @pl.when(j + 2 < chunks)
            def _():
                start(body_loads(j + 2))

            @pl.when(j + 2 == chunks)
            def _():
                start(tail_loads())

            work(cot_body.at[j], res_body.at[j])
            body_store(j).start()

    wait(tail_loads())
    work(cot_tail, res_tail)
    tail_store().start()
    head_store().wait()
    for j in range(chunks):
        body_store(j).wait()
    tail_store().wait()


def residual_of(here, step_size, acts_t, cot, residual, split):
    tokens, cols = cot.shape
    rows = residual.shape[0]
    head, chunks, chunk = chunking(cols)
    sem = pltpu.SemaphoreType.DMA((chunks + 2,))
    return pl.pallas_call(
        functools.partial(residual_kernel, split),
        out_shape=pltpu.HBM((rows, cols), jnp.bfloat16),
        in_specs=[smem()] * 2 + [vmem(), hbm(), hbm()],
        out_specs=hbm(),
        scratch_shapes=[
            pltpu.VMEM((tokens, head), jnp.bfloat16),
            pltpu.VMEM((rows, head), jnp.bfloat16),
            pltpu.VMEM((max(chunks, 1), tokens, chunk), jnp.bfloat16),
            pltpu.VMEM((max(chunks, 1), rows, chunk), jnp.bfloat16),
            pltpu.VMEM((tokens, head), jnp.bfloat16),
            pltpu.VMEM((rows, head), jnp.bfloat16),
            pltpu.SemaphoreType.DMA((chunks + 2, 2)),
            sem,
            sem,
        ],
        compiler_params=params(38),
        cost_estimate=cost(2 * tokens * rows * cols, 2 * tokens * (rows + cols) + 4 * rows * cols),
        name="residual_out",
    )(here, step_size, in_vmem(acts_t), in_hbm(cot), in_hbm(residual))


def finish_kernel(groups, keep, pair, col_blocks, me_ref, kept_ref, *refs):
    if pair:
        own_ref, arrived_ref, *refs = refs
    block_refs = refs[:groups]
    refs = refs[groups + 2 :]
    if pair:
        grad_ref, *refs = refs
    out_ref, res_ref, sum_ref, table_ref, scalar_ref, zero_ref, sem, table_sem, zero_sem, *refs = refs
    total = groups * keep
    me = me_ref[0]

    zero_ref[...] = jnp.zeros_like(zero_ref)
    zero_copies = []
    for k in range(keep):
        at = pl.multiple_of(kept_ref[k] // col_blocks * BLK, BLK)
        col = pl.multiple_of(kept_ref[k] % col_blocks * BLK, BLK)
        zero_copies.append(
            pltpu.make_async_copy(zero_ref, res_ref.at[pl.ds(at, BLK), pl.ds(col, BLK)], zero_sem.at[k])
        )
        zero_copies[k].start()

    row = lax.broadcasted_iota(jnp.int32, (total, BLK), 0)
    lane = lax.broadcasted_iota(jnp.int32, (total, BLK), 1)
    numbers = jnp.full((total, BLK), -1, jnp.int32)
    for g, block_ref in enumerate(block_refs):
        digits = block_ref[keep * BLK :, :].astype(jnp.float32).astype(jnp.int32)
        numbers = jnp.where(lane // keep == g, digits[0:1, :] * RADIX + digits[1:2, :], numbers)
    numbers = numbers.astype(jnp.float32)
    number = jnp.sum(jnp.where(lane == row, numbers, 0.0), axis=1, keepdims=True)
    first = jnp.min(jnp.where(numbers == number, lane.astype(jnp.float32), float(BLK)), axis=1, keepdims=True)
    number = jnp.broadcast_to(number, (total, BLK)).astype(jnp.int32)
    first = jnp.broadcast_to(first, (total, BLK)).astype(jnp.int32)
    table_ref[...] = jnp.where(lane == 0, jnp.where(number % groups == me, first, -1), number // groups)
    table = pltpu.make_async_copy(table_ref, scalar_ref, table_sem)
    table.start()

    grad_copies = []
    if pair:
        grad_buf, grad_sem = refs
        size = grad_buf.shape[0] // grad_sem.shape[0]
        for c in range(grad_sem.shape[0]):
            part = slice(c * size, (c + 1) * size)
            grad_buf[part, :] = (own_ref[part, :] + arrived_ref[part, :].astype(jnp.float32)).astype(jnp.bfloat16)
            grad_copies.append(pltpu.make_async_copy(grad_buf.at[part, :], grad_ref.at[part, :], grad_sem.at[c]))
            grad_copies[c].start()

    table.wait()

    def copy(i):
        return pltpu.make_async_copy(sum_ref.at[i], out_ref.at[scalar_ref[i, 1]], sem.at[i])

    def block(i):
        at = i % keep * BLK
        return block_refs[i // keep][at : at + BLK, :].astype(jnp.float32)

    for i in range(total):
        slot = scalar_ref[i, 0]

        @pl.when(slot == i)
        def _(i=i):
            sum_ref[i] = block(i)

        if i >= keep:

            @pl.when((slot >= 0) & (slot < i))
            def _(i=i, slot=slot):
                sum_ref[slot] += block(i)

    for i in range(total):

        @pl.when(scalar_ref[i, 0] == i)
        def _(i=i):
            copy(i).start()

    for done in zero_copies + grad_copies:
        done.wait()
    for i in range(total):

        @pl.when(scalar_ref[i, 0] == i)
        def _(i=i):
            copy(i).wait()


def finish(me, kept, parts, blocks, zeros, residual):
    groups = len(blocks)
    keep = kept.shape[0]
    out_shape = [pltpu.HBM(a.shape, a.dtype) for a in (zeros, residual)]
    out_specs = [hbm(), hbm()]
    scratch = [
        pltpu.VMEM((groups * keep, BLK, BLK), jnp.float32),
        pltpu.VMEM((groups * keep, BLK), jnp.int32),
        pltpu.SMEM((groups * keep, BLK), jnp.int32),
        pltpu.VMEM((BLK, BLK), jnp.bfloat16),
        pltpu.SemaphoreType.DMA((groups * keep,)),
        pltpu.SemaphoreType.DMA,
        pltpu.SemaphoreType.DMA((keep,)),
    ]
    if parts:
        out_shape.insert(0, pltpu.HBM(parts[0].shape, jnp.bfloat16))
        out_specs.insert(0, hbm())
        scratch += [pltpu.VMEM(parts[0].shape, jnp.bfloat16), pltpu.SemaphoreType.DMA((4,))]
        parts = [in_vmem(parts[0]), parts[1]]
    first = 2 + len(parts) + groups
    return pl.pallas_call(
        functools.partial(finish_kernel, groups, keep, bool(parts), residual.shape[1] // BLK),
        out_shape=out_shape,
        in_specs=[smem(), smem()] + [vmem()] * (len(parts) + groups) + [hbm(), hbm()],
        out_specs=out_specs,
        scratch_shapes=scratch,
        input_output_aliases={first: len(out_shape) - 2, first + 1: len(out_shape) - 1},
        compiler_params=params(10),
        cost_estimate=cost(groups * keep * BLK * BLK, groups * keep * BLK * BLK * 8),
        name="finish",
    )(me, kept, *parts, *blocks, in_hbm(zeros), in_hbm(residual))


def swapped(x, axis, mask):
    return lax.ppermute(x, axis, [(i, i ^ mask) for i in range(lax.axis_size(axis))])


def of_all_groups(x):
    return [x] + [swapped(x, "dp", mask) for mask in range(1, lax.axis_size("dp"))]


def body(activations, cotangent, weight, residual, step_size, kept_blocks):
    rows, cols = weight.shape
    groups = lax.axis_size("dp")
    owned_count = (rows // BLK) * (cols // BLK) // groups
    kept = kept_blocks.reshape(-1)
    me = lax.axis_index("dp").astype(jnp.int32).reshape(1)
    here = lax.axis_index("tensor").astype(jnp.int32).reshape(1)
    pair = lax.axis_size("tensor") == 2
    if pair:
        act = swapped(activations, "tensor", 1)
        away, acts_t, own, zeros, kept_cot, kept_res = input_grad_partials(
            here, me, kept, cotangent, weight, residual[0], owned_count, activations
        )
        parts = [own, swapped(away, "tensor", 1)]
    else:
        act = lax.all_gather(activations, "tensor", axis=0, tiled=True)
        acts_t = None
        own, zeros, kept_cot, kept_res = input_grad_partials(
            here, me, kept, cotangent, weight, residual[0], owned_count, None
        )
        summed = lax.psum_scatter(own, "tensor", scatter_dimension=0, tiled=True)
        parts = []
    acts_t, blocks = kept_blocks_of(kept, step_size, acts_t, act, kept_cot, kept_res, cols // BLK)
    all_blocks = of_all_groups(blocks)
    rounded = residual_of(here, step_size, acts_t, cotangent, residual[0], pair)
    *grads, owned, residual_out = finish(me, kept, parts, all_blocks, zeros, rounded)
    input_grad = grads[0] if pair else summed.astype(jnp.bfloat16)
    return (input_grad, residual_out[None], owned.reshape(1, 1, 1, owned_count, BLK, BLK))


def solution(mesh):
    in_specs = (
        P(("dp", "tensor"), "fsdp"),
        P("dp", "tensor"),
        P("fsdp", "tensor"),
        P("dp", "fsdp", "tensor"),
        P(),
        P("dp", "fsdp", "tensor", None),
    )
    out_specs = (
        P(("dp", "tensor"), "fsdp"),
        P("dp", "fsdp", "tensor"),
        P("dp", "fsdp", "tensor", None, None, None),
    )
    return jax.shard_map(body, mesh=mesh, in_specs=in_specs, out_specs=out_specs, check_vma=False)
```

```python
import functools

import jax
import jax.numpy as jnp
from jax import lax
from jax.experimental import pallas as pl
from jax.experimental.pallas import tpu as pltpu
from jax.sharding import PartitionSpec as P

BLK = 128
MIB = 1024 * 1024
LABEL_ROWS = 16
RADIX = 16


def cost(flops, nbytes):
    return pl.CostEstimate(flops=flops, bytes_accessed=nbytes, transcendentals=0)


def params(mib=62):
    return pltpu.CompilerParams(vmem_limit_bytes=mib * MIB)


def dot_nt(a, b):
    return lax.dot_general(a, b, (((1,), (1,)), ((), ())), preferred_element_type=jnp.float32)


def dot_nn(a, b):
    return lax.dot_general(a, b, (((1,), (0,)), ((), ())), preferred_element_type=jnp.float32)


def chunking(cols):
    if cols < 4096:
        return cols // 2, 0, cols // 2
    return 512, cols // 1024 - 1, 1024


def smem():
    return pl.BlockSpec(memory_space=pltpu.SMEM)


def vmem():
    return pl.BlockSpec(memory_space=pltpu.VMEM)


def hbm():
    return pl.BlockSpec(memory_space=pltpu.HBM)


def anywhere():
    return pl.BlockSpec(memory_space=pl.ANY)


def in_hbm(x):
    return pltpu.with_memory_space_constraint(x, pltpu.HBM)


def in_vmem(x):
    return pltpu.with_memory_space_constraint(x, pltpu.VMEM)


def cot_copies(here_ref, split, cot_ref, buf_ref, sems):
    if not split:
        return [pltpu.make_async_copy(cot_ref, buf_ref, sems.at[0])]
    half = buf_ref.shape[0] // 2
    copies = []
    for i, at in enumerate((here_ref[0], 1 - here_ref[0])):
        rows = pl.ds(pl.multiple_of(at * half, half), half)
        copies.append(pltpu.make_async_copy(cot_ref.at[rows], buf_ref.at[pl.ds(i * half, half)], sems.at[i]))
    return copies


def input_grad_kernel(split, zero_copies, here_ref, _, kept_in, cot_ref, w_ref, res_ref, *refs):
    if split:
        acts_ref, away_ref, acts_t_ref, *refs = refs
    own_ref, owned_ref, kept_cot_ref, kept_res_ref, *refs = refs
    acc_ref, cot_head, w_head, cot_body, w_body, cot_tail, w_tail, zero_ref, *refs = refs
    kept_ref, kept_sem, cot_sem, w_sem, zero_sem, kept_cot_sem, kept_res_sem, own_sem, *refs = refs
    zero_rows = zero_ref.shape[0]
    rows, hidden = w_ref.shape
    width = min(256, rows)
    keep = kept_cot_ref.shape[0]
    half = own_ref.shape[0]
    head, chunks, chunk = chunking(hidden)

    def loads(at, size, cot_buf, w_buf, i):
        part = pl.ds(at, size)
        return cot_copies(here_ref, split, cot_ref.at[:, part], cot_buf, cot_sem.at[i]) + [
            pltpu.make_async_copy(w_ref.at[:, part], w_buf, w_sem.at[i])
        ]

    def head_loads():
        return loads(0, head, cot_head, w_head, 0)

    def tail_loads():
        return loads(hidden - head, head, cot_tail, w_tail, 1)

    def body_loads(j):
        return loads(pl.multiple_of(head + j * chunk, BLK), chunk, cot_body.at[j], w_body.at[j], 2 + j)

    def start(copies):
        for copy in copies:
            copy.start()

    def wait(copies):
        for copy in copies:
            copy.wait()

    def side_copies():
        copies = []
        for z in range(zero_copies):
            part = pl.ds(z * zero_rows, zero_rows)
            copies.append(pltpu.make_async_copy(zero_ref, owned_ref.at[part], zero_sem.at[z]))
        for k in range(keep):
            col_blocks = hidden // BLK
            row = pl.ds(pl.multiple_of(kept_ref[k] // col_blocks * BLK, BLK), BLK)
            col = pl.ds(pl.multiple_of(kept_ref[k] % col_blocks * BLK, BLK), BLK)
            copies += cot_copies(here_ref, split, cot_ref.at[:, col], kept_cot_ref.at[k], kept_cot_sem.at[k])
            copies.append(pltpu.make_async_copy(res_ref.at[row, col], kept_res_ref.at[k], kept_res_sem.at[k]))
        return copies

    if split:
        acts_buf, acts_t_buf, away_buf, acts_sem, acts_t_sem, away_sem = refs
        acts_copy = pltpu.make_async_copy(acts_ref, acts_buf, acts_sem)
        acts_t_copy = pltpu.make_async_copy(acts_t_buf, acts_t_ref.at[:, pl.ds(0, half)], acts_t_sem)
        acts_copy.start()
    start(head_loads())
    start(body_loads(0) if chunks else tail_loads())
    kept_copy = pltpu.make_async_copy(kept_in, kept_ref, kept_sem)
    kept_copy.start()
    zero_ref[...] = jnp.zeros_like(zero_ref)
    if split:
        acts_copy.wait()
        acts_t_buf[...] = acts_buf[...].T
        acts_t_copy.start()
    wait(head_loads())
    kept_copy.wait()
    if chunks:
        start(body_loads(1))
    for at in range(0, rows, width):
        cols = slice(at, at + width)
        acc_ref[:, cols] = dot_nt(cot_head[...], w_head[cols, :])

    if chunks:

        @pl.loop(0, chunks)
        def _(j):
            wait(body_loads(j))

            @pl.when(j + 2 < chunks)
            def _():
                start(body_loads(j + 2))

            @pl.when(j + 2 == chunks)
            def _():
                start(tail_loads())
                start(side_copies())

            for at in range(0, rows, width):
                cols = slice(at, at + width)
                acc_ref[:, cols] += dot_nt(cot_body[j], w_body[j, cols, :])

    else:
        start(side_copies())
    wait(tail_loads())
    outputs = []
    for n, at in enumerate(range(0, rows, width)):
        cols = slice(at, at + width)
        total = acc_ref[:, cols] + dot_nt(cot_tail[...], w_tail[cols, :])
        if split:
            own_ref[:, cols] = total[:half]
            away_buf[:, cols] = total[half:].astype(jnp.bfloat16)
            outputs.append(pltpu.make_async_copy(away_buf.at[:, cols], away_ref.at[:, cols], away_sem.at[n]))
        else:
            acc_ref[:, cols] = total
            outputs.append(pltpu.make_async_copy(acc_ref.at[:, cols], own_ref.at[:, cols], own_sem.at[n]))
        outputs[n].start()
    if split:
        acts_t_copy.wait()
    wait(side_copies())
    wait(outputs)


def input_grad_partials(here, me, kept, cot, weight, residual, owned_count, acts):
    split = acts is not None
    tokens, cols = cot.shape
    rows = weight.shape[0]
    head, chunks, chunk = chunking(cols)
    keep = kept.shape[0]
    own_rows = tokens // 2 if split else tokens
    zero_rows = min(16, owned_count)
    zero_copies = owned_count // zero_rows
    out_shape = [
        pltpu.VMEM((own_rows, rows), jnp.float32) if split else jax.ShapeDtypeStruct((own_rows, rows), jnp.float32),
        pltpu.HBM((owned_count, BLK, BLK), jnp.float32),
        pltpu.VMEM((keep, tokens, BLK), jnp.bfloat16),
        pltpu.VMEM((keep, BLK, BLK), jnp.bfloat16),
    ]
    out_specs = [vmem() if split else anywhere(), hbm(), vmem(), vmem()]
    scratch = [
        pltpu.VMEM((tokens, rows), jnp.float32),
        pltpu.VMEM((tokens, head), jnp.bfloat16),
        pltpu.VMEM((rows, head), jnp.bfloat16),
        pltpu.VMEM((max(chunks, 1), tokens, chunk), jnp.bfloat16),
        pltpu.VMEM((max(chunks, 1), rows, chunk), jnp.bfloat16),
        pltpu.VMEM((tokens, head), jnp.bfloat16),
        pltpu.VMEM((rows, head), jnp.bfloat16),
        pltpu.VMEM((zero_rows, BLK, BLK), jnp.float32),
        pltpu.SMEM(kept.shape, jnp.int32),
        pltpu.SemaphoreType.DMA,
        pltpu.SemaphoreType.DMA((chunks + 2, 2)),
        pltpu.SemaphoreType.DMA((chunks + 2,)),
        pltpu.SemaphoreType.DMA((zero_copies,)),
        pltpu.SemaphoreType.DMA((keep, 2)),
        pltpu.SemaphoreType.DMA((keep,)),
        pltpu.SemaphoreType.DMA((4,)),
    ]
    if split:
        out_shape = [
            jax.ShapeDtypeStruct((own_rows, rows), jnp.bfloat16),
            pltpu.VMEM((rows, tokens), jnp.bfloat16),
        ] + out_shape
        out_specs = [anywhere(), vmem()] + out_specs
        scratch += [
            pltpu.VMEM(acts.shape, jnp.bfloat16),
            pltpu.VMEM((rows, own_rows), jnp.bfloat16),
            pltpu.VMEM((own_rows, rows), jnp.bfloat16),
            pltpu.SemaphoreType.DMA,
            pltpu.SemaphoreType.DMA,
            pltpu.SemaphoreType.DMA((4,)),
        ]
    return pl.pallas_call(
        functools.partial(input_grad_kernel, split, zero_copies),
        out_shape=out_shape,
        in_specs=[smem()] * 2 + [hbm()] * (4 + split),
        out_specs=out_specs,
        scratch_shapes=scratch,
        compiler_params=params(46),
        cost_estimate=cost(2 * tokens * rows * cols, 2 * cols * (tokens + rows) + 4 * owned_count * BLK * BLK),
        name="input_grad_partials",
    )(here, me, in_hbm(kept), in_hbm(cot), in_hbm(weight), in_hbm(residual), *([in_hbm(acts)] if split else []))


def kept_kernel(pair, col_blocks, kept_ref, step_ref, *refs):
    if pair:
        _, *refs = refs
    act_ref, cot_ref, res_ref, acts_t_ref, out_ref = refs
    keep = cot_ref.shape[0]
    acts_t_ref[:, acts_t_ref.shape[1] - act_ref.shape[0] :] = act_ref[...].T
    for k in range(keep):
        row = pl.ds(pl.multiple_of(kept_ref[k] // col_blocks * BLK, BLK), BLK)
        gradient = dot_nn(acts_t_ref[row, :], cot_ref[k])
        out_ref[k * BLK : (k + 1) * BLK, :] = (res_ref[k].astype(jnp.float32) + step_ref[0] * gradient).astype(
            jnp.bfloat16
        )
    lane = lax.broadcasted_iota(jnp.int32, (LABEL_ROWS, BLK), 1) % keep
    low = lax.broadcasted_iota(jnp.int32, (LABEL_ROWS, BLK), 0) % 2 == 1
    label = jnp.zeros((LABEL_ROWS, BLK), jnp.int32)
    for k in range(keep):
        digit = jnp.where(low, kept_ref[k] % RADIX, kept_ref[k] // RADIX)
        label = jnp.where(lane == k, digit, label)
    out_ref[keep * BLK :, :] = label.astype(jnp.float32).astype(jnp.bfloat16)


def kept_blocks_of(kept, step_size, acts_t, act, kept_cot, kept_res, col_blocks):
    rows = act.shape[1]
    keep, tokens = kept_cot.shape[:2]
    pair = acts_t is not None
    return pl.pallas_call(
        functools.partial(kept_kernel, pair, col_blocks),
        out_shape=[
            pltpu.VMEM((rows, tokens), jnp.bfloat16),
            jax.ShapeDtypeStruct((keep * BLK + LABEL_ROWS, BLK), jnp.bfloat16),
        ],
        in_specs=[smem()] * 2 + [vmem()] * (3 + pair),
        out_specs=[vmem(), vmem()],
        input_output_aliases={2: 0} if pair else {},
        compiler_params=params(4),
        cost_estimate=cost(2 * tokens * BLK * BLK * keep, 4 * tokens * rows + 2 * keep * tokens * BLK),
        name="kept_blocks",
    )(kept, step_size, *([in_vmem(acts_t)] if pair else []), act, in_vmem(kept_cot), in_vmem(kept_res))


def residual_kernel(split, here_ref, step_ref, acts_t_ref, cot_ref, res_ref, out_ref, *refs):
    cot_head, res_head, cot_body, res_body, cot_tail, res_tail, cot_sem, res_sem, out_sem = refs
    step = step_ref[0]
    hidden = cot_ref.shape[1]
    head, chunks, chunk = chunking(hidden)

    def loads(at, size, cot_buf, res_buf, i):
        part = pl.ds(at, size)
        return cot_copies(here_ref, split, cot_ref.at[:, part], cot_buf, cot_sem.at[i]) + [
            pltpu.make_async_copy(res_ref.at[:, part], res_buf, res_sem.at[i])
        ]

    def head_loads():
        return loads(0, head, cot_head, res_head, 0)

    def tail_loads():
        return loads(hidden - head, head, cot_tail, res_tail, 1)

    def body_loads(j):
        return loads(pl.multiple_of(head + j * chunk, BLK), chunk, cot_body.at[j], res_body.at[j], 2 + j)

    def store(at, size, res_buf, i):
        return pltpu.make_async_copy(res_buf, out_ref.at[:, pl.ds(at, size)], out_sem.at[i])

    def head_store():
        return store(0, head, res_head, 0)

    def tail_store():
        return store(hidden - head, head, res_tail, 1)

    def body_store(j):
        return store(pl.multiple_of(head + j * chunk, BLK), chunk, res_body.at[j], 2 + j)

    def start(copies):
        for copy in copies:
            copy.start()

    def wait(copies):
        for copy in copies:
            copy.wait()

    def work(cot_buf, res_buf):
        size = cot_buf.shape[1]
        width = min(512, size)
        for at in range(0, size, width):
            part = slice(at, at + width)
            gradient = dot_nn(acts_t_ref[...], cot_buf[:, part])
            res_buf[:, part] = (res_buf[:, part].astype(jnp.float32) + step * gradient).astype(jnp.bfloat16)

    start(head_loads())
    start(body_loads(0) if chunks else tail_loads())
    wait(head_loads())
    if chunks:
        start(body_loads(1))
    work(cot_head, res_head)
    head_store().start()

    if chunks:

        @pl.loop(0, chunks)
        def _(j):
            wait(body_loads(j))

            @pl.when(j + 2 < chunks)
            def _():
                start(body_loads(j + 2))

            @pl.when(j + 2 == chunks)
            def _():
                start(tail_loads())

            work(cot_body.at[j], res_body.at[j])
            body_store(j).start()

    wait(tail_loads())
    work(cot_tail, res_tail)
    tail_store().start()
    head_store().wait()
    for j in range(chunks):
        body_store(j).wait()
    tail_store().wait()


def residual_of(here, step_size, acts_t, cot, residual, split):
    tokens, cols = cot.shape
    rows = residual.shape[0]
    head, chunks, chunk = chunking(cols)
    sem = pltpu.SemaphoreType.DMA((chunks + 2,))
    return pl.pallas_call(
        functools.partial(residual_kernel, split),
        out_shape=pltpu.HBM((rows, cols), jnp.bfloat16),
        in_specs=[smem()] * 2 + [vmem(), hbm(), hbm()],
        out_specs=hbm(),
        scratch_shapes=[
            pltpu.VMEM((tokens, head), jnp.bfloat16),
            pltpu.VMEM((rows, head), jnp.bfloat16),
            pltpu.VMEM((max(chunks, 1), tokens, chunk), jnp.bfloat16),
            pltpu.VMEM((max(chunks, 1), rows, chunk), jnp.bfloat16),
            pltpu.VMEM((tokens, head), jnp.bfloat16),
            pltpu.VMEM((rows, head), jnp.bfloat16),
            pltpu.SemaphoreType.DMA((chunks + 2, 2)),
            sem,
            sem,
        ],
        compiler_params=params(38),
        cost_estimate=cost(2 * tokens * rows * cols, 2 * tokens * (rows + cols) + 4 * rows * cols),
        name="residual_out",
    )(here, step_size, in_vmem(acts_t), in_hbm(cot), in_hbm(residual))


def finish_kernel(groups, keep, pair, col_blocks, me_ref, kept_ref, *refs):
    if pair:
        own_ref, arrived_ref, *refs = refs
    block_refs = refs[:groups]
    refs = refs[groups + 2 :]
    if pair:
        grad_ref, *refs = refs
    out_ref, res_ref, sum_ref, table_ref, scalar_ref, zero_ref, sem, table_sem, zero_sem, *refs = refs
    total = groups * keep
    me = me_ref[0]

    zero_ref[...] = jnp.zeros_like(zero_ref)
    zero_copies = []
    for k in range(keep):
        at = pl.multiple_of(kept_ref[k] // col_blocks * BLK, BLK)
        col = pl.multiple_of(kept_ref[k] % col_blocks * BLK, BLK)
        zero_copies.append(
            pltpu.make_async_copy(zero_ref, res_ref.at[pl.ds(at, BLK), pl.ds(col, BLK)], zero_sem.at[k])
        )
        zero_copies[k].start()

    row = lax.broadcasted_iota(jnp.int32, (total, BLK), 0)
    lane = lax.broadcasted_iota(jnp.int32, (total, BLK), 1)
    numbers = jnp.full((total, BLK), -1, jnp.int32)
    for g, block_ref in enumerate(block_refs):
        digits = block_ref[keep * BLK :, :].astype(jnp.float32).astype(jnp.int32)
        numbers = jnp.where(lane // keep == g, digits[0:1, :] * RADIX + digits[1:2, :], numbers)
    numbers = numbers.astype(jnp.float32)
    number = jnp.sum(jnp.where(lane == row, numbers, 0.0), axis=1, keepdims=True)
    first = jnp.min(jnp.where(numbers == number, lane.astype(jnp.float32), float(BLK)), axis=1, keepdims=True)
    final = jnp.max(jnp.where(numbers == number, lane.astype(jnp.float32), -1.0), axis=1, keepdims=True)
    number = jnp.broadcast_to(number, (total, BLK)).astype(jnp.int32)
    first = jnp.broadcast_to(first, (total, BLK)).astype(jnp.int32)
    first = jnp.where(number % groups == me, first, -1)
    final = jnp.broadcast_to(final, (total, BLK)).astype(jnp.int32)
    table_ref[...] = jnp.where(lane == 0, first, jnp.where(lane == 1, number // groups, final))
    table = pltpu.make_async_copy(table_ref, scalar_ref, table_sem)
    table.start()

    grad_copies = []
    if pair:
        grad_buf, grad_sem = refs
        size = grad_buf.shape[0] // grad_sem.shape[0]
        for c in range(grad_sem.shape[0]):
            part = slice(c * size, (c + 1) * size)
            grad_buf[part, :] = (own_ref[part, :] + arrived_ref[part, :].astype(jnp.float32)).astype(jnp.bfloat16)
            grad_copies.append(pltpu.make_async_copy(grad_buf.at[part, :], grad_ref.at[part, :], grad_sem.at[c]))
            grad_copies[c].start()

    table.wait()

    def copy(i):
        return pltpu.make_async_copy(sum_ref.at[i], out_ref.at[scalar_ref[i, 1]], sem.at[i])

    def block(i):
        at = i % keep * BLK
        return block_refs[i // keep][at : at + BLK, :].astype(jnp.float32)

    for i in range(total):
        slot = scalar_ref[i, 0]

        @pl.when(slot >= 0)
        def _(i=i, slot=slot):
            @pl.when(slot == i)
            def _():
                sum_ref[i] = block(i)

            if i >= keep:

                @pl.when(slot < i)
                def _():
                    sum_ref[slot] += block(i)

            @pl.when(scalar_ref[i, 2] == i)
            def _():
                copy(slot).start()

    for done in zero_copies + grad_copies:
        done.wait()
    for i in range(total):

        @pl.when(scalar_ref[i, 0] == i)
        def _(i=i):
            copy(i).wait()


def finish(me, kept, parts, blocks, zeros, residual):
    groups = len(blocks)
    keep = kept.shape[0]
    out_shape = [pltpu.HBM(a.shape, a.dtype) for a in (zeros, residual)]
    out_specs = [hbm(), hbm()]
    scratch = [
        pltpu.VMEM((groups * keep, BLK, BLK), jnp.float32),
        pltpu.VMEM((groups * keep, BLK), jnp.int32),
        pltpu.SMEM((groups * keep, BLK), jnp.int32),
        pltpu.VMEM((BLK, BLK), jnp.bfloat16),
        pltpu.SemaphoreType.DMA((groups * keep,)),
        pltpu.SemaphoreType.DMA,
        pltpu.SemaphoreType.DMA((keep,)),
    ]
    if parts:
        out_shape.insert(0, pltpu.HBM(parts[0].shape, jnp.bfloat16))
        out_specs.insert(0, hbm())
        scratch += [pltpu.VMEM(parts[0].shape, jnp.bfloat16), pltpu.SemaphoreType.DMA((4,))]
        parts = [in_vmem(parts[0]), parts[1]]
    first = 2 + len(parts) + groups
    return pl.pallas_call(
        functools.partial(finish_kernel, groups, keep, bool(parts), residual.shape[1] // BLK),
        out_shape=out_shape,
        in_specs=[smem(), smem()] + [vmem()] * (len(parts) + groups) + [hbm(), hbm()],
        out_specs=out_specs,
        scratch_shapes=scratch,
        input_output_aliases={first: len(out_shape) - 2, first + 1: len(out_shape) - 1},
        compiler_params=params(10),
        cost_estimate=cost(groups * keep * BLK * BLK, groups * keep * BLK * BLK * 8),
        name="finish",
    )(me, kept, *parts, *blocks, in_hbm(zeros), in_hbm(residual))


def swapped(x, axis, mask):
    return lax.ppermute(x, axis, [(i, i ^ mask) for i in range(lax.axis_size(axis))])


def of_all_groups(x):
    return [x] + [swapped(x, "dp", mask) for mask in range(1, lax.axis_size("dp"))]


def body(activations, cotangent, weight, residual, step_size, kept_blocks):
    rows, cols = weight.shape
    groups = lax.axis_size("dp")
    owned_count = (rows // BLK) * (cols // BLK) // groups
    kept = kept_blocks.reshape(-1)
    me = lax.axis_index("dp").astype(jnp.int32).reshape(1)
    here = lax.axis_index("tensor").astype(jnp.int32).reshape(1)
    pair = lax.axis_size("tensor") == 2
    if pair:
        act = swapped(activations, "tensor", 1)
        away, acts_t, own, zeros, kept_cot, kept_res = input_grad_partials(
            here, me, kept, cotangent, weight, residual[0], owned_count, activations
        )
        parts = [own, swapped(away, "tensor", 1)]
    else:
        act = lax.all_gather(activations, "tensor", axis=0, tiled=True)
        acts_t = None
        own, zeros, kept_cot, kept_res = input_grad_partials(
            here, me, kept, cotangent, weight, residual[0], owned_count, None
        )
        summed = lax.psum_scatter(own, "tensor", scatter_dimension=0, tiled=True)
        parts = []
    acts_t, blocks = kept_blocks_of(kept, step_size, acts_t, act, kept_cot, kept_res, cols // BLK)
    all_blocks = of_all_groups(blocks)
    rounded = residual_of(here, step_size, acts_t, cotangent, residual[0], pair)
    *grads, owned, residual_out = finish(me, kept, parts, all_blocks, zeros, rounded)
    input_grad = grads[0] if pair else summed.astype(jnp.bfloat16)
    return (input_grad, residual_out[None], owned.reshape(1, 1, 1, owned_count, BLK, BLK))


def solution(mesh):
    in_specs = (
        P(("dp", "tensor"), "fsdp"),
        P("dp", "tensor"),
        P("fsdp", "tensor"),
        P("dp", "fsdp", "tensor"),
        P(),
        P("dp", "fsdp", "tensor", None),
    )
    out_specs = (
        P(("dp", "tensor"), "fsdp"),
        P("dp", "fsdp", "tensor"),
        P("dp", "fsdp", "tensor", None, None, None),
    )
    return jax.shard_map(body, mesh=mesh, in_specs=in_specs, out_specs=out_specs, check_vma=False)
```

```python
import functools

import jax
import jax.numpy as jnp
from jax import lax
from jax.experimental import pallas as pl
from jax.experimental.pallas import tpu as pltpu
from jax.sharding import PartitionSpec as P

BLK = 128
MIB = 1024 * 1024
LABEL_ROWS = 16
RADIX = 16
INPUT_GRAD_HEAD = 1024
RESIDUAL_HEAD = 512


def cost(flops, nbytes):
    return pl.CostEstimate(flops=flops, bytes_accessed=nbytes, transcendentals=0)


def params(mib=62):
    return pltpu.CompilerParams(vmem_limit_bytes=mib * MIB)


def dot_nt(a, b):
    return lax.dot_general(a, b, (((1,), (1,)), ((), ())), preferred_element_type=jnp.float32)


def dot_nn(a, b):
    return lax.dot_general(a, b, (((1,), (0,)), ((), ())), preferred_element_type=jnp.float32)


def chunking(cols, head):
    if cols < 8 * head:
        return cols // 2, 0, cols // 2
    return head, cols // (2 * head) - 1, 2 * head


def smem():
    return pl.BlockSpec(memory_space=pltpu.SMEM)


def vmem():
    return pl.BlockSpec(memory_space=pltpu.VMEM)


def hbm():
    return pl.BlockSpec(memory_space=pltpu.HBM)


def anywhere():
    return pl.BlockSpec(memory_space=pl.ANY)


def in_hbm(x):
    return pltpu.with_memory_space_constraint(x, pltpu.HBM)


def in_vmem(x):
    return pltpu.with_memory_space_constraint(x, pltpu.VMEM)


def cot_copies(here_ref, split, cot_ref, buf_ref, sems):
    if not split:
        return [pltpu.make_async_copy(cot_ref, buf_ref, sems.at[0])]
    half = buf_ref.shape[0] // 2
    copies = []
    for i, at in enumerate((here_ref[0], 1 - here_ref[0])):
        rows = pl.ds(pl.multiple_of(at * half, half), half)
        copies.append(pltpu.make_async_copy(cot_ref.at[rows], buf_ref.at[pl.ds(i * half, half)], sems.at[i]))
    return copies


def input_grad_kernel(split, zero_copies, here_ref, _, kept_in, cot_ref, w_ref, res_ref, *refs):
    if split:
        acts_ref, away_ref, acts_t_ref, *refs = refs
    own_ref, owned_ref, kept_cot_ref, kept_res_ref, *refs = refs
    acc_ref, cot_head, w_head, cot_body, w_body, cot_tail, w_tail, zero_ref, *refs = refs
    kept_ref, kept_sem, cot_sem, w_sem, zero_sem, kept_cot_sem, kept_res_sem, own_sem, *refs = refs
    zero_rows = zero_ref.shape[0]
    rows, hidden = w_ref.shape
    width = min(256, rows)
    keep = kept_cot_ref.shape[0]
    half = own_ref.shape[0]
    head, chunks, chunk = chunking(hidden, INPUT_GRAD_HEAD)

    def loads(at, size, cot_buf, w_buf, i):
        part = pl.ds(at, size)
        return cot_copies(here_ref, split, cot_ref.at[:, part], cot_buf, cot_sem.at[i]) + [
            pltpu.make_async_copy(w_ref.at[:, part], w_buf, w_sem.at[i])
        ]

    def head_loads():
        return loads(0, head, cot_head, w_head, 0)

    def tail_loads():
        return loads(hidden - head, head, cot_tail, w_tail, 1)

    def body_loads(j):
        return loads(pl.multiple_of(head + j * chunk, BLK), chunk, cot_body.at[j], w_body.at[j], 2 + j)

    def start(copies):
        for copy in copies:
            copy.start()

    def wait(copies):
        for copy in copies:
            copy.wait()

    def side_copies():
        copies = []
        for z in range(zero_copies):
            part = pl.ds(z * zero_rows, zero_rows)
            copies.append(pltpu.make_async_copy(zero_ref, owned_ref.at[part], zero_sem.at[z]))
        for k in range(keep):
            col_blocks = hidden // BLK
            row = pl.ds(pl.multiple_of(kept_ref[k] // col_blocks * BLK, BLK), BLK)
            col = pl.ds(pl.multiple_of(kept_ref[k] % col_blocks * BLK, BLK), BLK)
            copies += cot_copies(here_ref, split, cot_ref.at[:, col], kept_cot_ref.at[k], kept_cot_sem.at[k])
            copies.append(pltpu.make_async_copy(res_ref.at[row, col], kept_res_ref.at[k], kept_res_sem.at[k]))
        return copies

    if split:
        acts_buf, acts_t_buf, away_buf, acts_sem, acts_t_sem, away_sem = refs
        acts_copy = pltpu.make_async_copy(acts_ref, acts_buf, acts_sem)
        acts_t_copy = pltpu.make_async_copy(acts_t_buf, acts_t_ref.at[:, pl.ds(0, half)], acts_t_sem)
        acts_copy.start()
    start(head_loads())
    kept_copy = pltpu.make_async_copy(kept_in, kept_ref, kept_sem)
    kept_copy.start()
    zero_ref[...] = jnp.zeros_like(zero_ref)
    if split:
        acts_copy.wait()
        acts_t_buf[...] = acts_buf[...].T
        acts_t_copy.start()
    start(body_loads(0) if chunks else tail_loads())
    wait(head_loads())
    kept_copy.wait()
    if chunks:
        start(body_loads(1))
    for at in range(0, rows, width):
        cols = slice(at, at + width)
        acc_ref[:, cols] = dot_nt(cot_head[...], w_head[cols, :])

    if chunks:

        @pl.loop(0, chunks)
        def _(j):
            wait(body_loads(j))

            @pl.when(j + 2 < chunks)
            def _():
                start(body_loads(j + 2))

            @pl.when(j + 2 == chunks)
            def _():
                start(tail_loads())
                start(side_copies())

            for at in range(0, rows, width):
                cols = slice(at, at + width)
                acc_ref[:, cols] += dot_nt(cot_body[j], w_body[j, cols, :])

    else:
        start(side_copies())
    wait(tail_loads())
    outputs = []
    for n, at in enumerate(range(0, rows, width)):
        cols = slice(at, at + width)
        total = acc_ref[:, cols] + dot_nt(cot_tail[...], w_tail[cols, :])
        if split:
            own_ref[:, cols] = total[:half]
            away_buf[:, cols] = total[half:].astype(jnp.bfloat16)
            outputs.append(pltpu.make_async_copy(away_buf.at[:, cols], away_ref.at[:, cols], away_sem.at[n]))
        else:
            acc_ref[:, cols] = total
            outputs.append(pltpu.make_async_copy(acc_ref.at[:, cols], own_ref.at[:, cols], own_sem.at[n]))
    start(outputs)
    if split:
        acts_t_copy.wait()
    wait(side_copies())
    wait(outputs)


def input_grad_partials(here, me, kept, cot, weight, residual, owned_count, acts):
    split = acts is not None
    tokens, cols = cot.shape
    rows = weight.shape[0]
    head, chunks, chunk = chunking(cols, INPUT_GRAD_HEAD)
    keep = kept.shape[0]
    own_rows = tokens // 2 if split else tokens
    zero_rows = min(16, owned_count)
    zero_copies = owned_count // zero_rows
    out_shape = [
        pltpu.VMEM((own_rows, rows), jnp.float32) if split else jax.ShapeDtypeStruct((own_rows, rows), jnp.float32),
        pltpu.HBM((owned_count, BLK, BLK), jnp.float32),
        pltpu.VMEM((keep, tokens, BLK), jnp.bfloat16),
        pltpu.VMEM((keep, BLK, BLK), jnp.bfloat16),
    ]
    out_specs = [vmem() if split else anywhere(), hbm(), vmem(), vmem()]
    scratch = [
        pltpu.VMEM((tokens, rows), jnp.float32),
        pltpu.VMEM((tokens, head), jnp.bfloat16),
        pltpu.VMEM((rows, head), jnp.bfloat16),
        pltpu.VMEM((max(chunks, 1), tokens, chunk), jnp.bfloat16),
        pltpu.VMEM((max(chunks, 1), rows, chunk), jnp.bfloat16),
        pltpu.VMEM((tokens, head), jnp.bfloat16),
        pltpu.VMEM((rows, head), jnp.bfloat16),
        pltpu.VMEM((zero_rows, BLK, BLK), jnp.float32),
        pltpu.SMEM(kept.shape, jnp.int32),
        pltpu.SemaphoreType.DMA,
        pltpu.SemaphoreType.DMA((chunks + 2, 2)),
        pltpu.SemaphoreType.DMA((chunks + 2,)),
        pltpu.SemaphoreType.DMA((zero_copies,)),
        pltpu.SemaphoreType.DMA((keep, 2)),
        pltpu.SemaphoreType.DMA((keep,)),
        pltpu.SemaphoreType.DMA((4,)),
    ]
    if split:
        out_shape = [
            jax.ShapeDtypeStruct((own_rows, rows), jnp.bfloat16),
            pltpu.VMEM((rows, tokens), jnp.bfloat16),
        ] + out_shape
        out_specs = [anywhere(), vmem()] + out_specs
        scratch += [
            pltpu.VMEM(acts.shape, jnp.bfloat16),
            pltpu.VMEM((rows, own_rows), jnp.bfloat16),
            pltpu.VMEM((own_rows, rows), jnp.bfloat16),
            pltpu.SemaphoreType.DMA,
            pltpu.SemaphoreType.DMA,
            pltpu.SemaphoreType.DMA((4,)),
        ]
    return pl.pallas_call(
        functools.partial(input_grad_kernel, split, zero_copies),
        out_shape=out_shape,
        in_specs=[smem()] * 2 + [hbm()] * (4 + split),
        out_specs=out_specs,
        scratch_shapes=scratch,
        compiler_params=params(46),
        cost_estimate=cost(2 * tokens * rows * cols, 2 * cols * (tokens + rows) + 4 * owned_count * BLK * BLK),
        name="input_grad_partials",
    )(here, me, in_hbm(kept), in_hbm(cot), in_hbm(weight), in_hbm(residual), *([in_hbm(acts)] if split else []))


def kept_kernel(pair, col_blocks, kept_ref, step_ref, *refs):
    if pair:
        _, *refs = refs
    act_ref, cot_ref, res_ref, acts_t_ref, out_ref = refs
    keep = cot_ref.shape[0]
    acts_t_ref[:, acts_t_ref.shape[1] - act_ref.shape[0] :] = act_ref[...].T
    for k in range(keep):
        row = pl.ds(pl.multiple_of(kept_ref[k] // col_blocks * BLK, BLK), BLK)
        gradient = dot_nn(acts_t_ref[row, :], cot_ref[k])
        out_ref[k * BLK : (k + 1) * BLK, :] = (res_ref[k].astype(jnp.float32) + step_ref[0] * gradient).astype(
            jnp.bfloat16
        )
    lane = lax.broadcasted_iota(jnp.int32, (LABEL_ROWS, BLK), 1) % keep
    low = lax.broadcasted_iota(jnp.int32, (LABEL_ROWS, BLK), 0) % 2 == 1
    label = jnp.zeros((LABEL_ROWS, BLK), jnp.int32)
    for k in range(keep):
        digit = jnp.where(low, kept_ref[k] % RADIX, kept_ref[k] // RADIX)
        label = jnp.where(lane == k, digit, label)
    out_ref[keep * BLK :, :] = label.astype(jnp.float32).astype(jnp.bfloat16)


def kept_blocks_of(kept, step_size, acts_t, act, kept_cot, kept_res, col_blocks):
    rows = act.shape[1]
    keep, tokens = kept_cot.shape[:2]
    pair = acts_t is not None
    return pl.pallas_call(
        functools.partial(kept_kernel, pair, col_blocks),
        out_shape=[
            pltpu.VMEM((rows, tokens), jnp.bfloat16),
            jax.ShapeDtypeStruct((keep * BLK + LABEL_ROWS, BLK), jnp.bfloat16),
        ],
        in_specs=[smem()] * 2 + [vmem()] * (3 + pair),
        out_specs=[vmem(), vmem()],
        input_output_aliases={2: 0} if pair else {},
        compiler_params=params(4),
        cost_estimate=cost(2 * tokens * BLK * BLK * keep, 4 * tokens * rows + 2 * keep * tokens * BLK),
        name="kept_blocks",
    )(kept, step_size, *([in_vmem(acts_t)] if pair else []), act, in_vmem(kept_cot), in_vmem(kept_res))


def residual_kernel(split, here_ref, step_ref, acts_t_ref, cot_ref, res_ref, out_ref, *refs):
    cot_head, res_head, cot_body, res_body, cot_tail, res_tail, cot_sem, res_sem, out_sem = refs
    step = step_ref[0]
    hidden = cot_ref.shape[1]
    head, chunks, chunk = chunking(hidden, RESIDUAL_HEAD)

    def loads(at, size, cot_buf, res_buf, i):
        part = pl.ds(at, size)
        return cot_copies(here_ref, split, cot_ref.at[:, part], cot_buf, cot_sem.at[i]) + [
            pltpu.make_async_copy(res_ref.at[:, part], res_buf, res_sem.at[i])
        ]

    def head_loads():
        return loads(0, head, cot_head, res_head, 0)

    def tail_loads():
        return loads(hidden - head, head, cot_tail, res_tail, 1)

    def body_loads(j):
        return loads(pl.multiple_of(head + j * chunk, BLK), chunk, cot_body.at[j], res_body.at[j], 2 + j)

    def store(at, size, res_buf, i):
        return pltpu.make_async_copy(res_buf, out_ref.at[:, pl.ds(at, size)], out_sem.at[i])

    def head_store():
        return store(0, head, res_head, 0)

    def tail_store():
        return store(hidden - head, head, res_tail, 1)

    def body_store(j):
        return store(pl.multiple_of(head + j * chunk, BLK), chunk, res_body.at[j], 2 + j)

    def start(copies):
        for copy in copies:
            copy.start()

    def wait(copies):
        for copy in copies:
            copy.wait()

    def work(cot_buf, res_buf):
        size = cot_buf.shape[1]
        width = min(256, size)
        for at in range(0, size, width):
            part = slice(at, at + width)
            gradient = dot_nn(acts_t_ref[...], cot_buf[:, part])
            res_buf[:, part] = (res_buf[:, part].astype(jnp.float32) + step * gradient).astype(jnp.bfloat16)

    start(head_loads())
    start(body_loads(0) if chunks else tail_loads())
    wait(head_loads())
    if chunks:
        start(body_loads(1))
    work(cot_head, res_head)
    head_store().start()

    if chunks:

        @pl.loop(0, chunks)
        def _(j):
            wait(body_loads(j))

            @pl.when(j + 2 < chunks)
            def _():
                start(body_loads(j + 2))

            @pl.when(j + 2 == chunks)
            def _():
                start(tail_loads())

            work(cot_body.at[j], res_body.at[j])
            body_store(j).start()

    wait(tail_loads())
    work(cot_tail, res_tail)
    tail_store().start()
    head_store().wait()
    for j in range(chunks):
        body_store(j).wait()
    tail_store().wait()


def residual_of(here, step_size, acts_t, cot, residual, split):
    tokens, cols = cot.shape
    rows = residual.shape[0]
    head, chunks, chunk = chunking(cols, RESIDUAL_HEAD)
    sem = pltpu.SemaphoreType.DMA((chunks + 2,))
    return pl.pallas_call(
        functools.partial(residual_kernel, split),
        out_shape=pltpu.HBM((rows, cols), jnp.bfloat16),
        in_specs=[smem()] * 2 + [vmem(), hbm(), hbm()],
        out_specs=hbm(),
        scratch_shapes=[
            pltpu.VMEM((tokens, head), jnp.bfloat16),
            pltpu.VMEM((rows, head), jnp.bfloat16),
            pltpu.VMEM((max(chunks, 1), tokens, chunk), jnp.bfloat16),
            pltpu.VMEM((max(chunks, 1), rows, chunk), jnp.bfloat16),
            pltpu.VMEM((tokens, head), jnp.bfloat16),
            pltpu.VMEM((rows, head), jnp.bfloat16),
            pltpu.SemaphoreType.DMA((chunks + 2, 2)),
            sem,
            sem,
        ],
        compiler_params=params(38),
        cost_estimate=cost(2 * tokens * rows * cols, 2 * tokens * (rows + cols) + 4 * rows * cols),
        name="residual_out",
    )(here, step_size, in_vmem(acts_t), in_hbm(cot), in_hbm(residual))


def finish_kernel(groups, keep, pair, col_blocks, me_ref, kept_ref, *refs):
    if pair:
        own_ref, arrived_ref, *refs = refs
    block_refs = refs[:groups]
    refs = refs[groups + 2 :]
    if pair:
        grad_ref, *refs = refs
    out_ref, res_ref, sum_ref, table_ref, scalar_ref, zero_ref, sem, table_sem, zero_sem, *refs = refs
    total = groups * keep
    me = me_ref[0]

    zero_ref[...] = jnp.zeros_like(zero_ref)
    zero_copies = []
    for k in range(keep):
        at = pl.multiple_of(kept_ref[k] // col_blocks * BLK, BLK)
        col = pl.multiple_of(kept_ref[k] % col_blocks * BLK, BLK)
        zero_copies.append(
            pltpu.make_async_copy(zero_ref, res_ref.at[pl.ds(at, BLK), pl.ds(col, BLK)], zero_sem.at[k])
        )
        zero_copies[k].start()

    row = lax.broadcasted_iota(jnp.int32, (total, BLK), 0)
    lane = lax.broadcasted_iota(jnp.int32, (total, BLK), 1)
    numbers = jnp.full((total, BLK), -1, jnp.int32)
    for g, block_ref in enumerate(block_refs):
        digits = block_ref[keep * BLK :, :].astype(jnp.float32).astype(jnp.int32)
        numbers = jnp.where(lane // keep == g, digits[0:1, :] * RADIX + digits[1:2, :], numbers)
    numbers = numbers.astype(jnp.float32)
    number = jnp.sum(jnp.where(lane == row, numbers, 0.0), axis=1, keepdims=True)
    first = jnp.min(jnp.where(numbers == number, lane.astype(jnp.float32), float(BLK)), axis=1, keepdims=True)
    final = jnp.max(jnp.where(numbers == number, lane.astype(jnp.float32), -1.0), axis=1, keepdims=True)
    number = jnp.broadcast_to(number, (total, BLK)).astype(jnp.int32)
    first = jnp.broadcast_to(first, (total, BLK)).astype(jnp.int32)
    first = jnp.where(number % groups == me, first, -1)
    final = jnp.broadcast_to(final, (total, BLK)).astype(jnp.int32)
    table_ref[...] = jnp.where(lane == 0, first, jnp.where(lane == 1, number // groups, final))
    table = pltpu.make_async_copy(table_ref, scalar_ref, table_sem)
    table.start()

    grad_copies = []
    if pair:
        grad_buf, grad_sem = refs
        size = grad_buf.shape[0] // grad_sem.shape[0]
        for c in range(grad_sem.shape[0]):
            part = slice(c * size, (c + 1) * size)
            grad_buf[part, :] = (own_ref[part, :] + arrived_ref[part, :].astype(jnp.float32)).astype(jnp.bfloat16)
            grad_copies.append(pltpu.make_async_copy(grad_buf.at[part, :], grad_ref.at[part, :], grad_sem.at[c]))
            grad_copies[c].start()

    table.wait()

    def copy(i):
        return pltpu.make_async_copy(sum_ref.at[i], out_ref.at[scalar_ref[i, 1]], sem.at[i])

    def block(i):
        at = i % keep * BLK
        return block_refs[i // keep][at : at + BLK, :].astype(jnp.float32)

    for i in range(total):
        slot = scalar_ref[i, 0]

        @pl.when(slot >= 0)
        def _(i=i, slot=slot):
            @pl.when(slot == i)
            def _():
                sum_ref[i] = block(i)

            if i >= keep:

                @pl.when(slot < i)
                def _():
                    sum_ref[slot] += block(i)

            @pl.when(scalar_ref[i, 2] == i)
            def _():
                copy(slot).start()

    for done in zero_copies + grad_copies:
        done.wait()
    for i in range(total):

        @pl.when(scalar_ref[i, 0] == i)
        def _(i=i):
            copy(i).wait()


def finish(me, kept, parts, blocks, zeros, residual):
    groups = len(blocks)
    keep = kept.shape[0]
    out_shape = [pltpu.HBM(a.shape, a.dtype) for a in (zeros, residual)]
    out_specs = [hbm(), hbm()]
    scratch = [
        pltpu.VMEM((groups * keep, BLK, BLK), jnp.float32),
        pltpu.VMEM((groups * keep, BLK), jnp.int32),
        pltpu.SMEM((groups * keep, BLK), jnp.int32),
        pltpu.VMEM((BLK, BLK), jnp.bfloat16),
        pltpu.SemaphoreType.DMA((groups * keep,)),
        pltpu.SemaphoreType.DMA,
        pltpu.SemaphoreType.DMA((keep,)),
    ]
    if parts:
        out_shape.insert(0, pltpu.HBM(parts[0].shape, jnp.bfloat16))
        out_specs.insert(0, hbm())
        scratch += [pltpu.VMEM(parts[0].shape, jnp.bfloat16), pltpu.SemaphoreType.DMA((4,))]
        parts = [in_vmem(parts[0]), parts[1]]
    first = 2 + len(parts) + groups
    return pl.pallas_call(
        functools.partial(finish_kernel, groups, keep, bool(parts), residual.shape[1] // BLK),
        out_shape=out_shape,
        in_specs=[smem(), smem()] + [vmem()] * (len(parts) + groups) + [hbm(), hbm()],
        out_specs=out_specs,
        scratch_shapes=scratch,
        input_output_aliases={first: len(out_shape) - 2, first + 1: len(out_shape) - 1},
        compiler_params=params(10),
        cost_estimate=cost(groups * keep * BLK * BLK, groups * keep * BLK * BLK * 8),
        name="finish",
    )(me, kept, *parts, *blocks, in_hbm(zeros), in_hbm(residual))


def swapped(x, axis, mask):
    return lax.ppermute(x, axis, [(i, i ^ mask) for i in range(lax.axis_size(axis))])


def of_all_groups(x):
    return [x] + [swapped(x, "dp", mask) for mask in range(1, lax.axis_size("dp"))]


def body(activations, cotangent, weight, residual, step_size, kept_blocks):
    rows, cols = weight.shape
    groups = lax.axis_size("dp")
    owned_count = (rows // BLK) * (cols // BLK) // groups
    kept = kept_blocks.reshape(-1)
    me = lax.axis_index("dp").astype(jnp.int32).reshape(1)
    here = lax.axis_index("tensor").astype(jnp.int32).reshape(1)
    pair = lax.axis_size("tensor") == 2
    if pair:
        act = swapped(activations, "tensor", 1)
        away, acts_t, own, zeros, kept_cot, kept_res = input_grad_partials(
            here, me, kept, cotangent, weight, residual[0], owned_count, activations
        )
        parts = [own, swapped(away, "tensor", 1)]
    else:
        act = lax.all_gather(activations, "tensor", axis=0, tiled=True)
        acts_t = None
        own, zeros, kept_cot, kept_res = input_grad_partials(
            here, me, kept, cotangent, weight, residual[0], owned_count, None
        )
        summed = lax.psum_scatter(own, "tensor", scatter_dimension=0, tiled=True)
        parts = []
    acts_t, blocks = kept_blocks_of(kept, step_size, acts_t, act, kept_cot, kept_res, cols // BLK)
    all_blocks = of_all_groups(blocks)
    rounded = residual_of(here, step_size, acts_t, cotangent, residual[0], pair)
    *grads, owned, residual_out = finish(me, kept, parts, all_blocks, zeros, rounded)
    input_grad = grads[0] if pair else summed.astype(jnp.bfloat16)
    return (input_grad, residual_out[None], owned.reshape(1, 1, 1, owned_count, BLK, BLK))


def solution(mesh):
    in_specs = (
        P(("dp", "tensor"), "fsdp"),
        P("dp", "tensor"),
        P("fsdp", "tensor"),
        P("dp", "fsdp", "tensor"),
        P(),
        P("dp", "fsdp", "tensor", None),
    )
    out_specs = (
        P(("dp", "tensor"), "fsdp"),
        P("dp", "fsdp", "tensor"),
        P("dp", "fsdp", "tensor", None, None, None),
    )
    return jax.shard_map(body, mesh=mesh, in_specs=in_specs, out_specs=out_specs, check_vma=False)
```

```python
import functools

import jax
import jax.numpy as jnp
from jax import lax
from jax.experimental import pallas as pl
from jax.experimental.pallas import tpu as pltpu
from jax.sharding import PartitionSpec as P

BLK = 128
MIB = 1024 * 1024
LABEL_ROWS = 16
RADIX = 16


def cost(flops, nbytes):
    return pl.CostEstimate(flops=flops, bytes_accessed=nbytes, transcendentals=0)


def params(mib=62):
    return pltpu.CompilerParams(vmem_limit_bytes=mib * MIB)


def dot_nt(a, b):
    return lax.dot_general(a, b, (((1,), (1,)), ((), ())), preferred_element_type=jnp.float32)


def dot_nn(a, b):
    return lax.dot_general(a, b, (((1,), (0,)), ((), ())), preferred_element_type=jnp.float32)


def chunking(cols):
    if cols < 8192:
        return cols // 2, 0, cols // 2
    return 1024, cols // 2048 - 1, 2048


def column_chunking(cols):
    if cols < 8192:
        return cols // 2, 0, cols // 2, [cols // 2]
    return 1024, cols // 1024 - 2, 1024, [512, 512]


def smem():
    return pl.BlockSpec(memory_space=pltpu.SMEM)


def vmem():
    return pl.BlockSpec(memory_space=pltpu.VMEM)


def hbm():
    return pl.BlockSpec(memory_space=pltpu.HBM)


def anywhere():
    return pl.BlockSpec(memory_space=pl.ANY)


def in_hbm(x):
    return pltpu.with_memory_space_constraint(x, pltpu.HBM)


def in_vmem(x):
    return pltpu.with_memory_space_constraint(x, pltpu.VMEM)


def cot_copies(here_ref, split, cot_ref, buf_ref, sems):
    if not split:
        return [pltpu.make_async_copy(cot_ref, buf_ref, sems.at[0])]
    half = buf_ref.shape[0] // 2
    copies = []
    for i, at in enumerate((here_ref[0], 1 - here_ref[0])):
        rows = pl.ds(pl.multiple_of(at * half, half), half)
        copies.append(pltpu.make_async_copy(cot_ref.at[rows], buf_ref.at[pl.ds(i * half, half)], sems.at[i]))
    return copies


def input_grad_kernel(split, zero_copies, here_ref, _, kept_in, cot_ref, w_ref, res_ref, *refs):
    if split:
        acts_ref, away_ref, acts_t_ref, *refs = refs
    own_ref, owned_ref, kept_cot_ref, kept_res_ref, cot_first_ref, res_first_ref, *refs = refs
    acc_ref, cot_head, w_head, cot_body, w_body, cot_tail, w_tail, zero_ref, *refs = refs
    kept_ref, kept_sem, cot_sem, w_sem, zero_sem, kept_cot_sem, kept_res_sem, first_sem, own_sem, *refs = refs
    zero_rows = zero_ref.shape[0]
    rows, hidden = w_ref.shape
    width = min(256, rows)
    keep = kept_cot_ref.shape[0]
    half = own_ref.shape[0]
    head, chunks, chunk = chunking(hidden)

    def loads(at, size, cot_buf, w_buf, i):
        part = pl.ds(at, size)
        return cot_copies(here_ref, split, cot_ref.at[:, part], cot_buf, cot_sem.at[i]) + [
            pltpu.make_async_copy(w_ref.at[:, part], w_buf, w_sem.at[i])
        ]

    def head_loads():
        return loads(0, head, cot_head, w_head, 0)

    def tail_loads():
        return loads(hidden - head, head, cot_tail, w_tail, 1)

    def body_loads(j):
        return loads(pl.multiple_of(head + j * chunk, BLK), chunk, cot_body.at[j], w_body.at[j], 2 + j)

    def start(copies):
        for copy in copies:
            copy.start()

    def wait(copies):
        for copy in copies:
            copy.wait()

    def side_copies():
        part = pl.ds(0, res_first_ref.shape[1])
        copies = cot_copies(here_ref, split, cot_ref.at[:, part], cot_first_ref, first_sem)
        copies.append(pltpu.make_async_copy(res_ref.at[:, part], res_first_ref, first_sem.at[2]))
        for z in range(zero_copies):
            part = pl.ds(z * zero_rows, zero_rows)
            copies.append(pltpu.make_async_copy(zero_ref, owned_ref.at[part], zero_sem.at[z]))
        for k in range(keep):
            col_blocks = hidden // BLK
            row = pl.ds(pl.multiple_of(kept_ref[k] // col_blocks * BLK, BLK), BLK)
            col = pl.ds(pl.multiple_of(kept_ref[k] % col_blocks * BLK, BLK), BLK)
            copies += cot_copies(here_ref, split, cot_ref.at[:, col], kept_cot_ref.at[k], kept_cot_sem.at[k])
            copies.append(pltpu.make_async_copy(res_ref.at[row, col], kept_res_ref.at[k], kept_res_sem.at[k]))
        return copies

    if split:
        acts_buf, acts_t_buf, away_buf, acts_sem, acts_t_sem, away_sem = refs
        acts_copy = pltpu.make_async_copy(acts_ref, acts_buf, acts_sem)
        acts_t_copy = pltpu.make_async_copy(acts_t_buf, acts_t_ref.at[:, pl.ds(0, half)], acts_t_sem)
        acts_copy.start()
    start(head_loads())
    kept_copy = pltpu.make_async_copy(kept_in, kept_ref, kept_sem)
    kept_copy.start()
    zero_ref[...] = jnp.zeros_like(zero_ref)
    if split:
        acts_copy.wait()
        acts_t_buf[...] = acts_buf[...].T
        acts_t_copy.start()
    start(body_loads(0) if chunks else tail_loads())
    wait(head_loads())
    kept_copy.wait()
    if chunks:
        start(body_loads(1))
    for at in range(0, rows, width):
        cols = slice(at, at + width)
        acc_ref[:, cols] = dot_nt(cot_head[...], w_head[cols, :])

    if chunks:

        @pl.loop(0, chunks)
        def _(j):
            wait(body_loads(j))

            @pl.when(j + 2 < chunks)
            def _():
                start(body_loads(j + 2))

            @pl.when(j + 2 == chunks)
            def _():
                start(tail_loads())
                start(side_copies())

            for at in range(0, rows, width):
                cols = slice(at, at + width)
                acc_ref[:, cols] += dot_nt(cot_body[j], w_body[j, cols, :])

    else:
        start(side_copies())
    wait(tail_loads())
    outputs = []
    for n, at in enumerate(range(0, rows, width)):
        cols = slice(at, at + width)
        total = acc_ref[:, cols] + dot_nt(cot_tail[...], w_tail[cols, :])
        if split:
            own_ref[:, cols] = total[:half]
            away_buf[:, cols] = total[half:].astype(jnp.bfloat16)
            outputs.append(pltpu.make_async_copy(away_buf.at[:, cols], away_ref.at[:, cols], away_sem.at[n]))
        else:
            acc_ref[:, cols] = total
            outputs.append(pltpu.make_async_copy(acc_ref.at[:, cols], own_ref.at[:, cols], own_sem.at[n]))
    start(outputs)
    if split:
        acts_t_copy.wait()
    wait(side_copies())
    wait(outputs)


def input_grad_partials(here, me, kept, cot, weight, residual, owned_count, acts):
    split = acts is not None
    tokens, cols = cot.shape
    rows = weight.shape[0]
    head, chunks, chunk = chunking(cols)
    first = column_chunking(cols)[0]
    keep = kept.shape[0]
    own_rows = tokens // 2 if split else tokens
    zero_rows = min(16, owned_count)
    zero_copies = owned_count // zero_rows
    out_shape = [
        pltpu.VMEM((own_rows, rows), jnp.float32) if split else jax.ShapeDtypeStruct((own_rows, rows), jnp.float32),
        pltpu.HBM((owned_count, BLK, BLK), jnp.float32),
        pltpu.VMEM((keep, tokens, BLK), jnp.bfloat16),
        pltpu.VMEM((keep, BLK, BLK), jnp.bfloat16),
        pltpu.VMEM((tokens, first), jnp.bfloat16),
        pltpu.VMEM((rows, first), jnp.bfloat16),
    ]
    out_specs = [vmem() if split else anywhere(), hbm()] + [vmem()] * 4
    scratch = [
        pltpu.VMEM((tokens, rows), jnp.float32),
        pltpu.VMEM((tokens, head), jnp.bfloat16),
        pltpu.VMEM((rows, head), jnp.bfloat16),
        pltpu.VMEM((max(chunks, 1), tokens, chunk), jnp.bfloat16),
        pltpu.VMEM((max(chunks, 1), rows, chunk), jnp.bfloat16),
        pltpu.VMEM((tokens, head), jnp.bfloat16),
        pltpu.VMEM((rows, head), jnp.bfloat16),
        pltpu.VMEM((zero_rows, BLK, BLK), jnp.float32),
        pltpu.SMEM(kept.shape, jnp.int32),
        pltpu.SemaphoreType.DMA,
        pltpu.SemaphoreType.DMA((chunks + 2, 2)),
        pltpu.SemaphoreType.DMA((chunks + 2,)),
        pltpu.SemaphoreType.DMA((zero_copies,)),
        pltpu.SemaphoreType.DMA((keep, 2)),
        pltpu.SemaphoreType.DMA((keep,)),
        pltpu.SemaphoreType.DMA((3,)),
        pltpu.SemaphoreType.DMA((4,)),
    ]
    if split:
        out_shape = [
            jax.ShapeDtypeStruct((own_rows, rows), jnp.bfloat16),
            pltpu.VMEM((rows, tokens), jnp.bfloat16),
        ] + out_shape
        out_specs = [anywhere(), vmem()] + out_specs
        scratch += [
            pltpu.VMEM(acts.shape, jnp.bfloat16),
            pltpu.VMEM((rows, own_rows), jnp.bfloat16),
            pltpu.VMEM((own_rows, rows), jnp.bfloat16),
            pltpu.SemaphoreType.DMA,
            pltpu.SemaphoreType.DMA,
            pltpu.SemaphoreType.DMA((4,)),
        ]
    return pl.pallas_call(
        functools.partial(input_grad_kernel, split, zero_copies),
        out_shape=out_shape,
        in_specs=[smem()] * 2 + [hbm()] * (4 + split),
        out_specs=out_specs,
        scratch_shapes=scratch,
        compiler_params=params(43),
        cost_estimate=cost(2 * tokens * rows * cols, 2 * cols * (tokens + rows) + 4 * owned_count * BLK * BLK),
        name="input_grad_partials",
    )(here, me, in_hbm(kept), in_hbm(cot), in_hbm(weight), in_hbm(residual), *([in_hbm(acts)] if split else []))


def kept_kernel(pair, col_blocks, kept_ref, step_ref, *refs):
    if pair:
        _, *refs = refs
    act_ref, cot_ref, res_ref, acts_t_ref, out_ref = refs
    keep = cot_ref.shape[0]
    acts_t_ref[:, acts_t_ref.shape[1] - act_ref.shape[0] :] = act_ref[...].T
    for k in range(keep):
        row = pl.ds(pl.multiple_of(kept_ref[k] // col_blocks * BLK, BLK), BLK)
        gradient = dot_nn(acts_t_ref[row, :], cot_ref[k])
        out_ref[k * BLK : (k + 1) * BLK, :] = (res_ref[k].astype(jnp.float32) + step_ref[0] * gradient).astype(
            jnp.bfloat16
        )
    lane = lax.broadcasted_iota(jnp.int32, (LABEL_ROWS, BLK), 1) % keep
    low = lax.broadcasted_iota(jnp.int32, (LABEL_ROWS, BLK), 0) % 2 == 1
    label = jnp.zeros((LABEL_ROWS, BLK), jnp.int32)
    for k in range(keep):
        digit = jnp.where(low, kept_ref[k] % RADIX, kept_ref[k] // RADIX)
        label = jnp.where(lane == k, digit, label)
    out_ref[keep * BLK :, :] = label.astype(jnp.float32).astype(jnp.bfloat16)


def kept_blocks_of(kept, step_size, acts_t, act, kept_cot, kept_res, col_blocks):
    rows = act.shape[1]
    keep, tokens = kept_cot.shape[:2]
    pair = acts_t is not None
    return pl.pallas_call(
        functools.partial(kept_kernel, pair, col_blocks),
        out_shape=[
            pltpu.VMEM((rows, tokens), jnp.bfloat16),
            jax.ShapeDtypeStruct((keep * BLK + LABEL_ROWS, BLK), jnp.bfloat16),
        ],
        in_specs=[smem()] * 2 + [vmem()] * (3 + pair),
        out_specs=[vmem(), vmem()],
        input_output_aliases={2: 0} if pair else {},
        compiler_params=params(4),
        cost_estimate=cost(2 * tokens * BLK * BLK * keep, 4 * tokens * rows + 2 * keep * tokens * BLK),
        name="kept_blocks",
    )(kept, step_size, *([in_vmem(acts_t)] if pair else []), in_vmem(act), in_vmem(kept_cot), in_vmem(kept_res))


def residual_kernel(split, here_ref, step_ref, acts_t_ref, cot_first, res_first, cot_ref, res_ref, out_ref, *refs):
    first_out, cot_body, res_body, cot_tail, res_tail, cot_sem, res_sem, out_sem = refs
    step = step_ref[0]
    first, chunks, chunk, tails = column_chunking(cot_ref.shape[1])

    def loads(at, cot_buf, res_buf, i):
        part = pl.ds(at, res_buf.shape[1])
        return cot_copies(here_ref, split, cot_ref.at[:, part], cot_buf, cot_sem.at[i]) + [
            pltpu.make_async_copy(res_ref.at[:, part], res_buf, res_sem.at[i])
        ]

    def store(at, res_buf, i):
        return pltpu.make_async_copy(res_buf, out_ref.at[:, pl.ds(at, res_buf.shape[1])], out_sem.at[i])

    def body_at(j):
        return pl.multiple_of(first + j * chunk, BLK)

    def body_loads(j):
        return loads(body_at(j), cot_body.at[j], res_body.at[j], j)

    def body_store(j):
        return store(body_at(j), res_body.at[j], j)

    def tail_at(t):
        return first + chunks * chunk + sum(tails[:t])

    def tail_loads(t):
        return loads(tail_at(t), cot_tail.at[t], res_tail.at[t], chunks + t)

    def tail_store(t):
        return store(tail_at(t), res_tail.at[t], chunks + t)

    def start(copies):
        for copy in copies:
            copy.start()

    def wait(copies):
        for copy in copies:
            copy.wait()

    def start_tails():
        for t in range(len(tails)):
            start(tail_loads(t))

    def work(cot_buf, res_buf, out_buf):
        size = res_buf.shape[1]
        width = min(256, size)
        for at in range(0, size, width):
            part = slice(at, at + width)
            gradient = dot_nn(acts_t_ref[...], cot_buf[:, part])
            out_buf[:, part] = (res_buf[:, part].astype(jnp.float32) + step * gradient).astype(jnp.bfloat16)

    if chunks:
        start(body_loads(0))
    else:
        start_tails()
    work(cot_first, res_first, first_out)
    first_store = store(0, first_out, chunks + len(tails))
    first_store.start()

    if chunks:
        start(body_loads(1))

        @pl.loop(0, chunks)
        def _(j):
            wait(body_loads(j))

            @pl.when(j + 2 < chunks)
            def _():
                start(body_loads(j + 2))

            @pl.when(j + 2 == chunks)
            def _():
                start_tails()

            work(cot_body.at[j], res_body.at[j], res_body.at[j])
            body_store(j).start()

    for t in range(len(tails)):
        wait(tail_loads(t))
        work(cot_tail.at[t], res_tail.at[t], res_tail.at[t])
        tail_store(t).start()
    first_store.wait()
    for j in range(chunks):
        body_store(j).wait()
    for t in range(len(tails)):
        tail_store(t).wait()


def residual_of(here, step_size, acts_t, cot_first, res_first, cot, residual, split):
    tokens, cols = cot.shape
    rows = residual.shape[0]
    first, chunks, chunk, tails = column_chunking(cols)
    parts = chunks + len(tails)
    return pl.pallas_call(
        functools.partial(residual_kernel, split),
        out_shape=pltpu.HBM((rows, cols), jnp.bfloat16),
        in_specs=[smem()] * 2 + [vmem()] * 3 + [hbm()] * 2,
        out_specs=hbm(),
        scratch_shapes=[
            pltpu.VMEM((rows, first), jnp.bfloat16),
            pltpu.VMEM((max(chunks, 1), tokens, chunk), jnp.bfloat16),
            pltpu.VMEM((max(chunks, 1), rows, chunk), jnp.bfloat16),
            pltpu.VMEM((len(tails), tokens, tails[0]), jnp.bfloat16),
            pltpu.VMEM((len(tails), rows, tails[0]), jnp.bfloat16),
            pltpu.SemaphoreType.DMA((parts, 2)),
            pltpu.SemaphoreType.DMA((parts,)),
            pltpu.SemaphoreType.DMA((parts + 1,)),
        ],
        compiler_params=params(36),
        cost_estimate=cost(2 * tokens * rows * cols, 2 * tokens * (rows + cols) + 4 * rows * cols),
        name="residual_out",
    )(
        here,
        step_size,
        in_vmem(acts_t),
        in_vmem(cot_first),
        in_vmem(res_first),
        in_hbm(cot),
        in_hbm(residual),
    )


def finish_kernel(groups, keep, pair, col_blocks, me_ref, kept_ref, *refs):
    if pair:
        own_ref, arrived_ref, *refs = refs
    block_refs = refs[:groups]
    refs = refs[groups + 2 :]
    if pair:
        grad_ref, *refs = refs
    out_ref, res_ref, sum_ref, table_ref, scalar_ref, zero_ref, sem, table_sem, zero_sem, *refs = refs
    total = groups * keep
    me = me_ref[0]

    zero_ref[...] = jnp.zeros_like(zero_ref)
    zero_copies = []
    for k in range(keep):
        at = pl.multiple_of(kept_ref[k] // col_blocks * BLK, BLK)
        col = pl.multiple_of(kept_ref[k] % col_blocks * BLK, BLK)
        zero_copies.append(
            pltpu.make_async_copy(zero_ref, res_ref.at[pl.ds(at, BLK), pl.ds(col, BLK)], zero_sem.at[k])
        )
        zero_copies[k].start()

    row = lax.broadcasted_iota(jnp.int32, (total, BLK), 0)
    lane = lax.broadcasted_iota(jnp.int32, (total, BLK), 1)
    numbers = jnp.full((total, BLK), -1, jnp.int32)
    for g, block_ref in enumerate(block_refs):
        digits = block_ref[keep * BLK :, :].astype(jnp.float32).astype(jnp.int32)
        numbers = jnp.where(lane // keep == g, digits[0:1, :] * RADIX + digits[1:2, :], numbers)
    numbers = numbers.astype(jnp.float32)
    number = jnp.sum(jnp.where(lane == row, numbers, 0.0), axis=1, keepdims=True)
    first = jnp.min(jnp.where(numbers == number, lane.astype(jnp.float32), float(BLK)), axis=1, keepdims=True)
    final = jnp.max(jnp.where(numbers == number, lane.astype(jnp.float32), -1.0), axis=1, keepdims=True)
    number = jnp.broadcast_to(number, (total, BLK)).astype(jnp.int32)
    first = jnp.broadcast_to(first, (total, BLK)).astype(jnp.int32)
    first = jnp.where(number % groups == me, first, -1)
    final = jnp.broadcast_to(final, (total, BLK)).astype(jnp.int32)
    table_ref[...] = jnp.where(lane == 0, first, jnp.where(lane == 1, number // groups, final))
    table = pltpu.make_async_copy(table_ref, scalar_ref, table_sem)
    table.start()

    grad_copies = []
    if pair:
        grad_buf, grad_sem = refs
        size = grad_buf.shape[0] // grad_sem.shape[0]
        for c in range(grad_sem.shape[0]):
            part = slice(c * size, (c + 1) * size)
            grad_buf[part, :] = (own_ref[part, :] + arrived_ref[part, :].astype(jnp.float32)).astype(jnp.bfloat16)
            grad_copies.append(pltpu.make_async_copy(grad_buf.at[part, :], grad_ref.at[part, :], grad_sem.at[c]))
            grad_copies[c].start()

    table.wait()

    def copy(i):
        return pltpu.make_async_copy(sum_ref.at[i], out_ref.at[scalar_ref[i, 1]], sem.at[i])

    def block(i):
        at = i % keep * BLK
        return block_refs[i // keep][at : at + BLK, :].astype(jnp.float32)

    for i in range(total):
        slot = scalar_ref[i, 0]

        @pl.when(slot >= 0)
        def _(i=i, slot=slot):
            @pl.when(slot == i)
            def _():
                sum_ref[i] = block(i)

            if i >= keep:

                @pl.when(slot < i)
                def _():
                    sum_ref[slot] += block(i)

            @pl.when(scalar_ref[i, 2] == i)
            def _():
                copy(slot).start()

    for done in zero_copies + grad_copies:
        done.wait()
    for i in range(total):

        @pl.when(scalar_ref[i, 0] == i)
        def _(i=i):
            copy(i).wait()


def finish(me, kept, parts, blocks, zeros, residual):
    groups = len(blocks)
    keep = kept.shape[0]
    out_shape = [pltpu.HBM(a.shape, a.dtype) for a in (zeros, residual)]
    out_specs = [hbm(), hbm()]
    scratch = [
        pltpu.VMEM((groups * keep, BLK, BLK), jnp.float32),
        pltpu.VMEM((groups * keep, BLK), jnp.int32),
        pltpu.SMEM((groups * keep, BLK), jnp.int32),
        pltpu.VMEM((BLK, BLK), jnp.bfloat16),
        pltpu.SemaphoreType.DMA((groups * keep,)),
        pltpu.SemaphoreType.DMA,
        pltpu.SemaphoreType.DMA((keep,)),
    ]
    if parts:
        out_shape.insert(0, pltpu.HBM(parts[0].shape, jnp.bfloat16))
        out_specs.insert(0, hbm())
        scratch += [pltpu.VMEM(parts[0].shape, jnp.bfloat16), pltpu.SemaphoreType.DMA((4,))]
        parts = [in_vmem(parts[0]), parts[1]]
    first = 2 + len(parts) + groups
    return pl.pallas_call(
        functools.partial(finish_kernel, groups, keep, bool(parts), residual.shape[1] // BLK),
        out_shape=out_shape,
        in_specs=[smem(), smem()] + [vmem()] * (len(parts) + groups) + [hbm(), hbm()],
        out_specs=out_specs,
        scratch_shapes=scratch,
        input_output_aliases={first: len(out_shape) - 2, first + 1: len(out_shape) - 1},
        compiler_params=params(10),
        cost_estimate=cost(groups * keep * BLK * BLK, groups * keep * BLK * BLK * 8),
        name="finish",
    )(me, kept, *parts, *blocks, in_hbm(zeros), in_hbm(residual))


def swapped(x, axis, mask):
    return lax.ppermute(x, axis, [(i, i ^ mask) for i in range(lax.axis_size(axis))])


def of_all_groups(x):
    return [x] + [swapped(x, "dp", mask) for mask in range(1, lax.axis_size("dp"))]


def body(activations, cotangent, weight, residual, step_size, kept_blocks):
    rows, cols = weight.shape
    groups = lax.axis_size("dp")
    owned_count = (rows // BLK) * (cols // BLK) // groups
    kept = kept_blocks.reshape(-1)
    me = lax.axis_index("dp").astype(jnp.int32).reshape(1)
    here = lax.axis_index("tensor").astype(jnp.int32).reshape(1)
    pair = lax.axis_size("tensor") == 2
    if pair:
        act = swapped(activations, "tensor", 1)
        away, acts_t, own, zeros, kept_cot, kept_res, cot_first, res_first = input_grad_partials(
            here, me, kept, cotangent, weight, residual[0], owned_count, activations
        )
        parts = [own, swapped(away, "tensor", 1)]
    else:
        act = lax.all_gather(activations, "tensor", axis=0, tiled=True)
        acts_t = None
        own, zeros, kept_cot, kept_res, cot_first, res_first = input_grad_partials(
            here, me, kept, cotangent, weight, residual[0], owned_count, None
        )
        summed = lax.psum_scatter(own, "tensor", scatter_dimension=0, tiled=True)
        parts = []
    acts_t, blocks = kept_blocks_of(kept, step_size, acts_t, act, kept_cot, kept_res, cols // BLK)
    all_blocks = of_all_groups(blocks)
    rounded = residual_of(here, step_size, acts_t, cot_first, res_first, cotangent, residual[0], pair)
    *grads, owned, residual_out = finish(me, kept, parts, all_blocks, zeros, rounded)
    input_grad = grads[0] if pair else summed.astype(jnp.bfloat16)
    return (input_grad, residual_out[None], owned.reshape(1, 1, 1, owned_count, BLK, BLK))


def solution(mesh):
    in_specs = (
        P(("dp", "tensor"), "fsdp"),
        P("dp", "tensor"),
        P("fsdp", "tensor"),
        P("dp", "fsdp", "tensor"),
        P(),
        P("dp", "fsdp", "tensor", None),
    )
    out_specs = (
        P(("dp", "tensor"), "fsdp"),
        P("dp", "fsdp", "tensor"),
        P("dp", "fsdp", "tensor", None, None, None),
    )
    return jax.shard_map(body, mesh=mesh, in_specs=in_specs, out_specs=out_specs, check_vma=False)
```

```python
import functools

import jax
import jax.numpy as jnp
from jax import lax
from jax.experimental import pallas as pl
from jax.experimental.pallas import tpu as pltpu
from jax.sharding import PartitionSpec as P

BLK = 128
MIB = 1024 * 1024
LABEL_ROWS = 16
RADIX = 16


def cost(flops, nbytes):
    return pl.CostEstimate(flops=flops, bytes_accessed=nbytes, transcendentals=0)


def params(mib=62):
    return pltpu.CompilerParams(vmem_limit_bytes=mib * MIB)


def dot_nt(a, b):
    return lax.dot_general(a, b, (((1,), (1,)), ((), ())), preferred_element_type=jnp.float32)


def dot_nn(a, b):
    return lax.dot_general(a, b, (((1,), (0,)), ((), ())), preferred_element_type=jnp.float32)


def chunking(cols):
    if cols < 8192:
        return cols // 2, 0, cols // 2
    return 1024, cols // 2048 - 1, 2048


def smem():
    return pl.BlockSpec(memory_space=pltpu.SMEM)


def vmem():
    return pl.BlockSpec(memory_space=pltpu.VMEM)


def hbm():
    return pl.BlockSpec(memory_space=pltpu.HBM)


def anywhere():
    return pl.BlockSpec(memory_space=pl.ANY)


def in_hbm(x):
    return pltpu.with_memory_space_constraint(x, pltpu.HBM)


def in_vmem(x):
    return pltpu.with_memory_space_constraint(x, pltpu.VMEM)


def cot_copies(here_ref, split, cot_ref, buf_ref, sems):
    if not split:
        return [pltpu.make_async_copy(cot_ref, buf_ref, sems.at[0])]
    half = buf_ref.shape[0] // 2
    copies = []
    for i, at in enumerate((here_ref[0], 1 - here_ref[0])):
        rows = pl.ds(pl.multiple_of(at * half, half), half)
        copies.append(pltpu.make_async_copy(cot_ref.at[rows], buf_ref.at[pl.ds(i * half, half)], sems.at[i]))
    return copies


def input_grad_kernel(split, zero_copies, here_ref, _, kept_in, cot_ref, w_ref, res_ref, *refs):
    if split:
        acts_ref, away_ref, acts_t_ref, *refs = refs
    own_ref, owned_ref, kept_cot_ref, kept_res_ref, *refs = refs
    acc_ref, cot_head, w_head, cot_body, w_body, cot_tail, w_tail, zero_ref, *refs = refs
    kept_ref, kept_sem, cot_sem, w_sem, zero_sem, kept_cot_sem, kept_res_sem, own_sem, *refs = refs
    zero_rows = zero_ref.shape[0]
    rows, hidden = w_ref.shape
    width = min(256, rows)
    keep = kept_cot_ref.shape[0]
    half = own_ref.shape[0]
    head, chunks, chunk = chunking(hidden)

    def loads(at, size, cot_buf, w_buf, i):
        part = pl.ds(at, size)
        return cot_copies(here_ref, split, cot_ref.at[:, part], cot_buf, cot_sem.at[i]) + [
            pltpu.make_async_copy(w_ref.at[:, part], w_buf, w_sem.at[i])
        ]

    def head_loads():
        return loads(0, head, cot_head, w_head, 0)

    def tail_loads():
        return loads(hidden - head, head, cot_tail, w_tail, 1)

    def body_loads(j):
        return loads(pl.multiple_of(head + j * chunk, BLK), chunk, cot_body.at[j], w_body.at[j], 2 + j)

    def start(copies):
        for copy in copies:
            copy.start()

    def wait(copies):
        for copy in copies:
            copy.wait()

    def side_copies():
        copies = []
        for z in range(zero_copies):
            part = pl.ds(z * zero_rows, zero_rows)
            copies.append(pltpu.make_async_copy(zero_ref, owned_ref.at[part], zero_sem.at[z]))
        for k in range(keep):
            col_blocks = hidden // BLK
            row = pl.ds(pl.multiple_of(kept_ref[k] // col_blocks * BLK, BLK), BLK)
            col = pl.ds(pl.multiple_of(kept_ref[k] % col_blocks * BLK, BLK), BLK)
            copies += cot_copies(here_ref, split, cot_ref.at[:, col], kept_cot_ref.at[k], kept_cot_sem.at[k])
            copies.append(pltpu.make_async_copy(res_ref.at[row, col], kept_res_ref.at[k], kept_res_sem.at[k]))
        return copies

    if split:
        acts_buf, acts_t_buf, away_buf, acts_sem, acts_t_sem, away_sem = refs
        acts_copy = pltpu.make_async_copy(acts_ref, acts_buf, acts_sem)
        acts_t_copy = pltpu.make_async_copy(acts_t_buf, acts_t_ref.at[:, pl.ds(0, half)], acts_t_sem)
        acts_copy.start()
    start(head_loads())
    kept_copy = pltpu.make_async_copy(kept_in, kept_ref, kept_sem)
    kept_copy.start()
    zero_ref[...] = jnp.zeros_like(zero_ref)
    if split:
        acts_copy.wait()
        acts_t_buf[...] = acts_buf[...].T
        acts_t_copy.start()
    start(body_loads(0) if chunks else tail_loads())
    wait(head_loads())
    kept_copy.wait()
    if chunks:
        start(body_loads(1))
    for at in range(0, rows, width):
        cols = slice(at, at + width)
        acc_ref[:, cols] = dot_nt(cot_head[...], w_head[cols, :])

    if chunks:

        @pl.loop(0, chunks)
        def _(j):
            wait(body_loads(j))

            @pl.when(j + 2 < chunks)
            def _():
                start(body_loads(j + 2))

            @pl.when(j + 2 == chunks)
            def _():
                start(tail_loads())
                start(side_copies())

            for at in range(0, rows, width):
                cols = slice(at, at + width)
                acc_ref[:, cols] += dot_nt(cot_body[j], w_body[j, cols, :])

    else:
        start(side_copies())
    wait(tail_loads())
    outputs = []
    for n, at in enumerate(range(0, rows, width)):
        cols = slice(at, at + width)
        total = acc_ref[:, cols] + dot_nt(cot_tail[...], w_tail[cols, :])
        if split:
            own_ref[:, cols] = total[:half]
            away_buf[:, cols] = total[half:].astype(jnp.bfloat16)
            outputs.append(pltpu.make_async_copy(away_buf.at[:, cols], away_ref.at[:, cols], away_sem.at[n]))
        else:
            acc_ref[:, cols] = total
            outputs.append(pltpu.make_async_copy(acc_ref.at[:, cols], own_ref.at[:, cols], own_sem.at[n]))
    start(outputs)
    if split:
        acts_t_copy.wait()
    wait(side_copies())
    wait(outputs)


def input_grad_partials(here, me, kept, cot, weight, residual, owned_count, acts):
    split = acts is not None
    tokens, cols = cot.shape
    rows = weight.shape[0]
    head, chunks, chunk = chunking(cols)
    keep = kept.shape[0]
    own_rows = tokens // 2 if split else tokens
    zero_rows = min(16, owned_count)
    zero_copies = owned_count // zero_rows
    out_shape = [
        pltpu.VMEM((own_rows, rows), jnp.float32) if split else jax.ShapeDtypeStruct((own_rows, rows), jnp.float32),
        pltpu.HBM((owned_count, BLK, BLK), jnp.float32),
        pltpu.VMEM((keep, tokens, BLK), jnp.bfloat16),
        pltpu.VMEM((keep, BLK, BLK), jnp.bfloat16),
    ]
    out_specs = [vmem() if split else anywhere(), hbm()] + [vmem()] * 2
    scratch = [
        pltpu.VMEM((tokens, rows), jnp.float32),
        pltpu.VMEM((tokens, head), jnp.bfloat16),
        pltpu.VMEM((rows, head), jnp.bfloat16),
        pltpu.VMEM((max(chunks, 1), tokens, chunk), jnp.bfloat16),
        pltpu.VMEM((max(chunks, 1), rows, chunk), jnp.bfloat16),
        pltpu.VMEM((tokens, head), jnp.bfloat16),
        pltpu.VMEM((rows, head), jnp.bfloat16),
        pltpu.VMEM((zero_rows, BLK, BLK), jnp.float32),
        pltpu.SMEM(kept.shape, jnp.int32),
        pltpu.SemaphoreType.DMA,
        pltpu.SemaphoreType.DMA((chunks + 2, 2)),
        pltpu.SemaphoreType.DMA((chunks + 2,)),
        pltpu.SemaphoreType.DMA((zero_copies,)),
        pltpu.SemaphoreType.DMA((keep, 2)),
        pltpu.SemaphoreType.DMA((keep,)),
        pltpu.SemaphoreType.DMA((4,)),
    ]
    if split:
        out_shape = [
            jax.ShapeDtypeStruct((own_rows, rows), jnp.bfloat16),
            pltpu.VMEM((rows, tokens), jnp.bfloat16),
        ] + out_shape
        out_specs = [anywhere(), vmem()] + out_specs
        scratch += [
            pltpu.VMEM(acts.shape, jnp.bfloat16),
            pltpu.VMEM((rows, own_rows), jnp.bfloat16),
            pltpu.VMEM((own_rows, rows), jnp.bfloat16),
            pltpu.SemaphoreType.DMA,
            pltpu.SemaphoreType.DMA,
            pltpu.SemaphoreType.DMA((4,)),
        ]
    return pl.pallas_call(
        functools.partial(input_grad_kernel, split, zero_copies),
        out_shape=out_shape,
        in_specs=[smem()] * 2 + [hbm()] * (4 + split),
        out_specs=out_specs,
        scratch_shapes=scratch,
        compiler_params=params(43),
        cost_estimate=cost(2 * tokens * rows * cols, 2 * cols * (tokens + rows) + 4 * owned_count * BLK * BLK),
        name="input_grad_partials",
    )(here, me, in_hbm(kept), in_hbm(cot), in_hbm(weight), in_hbm(residual), *([in_hbm(acts)] if split else []))


def kept_kernel(pair, col_blocks, here_ref, kept_ref, step_ref, cot_in, res_in, *refs):
    if pair:
        _, *refs = refs
    act_ref, cot_ref, res_ref, acts_t_ref, out_ref, cot_first, res_first, first_sem = refs
    keep = cot_ref.shape[0]
    part = pl.ds(0, res_first.shape[1])
    copies = cot_copies(here_ref, pair, cot_in.at[:, part], cot_first, first_sem)
    copies.append(pltpu.make_async_copy(res_in.at[:, part], res_first, first_sem.at[2]))
    for copy in copies:
        copy.start()
    acts_t_ref[:, acts_t_ref.shape[1] - act_ref.shape[0] :] = act_ref[...].T
    for k in range(keep):
        row = pl.ds(pl.multiple_of(kept_ref[k] // col_blocks * BLK, BLK), BLK)
        gradient = dot_nn(acts_t_ref[row, :], cot_ref[k])
        out_ref[k * BLK : (k + 1) * BLK, :] = (res_ref[k].astype(jnp.float32) + step_ref[0] * gradient).astype(
            jnp.bfloat16
        )
    lane = lax.broadcasted_iota(jnp.int32, (LABEL_ROWS, BLK), 1) % keep
    low = lax.broadcasted_iota(jnp.int32, (LABEL_ROWS, BLK), 0) % 2 == 1
    label = jnp.zeros((LABEL_ROWS, BLK), jnp.int32)
    for k in range(keep):
        digit = jnp.where(low, kept_ref[k] % RADIX, kept_ref[k] // RADIX)
        label = jnp.where(lane == k, digit, label)
    out_ref[keep * BLK :, :] = label.astype(jnp.float32).astype(jnp.bfloat16)
    for copy in copies:
        copy.wait()


def kept_blocks_of(here, kept, step_size, cot, residual, acts_t, act, kept_cot, kept_res):
    rows, cols = residual.shape
    first = chunking(cols)[0]
    keep, tokens = kept_cot.shape[:2]
    pair = acts_t is not None
    return pl.pallas_call(
        functools.partial(kept_kernel, pair, cols // BLK),
        out_shape=[
            pltpu.VMEM((rows, tokens), jnp.bfloat16),
            jax.ShapeDtypeStruct((keep * BLK + LABEL_ROWS, BLK), jnp.bfloat16),
            pltpu.VMEM((tokens, first), jnp.bfloat16),
            pltpu.VMEM((rows, first), jnp.bfloat16),
        ],
        in_specs=[smem()] * 3 + [hbm()] * 2 + [vmem()] * (3 + pair),
        out_specs=[vmem()] * 4,
        scratch_shapes=[pltpu.SemaphoreType.DMA((3,))],
        input_output_aliases={5: 0} if pair else {},
        compiler_params=params(4),
        cost_estimate=cost(2 * tokens * BLK * BLK * keep, 4 * tokens * rows + 2 * keep * tokens * BLK),
        name="kept_blocks",
    )(
        here,
        kept,
        step_size,
        in_hbm(cot),
        in_hbm(residual),
        *([in_vmem(acts_t)] if pair else []),
        in_vmem(act),
        in_vmem(kept_cot),
        in_vmem(kept_res),
    )


def residual_kernel(split, here_ref, step_ref, acts_t_ref, cot_first, res_first, cot_ref, res_ref, out_ref, *refs):
    first_out, cot_body, res_body, cot_tail, res_tail, cot_sem, res_sem, out_sem = refs
    step = step_ref[0]
    first, chunks, chunk = chunking(cot_ref.shape[1])
    tails = [first]

    def loads(at, cot_buf, res_buf, i):
        part = pl.ds(at, res_buf.shape[1])
        return cot_copies(here_ref, split, cot_ref.at[:, part], cot_buf, cot_sem.at[i]) + [
            pltpu.make_async_copy(res_ref.at[:, part], res_buf, res_sem.at[i])
        ]

    def store(at, res_buf, i):
        return pltpu.make_async_copy(res_buf, out_ref.at[:, pl.ds(at, res_buf.shape[1])], out_sem.at[i])

    def body_at(j):
        return pl.multiple_of(first + j * chunk, BLK)

    def body_loads(j):
        return loads(body_at(j), cot_body.at[j], res_body.at[j], j)

    def body_store(j):
        return store(body_at(j), res_body.at[j], j)

    def tail_at(t):
        return first + chunks * chunk + sum(tails[:t])

    def tail_loads(t):
        return loads(tail_at(t), cot_tail.at[t], res_tail.at[t], chunks + t)

    def tail_store(t):
        return store(tail_at(t), res_tail.at[t], chunks + t)

    def start(copies):
        for copy in copies:
            copy.start()

    def wait(copies):
        for copy in copies:
            copy.wait()

    def start_tails():
        for t in range(len(tails)):
            start(tail_loads(t))

    def work(cot_buf, res_buf, out_buf):
        size = res_buf.shape[1]
        width = min(256, size)
        for at in range(0, size, width):
            part = slice(at, at + width)
            gradient = dot_nn(acts_t_ref[...], cot_buf[:, part])
            out_buf[:, part] = (res_buf[:, part].astype(jnp.float32) + step * gradient).astype(jnp.bfloat16)

    if chunks:
        start(body_loads(0))
    else:
        start_tails()
    work(cot_first, res_first, first_out)
    first_store = store(0, first_out, chunks + len(tails))
    first_store.start()

    if chunks:
        start(body_loads(1))

        @pl.loop(0, chunks)
        def _(j):
            wait(body_loads(j))

            @pl.when(j + 2 < chunks)
            def _():
                start(body_loads(j + 2))

            @pl.when(j + 2 == chunks)
            def _():
                start_tails()

            work(cot_body.at[j], res_body.at[j], res_body.at[j])
            body_store(j).start()

    for t in range(len(tails)):
        wait(tail_loads(t))
        work(cot_tail.at[t], res_tail.at[t], res_tail.at[t])
        tail_store(t).start()
    first_store.wait()
    for j in range(chunks):
        body_store(j).wait()
    for t in range(len(tails)):
        tail_store(t).wait()


def residual_of(here, step_size, acts_t, cot_first, res_first, cot, residual, split):
    tokens, cols = cot.shape
    rows = residual.shape[0]
    first, chunks, chunk = chunking(cols)
    tails = [first]
    parts = chunks + len(tails)
    return pl.pallas_call(
        functools.partial(residual_kernel, split),
        out_shape=pltpu.HBM((rows, cols), jnp.bfloat16),
        in_specs=[smem()] * 2 + [vmem()] * 3 + [hbm()] * 2,
        out_specs=hbm(),
        scratch_shapes=[
            pltpu.VMEM((rows, first), jnp.bfloat16),
            pltpu.VMEM((max(chunks, 1), tokens, chunk), jnp.bfloat16),
            pltpu.VMEM((max(chunks, 1), rows, chunk), jnp.bfloat16),
            pltpu.VMEM((len(tails), tokens, tails[0]), jnp.bfloat16),
            pltpu.VMEM((len(tails), rows, tails[0]), jnp.bfloat16),
            pltpu.SemaphoreType.DMA((parts, 2)),
            pltpu.SemaphoreType.DMA((parts,)),
            pltpu.SemaphoreType.DMA((parts + 1,)),
        ],
        compiler_params=params(36),
        cost_estimate=cost(2 * tokens * rows * cols, 2 * tokens * (rows + cols) + 4 * rows * cols),
        name="residual_out",
    )(
        here,
        step_size,
        in_vmem(acts_t),
        in_vmem(cot_first),
        in_vmem(res_first),
        in_hbm(cot),
        in_hbm(residual),
    )


def finish_kernel(groups, keep, pair, col_blocks, me_ref, kept_ref, *refs):
    if pair:
        own_ref, arrived_ref, *refs = refs
    block_refs = refs[:groups]
    refs = refs[groups + 2 :]
    if pair:
        grad_ref, *refs = refs
    out_ref, res_ref, sum_ref, table_ref, scalar_ref, zero_ref, sem, table_sem, zero_sem, *refs = refs
    total = groups * keep
    me = me_ref[0]

    zero_ref[...] = jnp.zeros_like(zero_ref)
    zero_copies = []
    for k in range(keep):
        at = pl.multiple_of(kept_ref[k] // col_blocks * BLK, BLK)
        col = pl.multiple_of(kept_ref[k] % col_blocks * BLK, BLK)
        zero_copies.append(
            pltpu.make_async_copy(zero_ref, res_ref.at[pl.ds(at, BLK), pl.ds(col, BLK)], zero_sem.at[k])
        )
        zero_copies[k].start()

    row = lax.broadcasted_iota(jnp.int32, (total, BLK), 0)
    lane = lax.broadcasted_iota(jnp.int32, (total, BLK), 1)
    numbers = jnp.full((total, BLK), -1, jnp.int32)
    for g, block_ref in enumerate(block_refs):
        digits = block_ref[keep * BLK :, :].astype(jnp.float32).astype(jnp.int32)
        numbers = jnp.where(lane // keep == g, digits[0:1, :] * RADIX + digits[1:2, :], numbers)
    numbers = numbers.astype(jnp.float32)
    number = jnp.sum(jnp.where(lane == row, numbers, 0.0), axis=1, keepdims=True)
    first = jnp.min(jnp.where(numbers == number, lane.astype(jnp.float32), float(BLK)), axis=1, keepdims=True)
    final = jnp.max(jnp.where(numbers == number, lane.astype(jnp.float32), -1.0), axis=1, keepdims=True)
    number = jnp.broadcast_to(number, (total, BLK)).astype(jnp.int32)
    first = jnp.broadcast_to(first, (total, BLK)).astype(jnp.int32)
    first = jnp.where(number % groups == me, first, -1)
    final = jnp.broadcast_to(final, (total, BLK)).astype(jnp.int32)
    table_ref[...] = jnp.where(lane == 0, first, jnp.where(lane == 1, number // groups, final))
    table = pltpu.make_async_copy(table_ref, scalar_ref, table_sem)
    table.start()

    grad_copies = []
    if pair:
        grad_buf, grad_sem = refs
        size = grad_buf.shape[0] // grad_sem.shape[0]
        for c in range(grad_sem.shape[0]):
            part = slice(c * size, (c + 1) * size)
            grad_buf[part, :] = (own_ref[part, :] + arrived_ref[part, :].astype(jnp.float32)).astype(jnp.bfloat16)
            grad_copies.append(pltpu.make_async_copy(grad_buf.at[part, :], grad_ref.at[part, :], grad_sem.at[c]))
            grad_copies[c].start()

    table.wait()

    def copy(i):
        return pltpu.make_async_copy(sum_ref.at[i], out_ref.at[scalar_ref[i, 1]], sem.at[i])

    def block(i):
        at = i % keep * BLK
        return block_refs[i // keep][at : at + BLK, :].astype(jnp.float32)

    for i in range(total):
        slot = scalar_ref[i, 0]

        @pl.when(slot >= 0)
        def _(i=i, slot=slot):
            @pl.when(slot == i)
            def _():
                sum_ref[i] = block(i)

            if i >= keep:

                @pl.when(slot < i)
                def _():
                    sum_ref[slot] += block(i)

            @pl.when(scalar_ref[i, 2] == i)
            def _():
                copy(slot).start()

    for done in zero_copies + grad_copies:
        done.wait()
    for i in range(total):

        @pl.when(scalar_ref[i, 0] == i)
        def _(i=i):
            copy(i).wait()


def finish(me, kept, parts, blocks, zeros, residual):
    groups = len(blocks)
    keep = kept.shape[0]
    out_shape = [pltpu.HBM(a.shape, a.dtype) for a in (zeros, residual)]
    out_specs = [hbm(), hbm()]
    scratch = [
        pltpu.VMEM((groups * keep, BLK, BLK), jnp.float32),
        pltpu.VMEM((groups * keep, BLK), jnp.int32),
        pltpu.SMEM((groups * keep, BLK), jnp.int32),
        pltpu.VMEM((BLK, BLK), jnp.bfloat16),
        pltpu.SemaphoreType.DMA((groups * keep,)),
        pltpu.SemaphoreType.DMA,
        pltpu.SemaphoreType.DMA((keep,)),
    ]
    if parts:
        out_shape.insert(0, pltpu.HBM(parts[0].shape, jnp.bfloat16))
        out_specs.insert(0, hbm())
        scratch += [pltpu.VMEM(parts[0].shape, jnp.bfloat16), pltpu.SemaphoreType.DMA((4,))]
        parts = [in_vmem(parts[0]), parts[1]]
    first = 2 + len(parts) + groups
    return pl.pallas_call(
        functools.partial(finish_kernel, groups, keep, bool(parts), residual.shape[1] // BLK),
        out_shape=out_shape,
        in_specs=[smem(), smem()] + [vmem()] * (len(parts) + groups) + [hbm(), hbm()],
        out_specs=out_specs,
        scratch_shapes=scratch,
        input_output_aliases={first: len(out_shape) - 2, first + 1: len(out_shape) - 1},
        compiler_params=params(10),
        cost_estimate=cost(groups * keep * BLK * BLK, groups * keep * BLK * BLK * 8),
        name="finish",
    )(me, kept, *parts, *blocks, in_hbm(zeros), in_hbm(residual))


def swapped(x, axis, mask):
    return lax.ppermute(x, axis, [(i, i ^ mask) for i in range(lax.axis_size(axis))])


def of_all_groups(x):
    return [x] + [swapped(x, "dp", mask) for mask in range(1, lax.axis_size("dp"))]


def body(activations, cotangent, weight, residual, step_size, kept_blocks):
    rows, cols = weight.shape
    groups = lax.axis_size("dp")
    owned_count = (rows // BLK) * (cols // BLK) // groups
    kept = kept_blocks.reshape(-1)
    me = lax.axis_index("dp").astype(jnp.int32).reshape(1)
    here = lax.axis_index("tensor").astype(jnp.int32).reshape(1)
    pair = lax.axis_size("tensor") == 2
    if pair:
        act = swapped(activations, "tensor", 1)
        away, acts_t, own, zeros, kept_cot, kept_res = input_grad_partials(
            here, me, kept, cotangent, weight, residual[0], owned_count, activations
        )
        parts = [own, swapped(away, "tensor", 1)]
    else:
        act = lax.all_gather(activations, "tensor", axis=0, tiled=True)
        acts_t = None
        own, zeros, kept_cot, kept_res = input_grad_partials(
            here, me, kept, cotangent, weight, residual[0], owned_count, None
        )
        summed = lax.psum_scatter(own, "tensor", scatter_dimension=0, tiled=True)
        parts = []
    acts_t, blocks, cot_first, res_first = kept_blocks_of(
        here, kept, step_size, cotangent, residual[0], acts_t, act, kept_cot, kept_res
    )
    all_blocks = of_all_groups(blocks)
    rounded = residual_of(here, step_size, acts_t, cot_first, res_first, cotangent, residual[0], pair)
    *grads, owned, residual_out = finish(me, kept, parts, all_blocks, zeros, rounded)
    input_grad = grads[0] if pair else summed.astype(jnp.bfloat16)
    return (input_grad, residual_out[None], owned.reshape(1, 1, 1, owned_count, BLK, BLK))


def solution(mesh):
    in_specs = (
        P(("dp", "tensor"), "fsdp"),
        P("dp", "tensor"),
        P("fsdp", "tensor"),
        P("dp", "fsdp", "tensor"),
        P(),
        P("dp", "fsdp", "tensor", None),
    )
    out_specs = (
        P(("dp", "tensor"), "fsdp"),
        P("dp", "fsdp", "tensor"),
        P("dp", "fsdp", "tensor", None, None, None),
    )
    return jax.shard_map(body, mesh=mesh, in_specs=in_specs, out_specs=out_specs, check_vma=False)
```

```python
import functools

import jax
import jax.numpy as jnp
from jax import lax
from jax.experimental import pallas as pl
from jax.experimental.pallas import tpu as pltpu
from jax.sharding import PartitionSpec as P

BLK = 128
MIB = 1024 * 1024
LABEL_ROWS = 16
RADIX = 16


def cost(flops, nbytes):
    return pl.CostEstimate(flops=flops, bytes_accessed=nbytes, transcendentals=0)


def params(mib=62):
    return pltpu.CompilerParams(vmem_limit_bytes=mib * MIB)


def dot_nt(a, b):
    return lax.dot_general(a, b, (((1,), (1,)), ((), ())), preferred_element_type=jnp.float32)


def dot_nn(a, b):
    return lax.dot_general(a, b, (((1,), (0,)), ((), ())), preferred_element_type=jnp.float32)


def chunking(cols):
    if cols < 8192:
        return cols // 2, 0, cols // 2
    return 1024, cols // 2048 - 1, 2048


def column_chunking(cols):
    if cols < 8192:
        return cols // 2, 0, cols // 2, [cols // 2]
    return 1024, cols // 1024 - 2, 1024, [512, 512]


def smem():
    return pl.BlockSpec(memory_space=pltpu.SMEM)


def vmem():
    return pl.BlockSpec(memory_space=pltpu.VMEM)


def hbm():
    return pl.BlockSpec(memory_space=pltpu.HBM)


def anywhere():
    return pl.BlockSpec(memory_space=pl.ANY)


def in_hbm(x):
    return pltpu.with_memory_space_constraint(x, pltpu.HBM)


def in_vmem(x):
    return pltpu.with_memory_space_constraint(x, pltpu.VMEM)


def row_copies(src_ref, dst_ref, sems, at=0, pieces=4):
    rows = dst_ref.shape[0] // pieces
    copies = []
    for i in range(pieces):
        part = pl.ds(i * rows, rows)
        copies.append(pltpu.make_async_copy(src_ref.at[part], dst_ref.at[part], sems.at[at + i]))
    return copies


def cot_copies(here_ref, split, cot_ref, buf_ref, sems, pieces=4):
    if not split:
        return row_copies(cot_ref, buf_ref, sems, 0, pieces)
    half = buf_ref.shape[0] // 2
    copies = []
    for i, at in enumerate((here_ref[0], 1 - here_ref[0])):
        rows = pl.ds(pl.multiple_of(at * half, half), half)
        copies += row_copies(cot_ref.at[rows], buf_ref.at[pl.ds(i * half, half)], sems, i * pieces // 2, pieces // 2)
    return copies


def input_grad_kernel(split, zero_copies, here_ref, _, kept_in, cot_ref, w_ref, res_ref, *refs):
    if split:
        acts_ref, away_ref, acts_t_ref, *refs = refs
    own_ref, owned_ref, kept_cot_ref, kept_res_ref, cot_first_ref, res_first_ref, *refs = refs
    acc_ref, cot_head, w_head, cot_body, w_body, cot_tail, w_tail, zero_ref, *refs = refs
    kept_ref, kept_sem, cot_sem, w_sem, zero_sem, kept_cot_sem, kept_res_sem, first_sem, own_sem, *refs = refs
    zero_rows = zero_ref.shape[0]
    rows, hidden = w_ref.shape
    width = min(256, rows)
    keep = kept_cot_ref.shape[0]
    half = own_ref.shape[0]
    head, chunks, chunk = chunking(hidden)

    def loads(at, size, cot_buf, w_buf, i):
        part = pl.ds(at, size)
        return cot_copies(here_ref, split, cot_ref.at[:, part], cot_buf, cot_sem.at[i]) + row_copies(
            w_ref.at[:, part], w_buf, w_sem.at[i]
        )

    def head_loads():
        return loads(0, head, cot_head, w_head, 0)

    def tail_loads():
        return loads(hidden - head, head, cot_tail, w_tail, 1)

    def body_loads(j):
        return loads(pl.multiple_of(head + j * chunk, BLK), chunk, cot_body.at[j], w_body.at[j], 2 + j)

    def start(copies):
        for copy in copies:
            copy.start()

    def wait(copies):
        for copy in copies:
            copy.wait()

    def side_copies():
        part = pl.ds(0, res_first_ref.shape[1])
        copies = cot_copies(here_ref, split, cot_ref.at[:, part], cot_first_ref, first_sem)
        copies += row_copies(res_ref.at[:, part], res_first_ref, first_sem, 4)
        for z in range(zero_copies):
            part = pl.ds(z * zero_rows, zero_rows)
            copies.append(pltpu.make_async_copy(zero_ref, owned_ref.at[part], zero_sem.at[z]))
        for k in range(keep):
            col_blocks = hidden // BLK
            row = pl.ds(pl.multiple_of(kept_ref[k] // col_blocks * BLK, BLK), BLK)
            col = pl.ds(pl.multiple_of(kept_ref[k] % col_blocks * BLK, BLK), BLK)
            copies += cot_copies(here_ref, split, cot_ref.at[:, col], kept_cot_ref.at[k], kept_cot_sem.at[k], 2)
            copies.append(pltpu.make_async_copy(res_ref.at[row, col], kept_res_ref.at[k], kept_res_sem.at[k]))
        return copies

    if split:
        acts_buf, acts_t_buf, away_buf, acts_sem, acts_t_sem, away_sem = refs
        acts_copy = pltpu.make_async_copy(acts_ref, acts_buf, acts_sem)
        acts_t_copy = pltpu.make_async_copy(acts_t_buf, acts_t_ref.at[:, pl.ds(0, half)], acts_t_sem)
        acts_copy.start()
    start(head_loads())
    kept_copy = pltpu.make_async_copy(kept_in, kept_ref, kept_sem)
    kept_copy.start()
    zero_ref[...] = jnp.zeros_like(zero_ref)
    if split:
        acts_copy.wait()
        acts_t_buf[...] = acts_buf[...].T
        acts_t_copy.start()
    start(body_loads(0) if chunks else tail_loads())
    wait(head_loads())
    kept_copy.wait()
    if chunks:
        start(body_loads(1))
    for at in range(0, rows, width):
        cols = slice(at, at + width)
        acc_ref[:, cols] = dot_nt(cot_head[...], w_head[cols, :])

    if chunks:

        @pl.loop(0, chunks)
        def _(j):
            wait(body_loads(j))

            @pl.when(j + 2 < chunks)
            def _():
                start(body_loads(j + 2))

            @pl.when(j + 2 == chunks)
            def _():
                start(tail_loads())
                start(side_copies())

            for at in range(0, rows, width):
                cols = slice(at, at + width)
                acc_ref[:, cols] += dot_nt(cot_body[j], w_body[j, cols, :])

    else:
        start(side_copies())
    wait(tail_loads())
    outputs = []
    for n, at in enumerate(range(0, rows, width)):
        cols = slice(at, at + width)
        total = acc_ref[:, cols] + dot_nt(cot_tail[...], w_tail[cols, :])
        if split:
            own_ref[:, cols] = total[:half]
            away_buf[:, cols] = total[half:].astype(jnp.bfloat16)
            outputs.append(pltpu.make_async_copy(away_buf.at[:, cols], away_ref.at[:, cols], away_sem.at[n]))
        else:
            acc_ref[:, cols] = total
            outputs.append(pltpu.make_async_copy(acc_ref.at[:, cols], own_ref.at[:, cols], own_sem.at[n]))
    start(outputs)
    if split:
        acts_t_copy.wait()
    wait(side_copies())
    wait(outputs)


def input_grad_partials(here, me, kept, cot, weight, residual, owned_count, acts):
    split = acts is not None
    tokens, cols = cot.shape
    rows = weight.shape[0]
    head, chunks, chunk = chunking(cols)
    first = column_chunking(cols)[0]
    keep = kept.shape[0]
    own_rows = tokens // 2 if split else tokens
    zero_rows = min(16, owned_count)
    zero_copies = owned_count // zero_rows
    out_shape = [
        pltpu.VMEM((own_rows, rows), jnp.float32) if split else jax.ShapeDtypeStruct((own_rows, rows), jnp.float32),
        pltpu.HBM((owned_count, BLK, BLK), jnp.float32),
        pltpu.VMEM((keep, tokens, BLK), jnp.bfloat16),
        pltpu.VMEM((keep, BLK, BLK), jnp.bfloat16),
        pltpu.VMEM((tokens, first), jnp.bfloat16),
        pltpu.VMEM((rows, first), jnp.bfloat16),
    ]
    out_specs = [vmem() if split else anywhere(), hbm()] + [vmem()] * 4
    scratch = [
        pltpu.VMEM((tokens, rows), jnp.float32),
        pltpu.VMEM((tokens, head), jnp.bfloat16),
        pltpu.VMEM((rows, head), jnp.bfloat16),
        pltpu.VMEM((max(chunks, 1), tokens, chunk), jnp.bfloat16),
        pltpu.VMEM((max(chunks, 1), rows, chunk), jnp.bfloat16),
        pltpu.VMEM((tokens, head), jnp.bfloat16),
        pltpu.VMEM((rows, head), jnp.bfloat16),
        pltpu.VMEM((zero_rows, BLK, BLK), jnp.float32),
        pltpu.SMEM(kept.shape, jnp.int32),
        pltpu.SemaphoreType.DMA,
        pltpu.SemaphoreType.DMA((chunks + 2, 4)),
        pltpu.SemaphoreType.DMA((chunks + 2, 4)),
        pltpu.SemaphoreType.DMA((zero_copies,)),
        pltpu.SemaphoreType.DMA((keep, 2)),
        pltpu.SemaphoreType.DMA((keep,)),
        pltpu.SemaphoreType.DMA((8,)),
        pltpu.SemaphoreType.DMA((4,)),
    ]
    if split:
        out_shape = [
            jax.ShapeDtypeStruct((own_rows, rows), jnp.bfloat16),
            pltpu.VMEM((rows, tokens), jnp.bfloat16),
        ] + out_shape
        out_specs = [anywhere(), vmem()] + out_specs
        scratch += [
            pltpu.VMEM(acts.shape, jnp.bfloat16),
            pltpu.VMEM((rows, own_rows), jnp.bfloat16),
            pltpu.VMEM((own_rows, rows), jnp.bfloat16),
            pltpu.SemaphoreType.DMA,
            pltpu.SemaphoreType.DMA,
            pltpu.SemaphoreType.DMA((4,)),
        ]
    return pl.pallas_call(
        functools.partial(input_grad_kernel, split, zero_copies),
        out_shape=out_shape,
        in_specs=[smem()] * 2 + [hbm()] * (4 + split),
        out_specs=out_specs,
        scratch_shapes=scratch,
        compiler_params=params(43),
        cost_estimate=cost(2 * tokens * rows * cols, 2 * cols * (tokens + rows) + 4 * owned_count * BLK * BLK),
        name="input_grad_partials",
    )(here, me, in_hbm(kept), in_hbm(cot), in_hbm(weight), in_hbm(residual), *([in_hbm(acts)] if split else []))


def kept_kernel(pair, col_blocks, kept_ref, step_ref, *refs):
    if pair:
        _, *refs = refs
    act_ref, cot_ref, res_ref, acts_t_ref, out_ref = refs
    keep = cot_ref.shape[0]
    acts_t_ref[:, acts_t_ref.shape[1] - act_ref.shape[0] :] = act_ref[...].T
    for k in range(keep):
        row = pl.ds(pl.multiple_of(kept_ref[k] // col_blocks * BLK, BLK), BLK)
        gradient = dot_nn(acts_t_ref[row, :], cot_ref[k])
        out_ref[k * BLK : (k + 1) * BLK, :] = (res_ref[k].astype(jnp.float32) + step_ref[0] * gradient).astype(
            jnp.bfloat16
        )
    lane = lax.broadcasted_iota(jnp.int32, (LABEL_ROWS, BLK), 1) % keep
    low = lax.broadcasted_iota(jnp.int32, (LABEL_ROWS, BLK), 0) % 2 == 1
    label = jnp.zeros((LABEL_ROWS, BLK), jnp.int32)
    for k in range(keep):
        digit = jnp.where(low, kept_ref[k] % RADIX, kept_ref[k] // RADIX)
        label = jnp.where(lane == k, digit, label)
    out_ref[keep * BLK :, :] = label.astype(jnp.float32).astype(jnp.bfloat16)


def kept_blocks_of(kept, step_size, acts_t, act, kept_cot, kept_res, col_blocks):
    rows = act.shape[1]
    keep, tokens = kept_cot.shape[:2]
    pair = acts_t is not None
    return pl.pallas_call(
        functools.partial(kept_kernel, pair, col_blocks),
        out_shape=[
            pltpu.VMEM((rows, tokens), jnp.bfloat16),
            jax.ShapeDtypeStruct((keep * BLK + LABEL_ROWS, BLK), jnp.bfloat16),
        ],
        in_specs=[smem()] * 2 + [vmem()] * (3 + pair),
        out_specs=[vmem(), vmem()],
        input_output_aliases={2: 0} if pair else {},
        compiler_params=params(4),
        cost_estimate=cost(2 * tokens * BLK * BLK * keep, 4 * tokens * rows + 2 * keep * tokens * BLK),
        name="kept_blocks",
    )(kept, step_size, *([in_vmem(acts_t)] if pair else []), in_vmem(act), in_vmem(kept_cot), in_vmem(kept_res))


def residual_kernel(split, here_ref, step_ref, acts_t_ref, cot_first, res_first, cot_ref, res_ref, out_ref, *refs):
    first_out, cot_body, res_body, cot_tail, res_tail, cot_sem, res_sem, out_sem = refs
    step = step_ref[0]
    first, chunks, chunk, tails = column_chunking(cot_ref.shape[1])

    def loads(at, cot_buf, res_buf, i):
        part = pl.ds(at, res_buf.shape[1])
        return cot_copies(here_ref, split, cot_ref.at[:, part], cot_buf, cot_sem.at[i]) + row_copies(
            res_ref.at[:, part], res_buf, res_sem.at[i]
        )

    def store(at, res_buf, i):
        return row_copies(res_buf, out_ref.at[:, pl.ds(at, res_buf.shape[1])], out_sem.at[i])

    def body_at(j):
        return pl.multiple_of(first + j * chunk, BLK)

    def body_loads(j):
        return loads(body_at(j), cot_body.at[j], res_body.at[j], j)

    def body_store(j):
        return store(body_at(j), res_body.at[j], j)

    def tail_at(t):
        return first + chunks * chunk + sum(tails[:t])

    def tail_loads(t):
        return loads(tail_at(t), cot_tail.at[t], res_tail.at[t], chunks + t)

    def tail_store(t):
        return store(tail_at(t), res_tail.at[t], chunks + t)

    def start(copies):
        for copy in copies:
            copy.start()

    def wait(copies):
        for copy in copies:
            copy.wait()

    def start_tails():
        for t in range(len(tails)):
            start(tail_loads(t))

    def work(cot_buf, res_buf, out_buf):
        size = res_buf.shape[1]
        width = min(256, size)
        for at in range(0, size, width):
            part = slice(at, at + width)
            gradient = dot_nn(acts_t_ref[...], cot_buf[:, part])
            out_buf[:, part] = (res_buf[:, part].astype(jnp.float32) + step * gradient).astype(jnp.bfloat16)

    if chunks:
        start(body_loads(0))
    else:
        start_tails()
    work(cot_first, res_first, first_out)
    first_store = store(0, first_out, chunks + len(tails))
    start(first_store)

    if chunks:
        start(body_loads(1))

        @pl.loop(0, chunks)
        def _(j):
            wait(body_loads(j))

            @pl.when(j + 2 < chunks)
            def _():
                start(body_loads(j + 2))

            @pl.when(j + 2 == chunks)
            def _():
                start_tails()

            work(cot_body.at[j], res_body.at[j], res_body.at[j])
            start(body_store(j))

    for t in range(len(tails)):
        wait(tail_loads(t))
        work(cot_tail.at[t], res_tail.at[t], res_tail.at[t])
        start(tail_store(t))
    wait(first_store)
    for j in range(chunks):
        wait(body_store(j))
    for t in range(len(tails)):
        wait(tail_store(t))


def residual_of(here, step_size, acts_t, cot_first, res_first, cot, residual, split):
    tokens, cols = cot.shape
    rows = residual.shape[0]
    first, chunks, chunk, tails = column_chunking(cols)
    parts = chunks + len(tails)
    return pl.pallas_call(
        functools.partial(residual_kernel, split),
        out_shape=pltpu.HBM((rows, cols), jnp.bfloat16),
        in_specs=[smem()] * 2 + [vmem()] * 3 + [hbm()] * 2,
        out_specs=hbm(),
        scratch_shapes=[
            pltpu.VMEM((rows, first), jnp.bfloat16),
            pltpu.VMEM((max(chunks, 1), tokens, chunk), jnp.bfloat16),
            pltpu.VMEM((max(chunks, 1), rows, chunk), jnp.bfloat16),
            pltpu.VMEM((len(tails), tokens, tails[0]), jnp.bfloat16),
            pltpu.VMEM((len(tails), rows, tails[0]), jnp.bfloat16),
            pltpu.SemaphoreType.DMA((parts, 4)),
            pltpu.SemaphoreType.DMA((parts, 4)),
            pltpu.SemaphoreType.DMA((parts + 1, 4)),
        ],
        compiler_params=params(36),
        cost_estimate=cost(2 * tokens * rows * cols, 2 * tokens * (rows + cols) + 4 * rows * cols),
        name="residual_out",
    )(
        here,
        step_size,
        in_vmem(acts_t),
        in_vmem(cot_first),
        in_vmem(res_first),
        in_hbm(cot),
        in_hbm(residual),
    )


def finish_kernel(groups, keep, pair, col_blocks, me_ref, kept_ref, *refs):
    if pair:
        own_ref, arrived_ref, *refs = refs
    block_refs = refs[:groups]
    refs = refs[groups + 2 :]
    if pair:
        grad_ref, *refs = refs
    out_ref, res_ref, sum_ref, table_ref, scalar_ref, zero_ref, sem, table_sem, zero_sem, *refs = refs
    total = groups * keep
    me = me_ref[0]

    zero_ref[...] = jnp.zeros_like(zero_ref)
    zero_copies = []
    for k in range(keep):
        at = pl.multiple_of(kept_ref[k] // col_blocks * BLK, BLK)
        col = pl.multiple_of(kept_ref[k] % col_blocks * BLK, BLK)
        zero_copies.append(
            pltpu.make_async_copy(zero_ref, res_ref.at[pl.ds(at, BLK), pl.ds(col, BLK)], zero_sem.at[k])
        )
        zero_copies[k].start()

    row = lax.broadcasted_iota(jnp.int32, (total, BLK), 0)
    lane = lax.broadcasted_iota(jnp.int32, (total, BLK), 1)
    numbers = jnp.full((total, BLK), -1, jnp.int32)
    for g, block_ref in enumerate(block_refs):
        digits = block_ref[keep * BLK :, :].astype(jnp.float32).astype(jnp.int32)
        numbers = jnp.where(lane // keep == g, digits[0:1, :] * RADIX + digits[1:2, :], numbers)
    numbers = numbers.astype(jnp.float32)
    number = jnp.sum(jnp.where(lane == row, numbers, 0.0), axis=1, keepdims=True)
    first = jnp.min(jnp.where(numbers == number, lane.astype(jnp.float32), float(BLK)), axis=1, keepdims=True)
    final = jnp.max(jnp.where(numbers == number, lane.astype(jnp.float32), -1.0), axis=1, keepdims=True)
    number = jnp.broadcast_to(number, (total, BLK)).astype(jnp.int32)
    first = jnp.broadcast_to(first, (total, BLK)).astype(jnp.int32)
    first = jnp.where(number % groups == me, first, -1)
    final = jnp.broadcast_to(final, (total, BLK)).astype(jnp.int32)
    table_ref[...] = jnp.where(lane == 0, first, jnp.where(lane == 1, number // groups, final))
    table = pltpu.make_async_copy(table_ref, scalar_ref, table_sem)
    table.start()

    grad_copies = []
    if pair:
        grad_buf, grad_sem = refs
        size = grad_buf.shape[0] // grad_sem.shape[0]
        for c in range(grad_sem.shape[0]):
            part = slice(c * size, (c + 1) * size)
            grad_buf[part, :] = (own_ref[part, :] + arrived_ref[part, :].astype(jnp.float32)).astype(jnp.bfloat16)
            grad_copies.append(pltpu.make_async_copy(grad_buf.at[part, :], grad_ref.at[part, :], grad_sem.at[c]))
            grad_copies[c].start()

    table.wait()

    def copy(i):
        return pltpu.make_async_copy(sum_ref.at[i], out_ref.at[scalar_ref[i, 1]], sem.at[i])

    def block(i):
        at = i % keep * BLK
        return block_refs[i // keep][at : at + BLK, :].astype(jnp.float32)

    for i in range(total):
        slot = scalar_ref[i, 0]

        @pl.when(slot >= 0)
        def _(i=i, slot=slot):
            @pl.when(slot == i)
            def _():
                sum_ref[i] = block(i)

            if i >= keep:

                @pl.when(slot < i)
                def _():
                    sum_ref[slot] += block(i)

            @pl.when(scalar_ref[i, 2] == i)
            def _():
                copy(slot).start()

    for done in zero_copies + grad_copies:
        done.wait()
    for i in range(total):

        @pl.when(scalar_ref[i, 0] == i)
        def _(i=i):
            copy(i).wait()


def finish(me, kept, parts, blocks, zeros, residual):
    groups = len(blocks)
    keep = kept.shape[0]
    out_shape = [pltpu.HBM(a.shape, a.dtype) for a in (zeros, residual)]
    out_specs = [hbm(), hbm()]
    scratch = [
        pltpu.VMEM((groups * keep, BLK, BLK), jnp.float32),
        pltpu.VMEM((groups * keep, BLK), jnp.int32),
        pltpu.SMEM((groups * keep, BLK), jnp.int32),
        pltpu.VMEM((BLK, BLK), jnp.bfloat16),
        pltpu.SemaphoreType.DMA((groups * keep,)),
        pltpu.SemaphoreType.DMA,
        pltpu.SemaphoreType.DMA((keep,)),
    ]
    if parts:
        out_shape.insert(0, pltpu.HBM(parts[0].shape, jnp.bfloat16))
        out_specs.insert(0, hbm())
        scratch += [pltpu.VMEM(parts[0].shape, jnp.bfloat16), pltpu.SemaphoreType.DMA((4,))]
        parts = [in_vmem(parts[0]), parts[1]]
    first = 2 + len(parts) + groups
    return pl.pallas_call(
        functools.partial(finish_kernel, groups, keep, bool(parts), residual.shape[1] // BLK),
        out_shape=out_shape,
        in_specs=[smem(), smem()] + [vmem()] * (len(parts) + groups) + [hbm(), hbm()],
        out_specs=out_specs,
        scratch_shapes=scratch,
        input_output_aliases={first: len(out_shape) - 2, first + 1: len(out_shape) - 1},
        compiler_params=params(10),
        cost_estimate=cost(groups * keep * BLK * BLK, groups * keep * BLK * BLK * 8),
        name="finish",
    )(me, kept, *parts, *blocks, in_hbm(zeros), in_hbm(residual))


def swapped(x, axis, mask):
    return lax.ppermute(x, axis, [(i, i ^ mask) for i in range(lax.axis_size(axis))])


def of_all_groups(x):
    return [x] + [swapped(x, "dp", mask) for mask in range(1, lax.axis_size("dp"))]


def body(activations, cotangent, weight, residual, step_size, kept_blocks):
    rows, cols = weight.shape
    groups = lax.axis_size("dp")
    owned_count = (rows // BLK) * (cols // BLK) // groups
    kept = kept_blocks.reshape(-1)
    me = lax.axis_index("dp").astype(jnp.int32).reshape(1)
    here = lax.axis_index("tensor").astype(jnp.int32).reshape(1)
    pair = lax.axis_size("tensor") == 2
    if pair:
        act = swapped(activations, "tensor", 1)
        away, acts_t, own, zeros, kept_cot, kept_res, cot_first, res_first = input_grad_partials(
            here, me, kept, cotangent, weight, residual[0], owned_count, activations
        )
        parts = [own, swapped(away, "tensor", 1)]
    else:
        act = lax.all_gather(activations, "tensor", axis=0, tiled=True)
        acts_t = None
        own, zeros, kept_cot, kept_res, cot_first, res_first = input_grad_partials(
            here, me, kept, cotangent, weight, residual[0], owned_count, None
        )
        summed = lax.psum_scatter(own, "tensor", scatter_dimension=0, tiled=True)
        parts = []
    acts_t, blocks = kept_blocks_of(kept, step_size, acts_t, act, kept_cot, kept_res, cols // BLK)
    all_blocks = of_all_groups(blocks)
    rounded = residual_of(here, step_size, acts_t, cot_first, res_first, cotangent, residual[0], pair)
    *grads, owned, residual_out = finish(me, kept, parts, all_blocks, zeros, rounded)
    input_grad = grads[0] if pair else summed.astype(jnp.bfloat16)
    return (input_grad, residual_out[None], owned.reshape(1, 1, 1, owned_count, BLK, BLK))


def solution(mesh):
    in_specs = (
        P(("dp", "tensor"), "fsdp"),
        P("dp", "tensor"),
        P("fsdp", "tensor"),
        P("dp", "fsdp", "tensor"),
        P(),
        P("dp", "fsdp", "tensor", None),
    )
    out_specs = (
        P(("dp", "tensor"), "fsdp"),
        P("dp", "fsdp", "tensor"),
        P("dp", "fsdp", "tensor", None, None, None),
    )
    return jax.shard_map(body, mesh=mesh, in_specs=in_specs, out_specs=out_specs, check_vma=False)
```
